32 devices in a mesh: dp: 4 (over x, core), seq: 8 (over z, y).
Axes of the slice: x: 2, y: 2, z: 4, core: 2. Of those that a mesh axis runs over, the one named last changes fastest.
Arguments:
- inputs: bfloat16 [4, 4096, 1024], P('dp', 'seq'), may hold values from -6 to 6
- first_values: bfloat16 [4, 4096, 1024], P('dp', 'seq'), may hold values from -6 to 6
- lengths: int32 [4, 8], P('dp'), may hold values from 1 to 4096, as said below
- w_query: bfloat16 [1024, 1024], P(('dp', 'seq')), may hold values from -0.1875 to 0.1875
- w_key: bfloat16 [1024, 1024], P(('dp', 'seq')), may hold values from -0.1875 to 0.1875
- w_value: bfloat16 [1024, 1024], P(('dp', 'seq')), may hold values from -0.1875 to 0.1875
- w_out: bfloat16 [1024, 1024], P(('dp', 'seq')), may hold values from -2 to 2
- gain_attn: bfloat16 [1024], P(('dp', 'seq')), may hold values from 0.5 to 1.5
- w_gate: bfloat16 [1024, 2816], P(('dp', 'seq')), may hold values from -0.1875 to 0.1875
- w_up: bfloat16 [1024, 2816], P(('dp', 'seq')), may hold values from -0.1875 to 0.1875
- w_down: bfloat16 [2816, 1024], P(('dp', 'seq')), may hold values from -0.109375 to 0.109375
- gain_mlp: bfloat16 [1024], P(('dp', 'seq')), may hold values from 0.5 to 1.5
- cotangent: bfloat16 [4, 4096, 1024], P('dp', 'seq'), may hold values from -6 to 6
Outputs:
- output: bfloat16 [4, 4096, 1024], P('dp', 'seq')
- grad_inputs: float32 [4, 4096, 1024], P('dp', 'seq')
- grad_first_values: float32 [4, 4096, 1024], P('dp', 'seq')
- grad_w_query: float32 [1024, 1024], P(('dp', 'seq'))
- grad_w_key: float32 [1024, 1024], P(('dp', 'seq'))
- grad_w_value: float32 [1024, 1024], P(('dp', 'seq'))
- grad_w_out: float32 [1024, 1024], P(('dp', 'seq'))
- grad_gain_attn: float32 [1024], P(('dp', 'seq'))
- grad_w_gate: float32 [1024, 2816], P(('dp', 'seq'))
- grad_w_up: float32 [1024, 2816], P(('dp', 'seq'))
- grad_w_down: float32 [2816, 1024], P(('dp', 'seq'))
- grad_gain_mlp: float32 [1024], P(('dp', 'seq'))
The draws below stay inside these ranges and needn't reach their ends.
Inputs may be any that keep to these rules, and one draw needn't show every extreme that they name: Each row's 8 lengths sum to 4096; one of them, at a place drawn for each row, is longer than 3584; each of the others is below 73.
All inputs are finite; a program needn't handle non-finite values.
Results may differ from the reference program's by a relative error of at most 0.023.
Values may be sent and summed in bfloat16 or wider, within the bound.
A program may use at most 192 MiB of HBM per device.

```python
import math
from functools import partial
import jax
import jax.numpy as jnp
from jax import lax

D = 1024
HEADS = 16
HEAD_DIM = 64
FF = 2816
GROUP = 512
NDOC = 8
LENGTH = 4096
ROWS = 4


def draw_lengths(key, part):
    key = jax.random.fold_in(key, 11)
    first_key, second_key = jax.random.split(key)
    others = jax.random.randint(first_key, (ROWS, NDOC), 1, GROUP // (NDOC - 1), dtype=jnp.int32)
    longest_at = jax.random.randint(second_key, (ROWS, 1), 0, NDOC, dtype=jnp.int32)
    slots = jnp.arange(NDOC, dtype=jnp.int32)[None, :]
    remains = jnp.where(slots == longest_at, 0, others)
    longest = LENGTH - jnp.sum(remains, axis=1, keepdims=True)
    return jnp.where(slots == longest_at, longest, remains).astype(jnp.int32)


def block_levels(own_key, dims, shards, least, high):
    factor_of = 1.0
    for dim, parts in shards:
        steps = jax.random.uniform(jax.random.fold_in(jax.random.fold_in(own_key, 6), dim), (parts,), jnp.float32, least / len(shards), high / len(shards))
        factor_of = factor_of * jnp.repeat(jnp.exp(steps), dims[dim] // parts).reshape((-1,) + (1,) * (len(dims) - 1 - dim))
    return factor_of


def scatter_about(own_key, extent, scale, reach, shards=(), held_as=jnp.bfloat16):
    factor_of = block_levels(own_key, extent, shards, -0.22, 0.18) if shards else 1.0
    drawn = jax.random.normal(own_key, extent, jnp.float32) * scale * factor_of
    return jnp.minimum(jnp.maximum(drawn, -reach), reach).astype(held_as)


def setup_inputs(seed: int = 0) -> dict:
    arg_keys = jax.random.split(jax.random.key(seed), 14)
    inputs = scatter_about(arg_keys[0], (ROWS, LENGTH, D), 1.0, 6.0, ((0, 4), (1, 8)))
    first_values = scatter_about(arg_keys[1], (ROWS, LENGTH, D), 1.0, 6.0, ((0, 4), (1, 8)))
    lengths = draw_lengths(jax.random.fold_in(arg_keys[13], 71), 0)
    w_query = scatter_about(arg_keys[3], (D, D), D ** -0.5, 0.1875, ((0, 32),))
    w_key = scatter_about(arg_keys[4], (D, D), D ** -0.5, 0.1875, ((0, 32),))
    w_value = scatter_about(arg_keys[5], (D, D), D ** -0.5, 0.1875, ((0, 32),))
    w_out = scatter_about(arg_keys[6], (D, D), 8 ** -0.5, 2.0, ((0, 32),))
    gain_attn = jnp.clip(1.0 + 0.1 * jax.random.normal(arg_keys[7], (D,), jnp.float32), 0.5, 1.5).astype(jnp.bfloat16)
    w_gate = scatter_about(arg_keys[8], (D, FF), D ** -0.5, 0.1875, ((0, 32),))
    w_up = scatter_about(arg_keys[9], (D, FF), D ** -0.5, 0.1875, ((0, 32),))
    w_down = scatter_about(arg_keys[10], (FF, D), FF ** -0.5, 0.109375, ((0, 32),))
    gain_mlp = jnp.clip(1.0 + 0.1 * jax.random.normal(arg_keys[11], (D,), jnp.float32), 0.5, 1.5).astype(jnp.bfloat16)
    cotangent = scatter_about(arg_keys[12], (ROWS, LENGTH, D), 1.0, 6.0, ((0, 4), (1, 8)))
    return dict(inputs=inputs, first_values=first_values, lengths=lengths, w_query=w_query, w_key=w_key, w_value=w_value, w_out=w_out, gain_attn=gain_attn, w_gate=w_gate, w_up=w_up, w_down=w_down, gain_mlp=gain_mlp, cotangent=cotangent)


EPS = 1e-06
THETA = 10000.0
HIGHEST = lax.Precision.HIGHEST

@jax.custom_vjp
def low(v):
    return lax.optimization_barrier(v.astype(jnp.bfloat16)).astype(jnp.float32)

@jax.custom_vjp
def low_back(v):
    return v

def low_keep(v):
    return (low(v), None)

def low_pass(kept, grad):
    return (grad,)

def back_keep(v):
    return (v, None)

def back_low(kept, grad):
    return (low(grad),)
low.defvjp(low_keep, low_pass)
low_back.defvjp(back_keep, back_low)

def doc_tables(lengths, full_len):
    row_count, doc_count = lengths.shape
    doc_ends = jnp.cumsum(lengths, axis=1)
    doc_starts = doc_ends - lengths
    position = jnp.arange(full_len, dtype=jnp.int32)
    segment = lax.optimization_barrier(jnp.sum((position[None, :, None] >= doc_ends[:, None, :]).astype(jnp.int32), axis=2))
    chosen = segment[:, :, None] == jnp.arange(doc_count, dtype=jnp.int32)[None, None, :]
    offsets = lax.optimization_barrier(jnp.sum(jnp.where(chosen, doc_starts[:, None, :], 0), axis=2))
    row_base = jnp.arange(row_count, dtype=jnp.int32)[:, None] * doc_count
    return ((segment + row_base).astype(jnp.int32), (position[None, :] - offsets).astype(jnp.int32))

def rotate(values, position, direction):
    half_dim = values.shape[-1] // 2
    freqs = THETA ** (-jnp.arange(half_dim, dtype=jnp.float32) * 2.0 / values.shape[-1])
    angles = position.astype(jnp.float32)[..., None] * freqs
    cosine = jnp.cos(angles)[..., None, :]
    sine = direction * jnp.sin(angles)[..., None, :]
    first = values[..., :half_dim]
    second = values[..., half_dim:]
    return jnp.concatenate([first * cosine - second * sine, first * sine + second * cosine], axis=-1)

def rms_norm(values, gain):
    return values * lax.rsqrt(lax.optimization_barrier(jnp.mean(values * values, axis=-1, keepdims=True)) + EPS) * gain

def product(left, right):
    return jnp.dot(left, right, precision=HIGHEST)

def attend_block(operands, keys, mixed, key_seg):
    query_block, query_seg, query_time = operands
    scores = jnp.einsum('qhd,khd->hqk', query_block, keys, precision=HIGHEST) * HEAD_DIM ** (-0.5)
    scores = low_back(scores)
    key_time = jnp.arange(keys.shape[0], dtype=jnp.int32)
    allowed = (query_seg[:, None] == key_seg[None, :]) & (query_time[:, None] >= key_time[None, :])
    scores = jnp.where(allowed[None], scores, -1e+30)
    weights = jax.nn.softmax(scores, axis=-1)
    weights = low(weights)
    return jnp.einsum('hqk,khd->qhd', weights, mixed, precision=HIGHEST)

def attend_row(row_data):
    queries, keys, mixed, segment = row_data
    block_rows = math.gcd(LENGTH, 512)
    block_count = LENGTH // block_rows
    times = jnp.arange(LENGTH, dtype=jnp.int32)
    blocks = (queries.reshape(block_count, block_rows, HEADS, HEAD_DIM), segment.reshape(block_count, block_rows), times.reshape(block_count, block_rows))
    step_fn = jax.checkpoint(partial(attend_block, keys=keys, mixed=mixed, key_seg=segment))
    result = lax.map(step_fn, blocks)
    return result.reshape(LENGTH, HEADS, HEAD_DIM)

def forward(inputs, first_values, w_query, w_key, w_value, w_out, gain_attn, w_gate, w_up, w_down, gain_mlp, segment, position):
    hidden_in = low(rms_norm(inputs, gain_attn))
    queries = low_back(product(hidden_in, w_query)).reshape(ROWS, LENGTH, HEADS, HEAD_DIM)
    queries = low(rotate(queries, position, 1.0))
    keys = low_back(product(hidden_in, w_key)).reshape(ROWS, LENGTH, HEADS, HEAD_DIM)
    keys = low(rotate(keys, position, 1.0))
    values = low_back(product(hidden_in, w_value))
    mixed = low(0.5 * values + 0.5 * first_values).reshape(ROWS, LENGTH, HEADS, HEAD_DIM)
    attended = lax.map(attend_row, (queries, keys, mixed, segment)).reshape(ROWS, LENGTH, D)
    attended = low(low_back(attended))
    branch = low_back(product(attended, w_out))
    middle = inputs + branch
    hidden_mlp = low(rms_norm(middle, gain_mlp))
    gate = low_back(product(hidden_mlp, w_gate))
    upward = low_back(product(hidden_mlp, w_up))
    inner = low(jax.nn.silu(gate) * upward)
    return middle + product(inner, w_down)

def reference(inputs, first_values, lengths, w_query, w_key, w_value, w_out, gain_attn, w_gate, w_up, w_down, gain_mlp, cotangent):
    segment, position = doc_tables(lengths, LENGTH)
    params = [inputs, first_values, w_query, w_key, w_value, w_out, gain_attn, w_gate, w_up, w_down, gain_mlp]
    floats = [entry.astype(jnp.float32) for entry in params]

    def closed(*arrays):
        return forward(*arrays, segment, position)
    output, pullback = jax.vjp(closed, *floats)
    grads = pullback(cotangent.astype(jnp.float32))
    return (output.astype(jnp.bfloat16), grads[0], grads[1], grads[2], grads[3], grads[4], grads[5], grads[6], grads[7], grads[8], grads[9], grads[10])
```

```python
import functools

import jax
import jax.numpy as jnp
from jax import lax
from jax.experimental import pallas as pl
from jax.experimental.pallas import tpu as pltpu
from jax.sharding import PartitionSpec as P

HEAD_DIM = 64
EPS = 1e-06
THETA = 10000.0
NEG = -1e30
MESH = pl.DeviceIdType.MESH
BF16 = jnp.bfloat16
F32 = jnp.float32
VMEM = pltpu.VMEM
MIB = 1 << 20


def dot(left, right, left_dim=1, right_dim=0):
    return lax.dot_general(
        left, right, (((left_dim,), (right_dim,)), ((), ())), preferred_element_type=F32
    )


def across(left, right):
    return dot(left, right, 0, 0)


def against(left, right):
    return dot(left, right, 1, 1)


def norm_back(grad_normed, values, gain):
    scale_inv = lax.rsqrt(jnp.mean(values * values, axis=-1, keepdims=True) + EPS)
    normed = values * scale_inv
    grad_scaled = grad_normed * gain
    grad_values = scale_inv * (
        grad_scaled - normed * jnp.mean(grad_scaled * normed, axis=-1, keepdims=True)
    )
    grad_gain = jnp.sum(grad_normed * normed, axis=0)
    return (grad_values, grad_gain)


def turned(values, cosine, sine):
    lane = lax.broadcasted_iota(jnp.int32, values.shape, 1) % HEAD_DIM
    other = jnp.where(
        lane < HEAD_DIM // 2,
        pltpu.roll(values, 128 - HEAD_DIM // 2, 1),
        pltpu.roll(values, HEAD_DIM // 2, 1),
    )
    return values * cosine + other * sine


def project_kernel(width, x, gain, wq, wk, wv, first, cosine, sine, q_out, k_out, v_out, h_out):
    @pl.when(pl.program_id(0) == 0)
    def _():
        values = x[...].astype(F32)
        scale = lax.rsqrt(jnp.mean(values * values, axis=-1, keepdims=True) + EPS)
        h_out[...] = (values * scale * gain[...]).astype(BF16)

    hidden = h_out[...]
    cos, sin = cosine[...], sine[...]
    for weight, out, scale in ((wq, q_out, HEAD_DIM**-0.5), (wk, k_out, 1.0)):
        raw = dot(hidden, weight[...])
        for part in range(2):
            done = turned(raw[:, part * 128 : part * 128 + 128], cos, sin) * scale
            for piece in range(128 // width):
                out[part * (128 // width) + piece] = done[
                    :, piece * width : (piece + 1) * width
                ].astype(BF16)
    mixed = (0.5 * dot(hidden, wv[...]) + 0.5 * first[...].astype(F32)).astype(BF16)
    for piece in range(256 // width):
        v_out[piece] = mixed[:, piece * width : (piece + 1) * width]


def project(x, gain, wq, wk, wv, first, cosine, sine, parts):
    tokens, dim = x.shape
    width = dim // parts
    whole = lambda shape: pl.BlockSpec(shape, lambda g: (0,) * len(shape))
    cols = lambda rows: pl.BlockSpec((rows, 256), lambda g: (0, g))
    out = pl.BlockSpec((256 // width, tokens, width), lambda g: (g, 0, 0))
    split = jax.ShapeDtypeStruct((parts, tokens, width), BF16)
    return pl.pallas_call(
        functools.partial(project_kernel, width),
        grid=(dim // 256,),
        in_specs=[
            whole((tokens, dim)),
            whole((1, dim)),
            cols(dim),
            cols(dim),
            cols(dim),
            cols(tokens),
            whole((tokens, 128)),
            whole((tokens, 128)),
        ],
        out_specs=[out, out, out, whole((tokens, dim))],
        out_shape=[split, split, split, jax.ShapeDtypeStruct((tokens, dim), BF16)],
        compiler_params=pltpu.CompilerParams(vmem_limit_bytes=40 * MIB),
        cost_estimate=pl.CostEstimate(
            flops=6 * tokens * dim * dim, bytes_accessed=16 * tokens * dim, transcendentals=0
        ),
        name="project",
    )(x, gain, wq, wk, wv, first, cosine, sine)


def unproject_kernel(width, dq, dk, dv, cosine, sine, q_out, k_out, v_out, first_out):
    cos, sin = cosine[...], sine[...]
    for part in range(2):
        lanes = slice(part * 128, part * 128 + 128)
        picks = range(part * (128 // width), (part + 1) * (128 // width))
        join = lambda ref: jnp.concatenate([ref[p] for p in picks], axis=1).astype(F32)
        q_out[:, lanes] = turned(join(dq), cos, -sin).astype(BF16)
        k_out[:, lanes] = turned(join(dk), cos, -sin).astype(BF16)
        value = 0.5 * join(dv)
        first_out[:, lanes] = value
        v_out[:, lanes] = value.astype(BF16)


def unproject(dq, dk, dv, cosine, sine):
    parts, tokens, width = dq.shape
    dim = parts * width
    split = pl.BlockSpec((256 // width, tokens, width), lambda g: (g, 0, 0))
    table = pl.BlockSpec((tokens, 128), lambda g: (0, 0))
    cols = pl.BlockSpec((tokens, 256), lambda g: (0, g))
    low = jax.ShapeDtypeStruct((tokens, dim), BF16)
    return pl.pallas_call(
        functools.partial(unproject_kernel, width),
        grid=(dim // 256,),
        in_specs=[split, split, split, table, table],
        out_specs=[cols, cols, cols, cols],
        out_shape=[low, low, low, jax.ShapeDtypeStruct((tokens, dim), F32)],
        compiler_params=pltpu.CompilerParams(vmem_limit_bytes=40 * MIB),
        name="unproject",
    )(dq, dk, dv, cosine, sine)


def greet(parts, me):
    barrier = pltpu.get_barrier_semaphore()
    for step in range(1, parts):
        pl.semaphore_signal(
            barrier, 1, device_id={"seq": lax.rem(me + step, parts)}, device_id_type=MESH
        )
    pl.semaphore_wait(barrier, parts - 1)


def send(source, target, send_sem, recv_sem, peer):
    return pltpu.make_async_remote_copy(
        src_ref=source,
        dst_ref=target,
        send_sem=send_sem,
        recv_sem=recv_sem,
        device_id={"seq": peer},
        device_id_type=MESH,
    )


def arrive(ref, sem):
    pltpu.make_async_copy(ref, ref, sem).wait()


def own_head(values, head, width):
    if width == HEAD_DIM:
        return values
    lane = lax.broadcasted_iota(jnp.int32, values.shape, 1)
    return jnp.where(lane // HEAD_DIM == head, values, jnp.zeros_like(values))


def allowed_tile(i, j, tokens, start):
    key = j * tokens + lax.broadcasted_iota(jnp.int32, (tokens, tokens), 0)
    query = i * tokens + lax.broadcasted_iota(jnp.int32, (tokens, tokens), 1)
    return (key <= query) & (key >= start[i])


def forward_kernel(
    parts, heads,
    q_in, k_in, v_in, start,
    q_all, k_all, v_all, o_all, lse_all, attended,
    v_turn, q_own, best, total, accum, o_send,
    in_send, in_recv, o_out, o_in,
):
    _, tokens, width = q_in.shape
    me = lax.axis_index("seq")
    greet(parts, me)
    pairs = ((q_in, q_all), (k_in, k_all), (v_in, v_all))
    for index, (source, target) in enumerate(pairs):
        pltpu.make_async_copy(source.at[me], target.at[me], in_recv.at[index, me]).start()

    def start_step(step, _):
        peer = lax.rem(me + step, parts)
        for index, (source, target) in enumerate(pairs):
            send(
                source.at[peer], target.at[me],
                in_send.at[index, peer], in_recv.at[index, me], peer,
            ).start()
        return 0

    lax.fori_loop(1, parts, start_step, 0)

    def tile(i, j, masked):
        if masked:
            allowed = allowed_tile(i, j, tokens, start)
        for head in range(heads):
            rows = slice(head * HEAD_DIM, (head + 1) * HEAD_DIM)
            scores = against(k_all[j], q_own[head])
            if masked:
                scores = jnp.where(allowed, scores, NEG)
            old = best[head]
            new = jnp.maximum(old, jnp.max(scores, axis=0, keepdims=True))
            weights = jnp.exp(scores - new)
            factor = jnp.exp(old - new)
            best[head] = new
            total[head] = total[head] * factor + jnp.sum(weights, axis=0, keepdims=True)
            accum[rows] = accum[rows] * factor + dot(v_turn[j, rows], weights.astype(BF16))

    def query_block(i, _):
        for index, (_, target) in enumerate(pairs):
            arrive(target.at[i], in_recv.at[index, i])
        v_turn[i] = v_all[i].T
        for head in range(heads):
            q_own[head] = own_head(q_all[i], head, width)
        best[...] = jnp.full(best.shape, NEG, F32)
        total[...] = jnp.zeros(total.shape, F32)
        accum[...] = jnp.zeros(accum.shape, F32)

        def key_block(j, _):
            masked = (j == 0) | (j == i) | (i == parts - 1)

            @pl.when(masked)
            def _():
                tile(i, j, True)

            @pl.when(jnp.logical_not(masked))
            def _():
                tile(i, j, False)

            return 0

        lax.fori_loop(0, i + 1, key_block, 0)
        for head in range(heads):
            rows = slice(head * HEAD_DIM, (head + 1) * HEAD_DIM)
            o_all[i, rows] = accum[rows] / total[head]
            lse_all[i, head] = best[head] + jnp.log(total[head])
        o_send[i] = o_all[i].T.astype(BF16)

        @pl.when(i == me)
        def _():
            pltpu.make_async_copy(o_send.at[i], attended.at[me], o_in.at[me]).start()

        @pl.when(i != me)
        def _():
            send(o_send.at[i], attended.at[me], o_out.at[i], o_in.at[me], i).start()

        return 0

    lax.fori_loop(0, parts, query_block, 0)

    def finish(step, _):
        peer = lax.rem(me + step, parts)
        for index, (source, _) in enumerate(pairs):
            arrive(source.at[peer], in_send.at[index, peer])
        arrive(o_send.at[peer], o_out.at[peer])
        arrive(attended.at[peer], o_in.at[peer])
        return 0

    lax.fori_loop(1, parts, finish, 0)
    arrive(attended.at[me], o_in.at[me])


def attend(q, k, v, start):
    parts, tokens, width = q.shape
    heads = width // HEAD_DIM
    whole = pl.BlockSpec(memory_space=VMEM)
    split = jax.ShapeDtypeStruct(q.shape, BF16)
    flops = 4 * parts * parts * tokens * tokens * width // 2
    return pl.pallas_call(
        functools.partial(forward_kernel, parts, heads),
        in_specs=[whole] * 4,
        out_specs=[whole] * 6,
        out_shape=[
            split,
            split,
            split,
            jax.ShapeDtypeStruct((parts, width, tokens), F32),
            jax.ShapeDtypeStruct((parts, heads, 1, tokens), F32),
            split,
        ],
        scratch_shapes=[
            VMEM((parts, width, tokens), BF16),
            VMEM((heads, tokens, width), BF16),
            VMEM((heads, 1, tokens), F32),
            VMEM((heads, 1, tokens), F32),
            VMEM((width, tokens), F32),
            VMEM((parts, tokens, width), BF16),
            pltpu.SemaphoreType.DMA((3, parts)),
            pltpu.SemaphoreType.DMA((3, parts)),
            pltpu.SemaphoreType.DMA((parts,)),
            pltpu.SemaphoreType.DMA((parts,)),
        ],
        compiler_params=pltpu.CompilerParams(
            collective_id=1, has_side_effects=True, vmem_limit_bytes=48 * MIB
        ),
        cost_estimate=pl.CostEstimate(
            flops=4 * flops, bytes_accessed=16 * q.size, transcendentals=flops // 256
        ),
        name="attend",
    )(q, k, v, start)


def backward_kernel(
    parts, heads,
    d_in, q_all, k_all, v_all, o_all, lse_all, start,
    dq_got, dk_got, dv_got,
    d_all, q_own, d_own, k_turn, delta, dq_turn, dk_sum, dv_sum, dq_send, dk_send, dv_send,
    in_send, in_recv, out_send, out_recv,
):
    _, tokens, width = d_in.shape
    me = lax.axis_index("seq")
    greet(parts, me)
    pltpu.make_async_copy(d_in.at[me], d_all.at[me], in_recv.at[me]).start()

    def start_step(step, _):
        peer = lax.rem(me + step, parts)
        send(d_in.at[peer], d_all.at[me], in_send.at[peer], in_recv.at[me], peer).start()
        return 0

    lax.fori_loop(1, parts, start_step, 0)
    sends = ((dq_send, dq_got), (dk_send, dk_got), (dv_send, dv_got))

    def give(index, block):
        source, target = sends[index]

        @pl.when(block == me)
        def _():
            pltpu.make_async_copy(
                source.at[block], target.at[me], out_recv.at[index, me]
            ).start()

        @pl.when(block != me)
        def _():
            send(
                source.at[block], target.at[me],
                out_send.at[index, block], out_recv.at[index, me], block,
            ).start()

    def tile(i, j, masked):
        if masked:
            allowed = allowed_tile(i, j, tokens, start)
        for head in range(heads):
            rows = slice(head * HEAD_DIM, (head + 1) * HEAD_DIM)
            query, grad = q_own[head, i], d_own[head, i]
            scores = against(k_all[j], query)
            if masked:
                scores = jnp.where(allowed, scores, NEG)
            weights = jnp.exp(scores - lse_all[i, head])
            dv_sum[...] += dot(weights.astype(BF16), grad)
            slope = against(v_all[j], grad) - delta[i, head]
            d_scores = (weights * slope).astype(BF16)
            dk_sum[...] += dot(d_scores, query)
            dq_turn[i, rows] += dot(k_turn[j, rows], d_scores)

    dq_turn[...] = jnp.zeros(dq_turn.shape, F32)

    def key_block(step, _):
        j = parts - 1 - step
        arrive(d_all.at[j], in_recv.at[j])
        got = d_all[j]
        product = got.astype(F32).T * o_all[j]
        for head in range(heads):
            rows = slice(head * HEAD_DIM, (head + 1) * HEAD_DIM)
            delta[j, head] = jnp.sum(product[rows], axis=0, keepdims=True)
            q_own[head, j] = own_head(q_all[j], head, width)
            d_own[head, j] = own_head(got, head, width)
        k_turn[j] = k_all[j].T
        dk_sum[...] = jnp.zeros(dk_sum.shape, F32)
        dv_sum[...] = jnp.zeros(dv_sum.shape, F32)

        def query_block(i, _):
            masked = (j == 0) | (j == i) | (i == parts - 1)

            @pl.when(masked)
            def _():
                tile(i, j, True)

            @pl.when(jnp.logical_not(masked))
            def _():
                tile(i, j, False)

            @pl.when(j == 0)
            def _():
                dq_send[i] = (dq_turn[i] * HEAD_DIM**-0.5).T.astype(BF16)
                give(0, i)

            return 0

        lax.fori_loop(j, parts, query_block, 0)
        dk_send[j] = dk_sum[...].astype(BF16)
        dv_send[j] = dv_sum[...].astype(BF16)
        give(1, j)
        give(2, j)
        return 0

    lax.fori_loop(0, parts, key_block, 0)

    def finish(step, _):
        peer = lax.rem(me + step, parts)
        arrive(d_in.at[peer], in_send.at[peer])
        for index, (source, target) in enumerate(sends):
            arrive(source.at[peer], out_send.at[index, peer])
            arrive(target.at[peer], out_recv.at[index, peer])
        return 0

    lax.fori_loop(1, parts, finish, 0)
    for index, (_, target) in enumerate(sends):
        arrive(target.at[me], out_recv.at[index, me])


def attend_back(d_att, q, k, v, o, lse, start):
    parts, tokens, width = q.shape
    heads = width // HEAD_DIM
    whole = pl.BlockSpec(memory_space=VMEM)
    split = jax.ShapeDtypeStruct(q.shape, BF16)
    flops = 10 * parts * parts * tokens * tokens * width // 2
    return pl.pallas_call(
        functools.partial(backward_kernel, parts, heads),
        in_specs=[whole] * 7,
        out_specs=[whole] * 3,
        out_shape=[split] * 3,
        scratch_shapes=[
            VMEM((parts, tokens, width), BF16),
            VMEM((heads, parts, tokens, width), BF16),
            VMEM((heads, parts, tokens, width), BF16),
            VMEM((parts, width, tokens), BF16),
            VMEM((parts, heads, 1, tokens), F32),
            VMEM((parts, width, tokens), F32),
            VMEM((tokens, width), F32),
            VMEM((tokens, width), F32),
            VMEM((parts, tokens, width), BF16),
            VMEM((parts, tokens, width), BF16),
            VMEM((parts, tokens, width), BF16),
            pltpu.SemaphoreType.DMA((parts,)),
            pltpu.SemaphoreType.DMA((parts,)),
            pltpu.SemaphoreType.DMA((3, parts)),
            pltpu.SemaphoreType.DMA((3, parts)),
        ],
        compiler_params=pltpu.CompilerParams(
            collective_id=2, has_side_effects=True, vmem_limit_bytes=48 * MIB
        ),
        cost_estimate=pl.CostEstimate(
            flops=4 * flops, bytes_accessed=20 * q.size, transcendentals=flops // 640
        ),
        name="attend_back",
    )(d_att, q, k, v, o, lse, start)


def shards(
    inputs, first_values, lengths, w_query, w_key, w_value, w_out, gain_attn,
    w_gate, w_up, w_down, gain_mlp, cotangent,
):
    row_count, tokens, width = inputs.shape
    assert row_count == 1
    parts = lax.axis_size("seq")
    rank = lax.axis_index("seq")
    both = ("dp", "seq")
    gather = lambda value: lax.all_gather(value, both, axis=0, tiled=True)

    qkv = gather(jnp.concatenate([w_query, w_key, w_value], axis=1))
    gains = gather(jnp.stack([gain_attn, gain_mlp], axis=1)).astype(F32)
    gain_one, gain_two = gains[:, 0], gains[:, 1]
    rest = gather(jnp.concatenate([w_out, w_gate, w_up], axis=1))
    down_full = gather(w_down)
    hidden_size = w_gate.shape[1]
    query_full, key_full, value_full = (qkv[:, n * width : (n + 1) * width] for n in range(3))
    out_full = rest[:, :width]
    gate_full = rest[:, width : width + hidden_size]
    up_full = rest[:, width + hidden_size :]

    ends = jnp.cumsum(lengths[0])
    begins = ends - lengths[0]
    time = jnp.arange(tokens * parts, dtype=jnp.int32)
    inside = (time[:, None] >= begins[None, :]) & (time[:, None] < ends[None, :])
    start_all = jnp.sum(jnp.where(inside, begins[None, :], 0), axis=1)
    own_start = lax.dynamic_slice_in_dim(start_all, rank * tokens, tokens)
    position = (rank * tokens + jnp.arange(tokens, dtype=jnp.int32) - own_start).astype(F32)
    half = HEAD_DIM // 2
    angles = position[:, None] * THETA ** (-jnp.arange(half, dtype=F32) * 2.0 / HEAD_DIM)
    cosine = jnp.tile(jnp.cos(angles), (1, 4))
    sine = jnp.sin(angles)
    sine = jnp.tile(jnp.concatenate([-sine, sine], axis=1), (1, 2))
    start = start_all.reshape(parts, 1, tokens)

    x_low = inputs.reshape(tokens, width)
    q, k, v, hidden_in = project(
        x_low, gain_one[None], query_full, key_full, value_full,
        first_values.reshape(tokens, width), cosine, sine, parts,
    )
    q_all, k_all, v_all, o_all, lse_all, attended = attend(q, k, v, start)
    attended = attended.transpose(1, 0, 2).reshape(tokens, width)

    x_in = x_low.astype(F32)
    middle = x_in + dot(attended, out_full)
    scale = lax.rsqrt(jnp.mean(middle * middle, axis=-1, keepdims=True) + EPS)
    hidden_mlp = (middle * scale * gain_two).astype(BF16)
    gate = dot(hidden_mlp, gate_full)
    upward = dot(hidden_mlp, up_full)
    sigma = jax.nn.sigmoid(gate)
    silu_gate = gate * sigma
    inner = (silu_gate * upward).astype(BF16)
    output = (middle + dot(inner, down_full)).astype(BF16).reshape(inputs.shape)
    grad_y = cotangent.reshape(tokens, width)
    grad_down = across(inner, grad_y)
    grad_inner = against(grad_y, down_full)
    grad_gate_low = (grad_inner * upward * sigma * (1.0 + gate * (1.0 - sigma))).astype(BF16)
    grad_up_low = (grad_inner * silu_gate).astype(BF16)
    grad_gate = across(hidden_mlp, grad_gate_low)
    grad_up = across(hidden_mlp, grad_up_low)
    grad_hidden_mlp = against(grad_gate_low, gate_full) + against(grad_up_low, up_full)
    grad_middle, grad_gain_two = norm_back(grad_hidden_mlp, middle, gain_two)
    grad_middle = grad_middle + grad_y.astype(F32)
    grad_branch = grad_middle.astype(BF16)
    grad_out = across(attended, grad_branch)
    d_att = against(grad_branch, out_full).astype(BF16)
    d_att = d_att.reshape(tokens, parts, width // parts).transpose(1, 0, 2)

    dq, dk, dv = attend_back(d_att, q_all, k_all, v_all, o_all, lse_all, start)
    dq, dk, dv, grad_first = unproject(dq, dk, dv, cosine, sine)
    grad_query_w = across(hidden_in, dq)
    grad_key_w = across(hidden_in, dk)
    grad_value_w = across(hidden_in, dv)
    grad_hidden_in = against(dq, query_full) + against(dk, key_full) + against(dv, value_full)
    grad_x, grad_gain_one = norm_back(grad_hidden_in, x_in, gain_one)
    grad_x = grad_x + grad_middle
    scatter = lambda value: lax.psum_scatter(value, both, scatter_dimension=0, tiled=True)
    return (
        output,
        grad_x.reshape(inputs.shape),
        grad_first.reshape(inputs.shape),
        scatter(grad_query_w),
        scatter(grad_key_w),
        scatter(grad_value_w),
        scatter(grad_out),
        scatter(grad_gain_one),
        scatter(grad_gate),
        scatter(grad_up),
        scatter(grad_down),
        scatter(grad_gain_two),
    )


def solution(mesh):
    tokens = P("dp", "seq", None)
    matrix = P(("dp", "seq"), None)
    vector = P(("dp", "seq"))
    return jax.shard_map(
        shards,
        mesh=mesh,
        in_specs=(
            tokens, tokens, P("dp", None), matrix, matrix, matrix, matrix, vector,
            matrix, matrix, matrix, vector, tokens,
        ),
        out_specs=(
            tokens, tokens, tokens, matrix, matrix, matrix, matrix, vector,
            matrix, matrix, matrix, vector,
        ),
        check_vma=False,
    )
```

```python
import functools

import jax
import jax.numpy as jnp
from jax import lax
from jax.experimental import pallas as pl
from jax.experimental.pallas import tpu as pltpu
from jax.sharding import PartitionSpec as P

HEAD_DIM = 64
EPS = 1e-06
THETA = 10000.0
NEG = -1e30
MESH = pl.DeviceIdType.MESH
BF16 = jnp.bfloat16
F32 = jnp.float32
VMEM = pltpu.VMEM
MIB = 1 << 20


def dot(left, right, left_dim=1, right_dim=0):
    return lax.dot_general(
        left, right, (((left_dim,), (right_dim,)), ((), ())), preferred_element_type=F32
    )


def across(left, right):
    return dot(left, right, 0, 0)


def against(left, right):
    return dot(left, right, 1, 1)


def norm_back(grad_normed, values, gain):
    scale_inv = lax.rsqrt(jnp.mean(values * values, axis=-1, keepdims=True) + EPS)
    normed = values * scale_inv
    grad_scaled = grad_normed * gain
    grad_values = scale_inv * (
        grad_scaled - normed * jnp.mean(grad_scaled * normed, axis=-1, keepdims=True)
    )
    grad_gain = jnp.sum(grad_normed * normed, axis=0)
    return (grad_values, grad_gain)


def turned(values, cosine, sine):
    lane = lax.broadcasted_iota(jnp.int32, values.shape, 1) % HEAD_DIM
    other = jnp.where(
        lane < HEAD_DIM // 2,
        pltpu.roll(values, 128 - HEAD_DIM // 2, 1),
        pltpu.roll(values, HEAD_DIM // 2, 1),
    )
    return values * cosine + other * sine


def project_kernel(width, x, gain, wq, wk, wv, first, cosine, sine, q_out, k_out, v_out, h_out):
    @pl.when(pl.program_id(0) == 0)
    def _():
        values = x[...].astype(F32)
        scale = lax.rsqrt(jnp.mean(values * values, axis=-1, keepdims=True) + EPS)
        h_out[...] = (values * scale * gain[...]).astype(BF16)

    hidden = h_out[...]
    cos, sin = cosine[...], sine[...]
    for weight, out, scale in ((wq, q_out, HEAD_DIM**-0.5), (wk, k_out, 1.0)):
        raw = dot(hidden, weight[...])
        for part in range(2):
            done = turned(raw[:, part * 128 : part * 128 + 128], cos, sin) * scale
            for piece in range(128 // width):
                out[part * (128 // width) + piece] = done[
                    :, piece * width : (piece + 1) * width
                ].astype(BF16)
    mixed = (0.5 * dot(hidden, wv[...]) + 0.5 * first[...].astype(F32)).astype(BF16)
    for piece in range(256 // width):
        v_out[piece] = mixed[:, piece * width : (piece + 1) * width]


def project(x, gain, wq, wk, wv, first, cosine, sine, parts):
    tokens, dim = x.shape
    width = dim // parts
    whole = lambda shape: pl.BlockSpec(shape, lambda g: (0,) * len(shape))
    cols = lambda rows: pl.BlockSpec((rows, 256), lambda g: (0, g))
    out = pl.BlockSpec((256 // width, tokens, width), lambda g: (g, 0, 0))
    split = jax.ShapeDtypeStruct((parts, tokens, width), BF16)
    return pl.pallas_call(
        functools.partial(project_kernel, width),
        grid=(dim // 256,),
        in_specs=[
            whole((tokens, dim)),
            whole((1, dim)),
            cols(dim),
            cols(dim),
            cols(dim),
            cols(tokens),
            whole((tokens, 128)),
            whole((tokens, 128)),
        ],
        out_specs=[out, out, out, whole((tokens, dim))],
        out_shape=[split, split, split, jax.ShapeDtypeStruct((tokens, dim), BF16)],
        compiler_params=pltpu.CompilerParams(vmem_limit_bytes=40 * MIB),
        cost_estimate=pl.CostEstimate(
            flops=6 * tokens * dim * dim, bytes_accessed=16 * tokens * dim, transcendentals=0
        ),
        name="project",
    )(x, gain, wq, wk, wv, first, cosine, sine)


def unproject_kernel(width, dq, dk, dv, cosine, sine, q_out, k_out, v_out, first_out):
    cos, sin = cosine[...], sine[...]
    for part in range(2):
        lanes = slice(part * 128, part * 128 + 128)
        picks = range(part * (128 // width), (part + 1) * (128 // width))
        join = lambda ref: jnp.concatenate([ref[p] for p in picks], axis=1).astype(F32)
        q_out[:, lanes] = turned(join(dq), cos, -sin).astype(BF16)
        k_out[:, lanes] = turned(join(dk), cos, -sin).astype(BF16)
        value = 0.5 * join(dv)
        first_out[:, lanes] = value
        v_out[:, lanes] = value.astype(BF16)


def unproject(dq, dk, dv, cosine, sine):
    parts, tokens, width = dq.shape
    dim = parts * width
    split = pl.BlockSpec((256 // width, tokens, width), lambda g: (g, 0, 0))
    table = pl.BlockSpec((tokens, 128), lambda g: (0, 0))
    cols = pl.BlockSpec((tokens, 256), lambda g: (0, g))
    low = jax.ShapeDtypeStruct((tokens, dim), BF16)
    return pl.pallas_call(
        functools.partial(unproject_kernel, width),
        grid=(dim // 256,),
        in_specs=[split, split, split, table, table],
        out_specs=[cols, cols, cols, cols],
        out_shape=[low, low, low, jax.ShapeDtypeStruct((tokens, dim), F32)],
        compiler_params=pltpu.CompilerParams(vmem_limit_bytes=40 * MIB),
        name="unproject",
    )(dq, dk, dv, cosine, sine)


def greet(parts, me):
    barrier = pltpu.get_barrier_semaphore()
    for step in range(1, parts):
        pl.semaphore_signal(
            barrier, 1, device_id={"seq": lax.rem(me + step, parts)}, device_id_type=MESH
        )
    return parts - 1


def send(source, target, send_sem, recv_sem, peer):
    return pltpu.make_async_remote_copy(
        src_ref=source,
        dst_ref=target,
        send_sem=send_sem,
        recv_sem=recv_sem,
        device_id={"seq": peer},
        device_id_type=MESH,
    )


def arrive(ref, sem):
    pltpu.make_async_copy(ref, ref, sem).wait()


def own_head(values, head, width):
    if width == HEAD_DIM:
        return values
    lane = lax.broadcasted_iota(jnp.int32, values.shape, 1)
    return jnp.where(lane // HEAD_DIM == head, values, jnp.zeros_like(values))


def allowed_tile(i, j, tokens, start):
    key = j * tokens + lax.broadcasted_iota(jnp.int32, (tokens, tokens), 0)
    query = i * tokens + lax.broadcasted_iota(jnp.int32, (tokens, tokens), 1)
    return (key <= query) & (key >= start[i])


def forward_kernel(
    parts, heads, plan, count,
    q_in, k_in, v_in, start, *refs,
):
    late, ready = refs[:1], refs[1:count]
    q_all, k_all, v_all, o_all, lse_all, attended = refs[count : count + 6]
    fulls = refs[count + 6 : 2 * count + 6]
    late_held = refs[2 * count + 6]
    v_turn, total, o_send, in_send, in_recv, o_out, o_in, *sems = refs[2 * count + 7 :]
    place = Place()
    _, tokens, width = q_in.shape
    half = parts // 2
    me = lax.axis_index("seq")
    own = me // half
    place.greet(greet(parts, me))
    spread = WeightSpread(place, plan, late, late_held, ready, fulls, sems)
    pairs = ((q_in, q_all), (k_in, k_all), (v_in, v_all))

    def moved(index, peer):
        source, target = pairs[index]
        return send(
            source.at[peer], target.at[me], in_send.at[index, peer], in_recv.at[index, me], peer
        )

    def over(first, action):
        def body(step, _):
            action(first + lax.rem(me + step, half))
            return 0

        lax.fori_loop(0, half, body, 0)

    def start_cross(indices):
        over((1 - own) * half, lambda peer: [moved(index, peer).start() for index in indices])

    def sent_cross(indices):
        over((1 - own) * half, lambda peer: [moved(index, peer).wait_send() for index in indices])

    for index, (source, target) in enumerate(pairs):
        pltpu.make_async_copy(source.at[me], target.at[me], in_recv.at[index, me]).start()
    pl.when(own == 0)(lambda: start_cross((1, 2)))
    pl.when(own == 1)(lambda: start_cross((0,)))

    def start_near(peer):
        @pl.when(peer != me)
        def _():
            for index in range(3):
                moved(index, peer).start()

    over(own * half, start_near)

    def got(index, block):
        arrive(pairs[index][1].at[block], in_recv.at[index, block])

    def got_keys(block):
        got(1, block)
        got(2, block)
        v_turn[block] = v_all[block].T

    def tile(i, j, masked):
        if masked:
            allowed = allowed_tile(i, j, tokens, start)
        queries, keys = q_all[i], k_all[j]
        for head in range(heads):
            rows = slice(head * HEAD_DIM, (head + 1) * HEAD_DIM)
            scores = against(keys, own_head(queries, head, width))
            if masked:
                scores = jnp.where(allowed, scores, NEG)
            old = lse_all[i, head]
            new = jnp.maximum(old, jnp.max(scores, axis=0, keepdims=True))
            weights = jnp.exp(scores - new)
            factor = jnp.exp(old - new)
            lse_all[i, head] = new
            total[i, head] = total[i, head] * factor + jnp.sum(weights, axis=0, keepdims=True)
            o_all[i, rows] = o_all[i, rows] * factor + dot(
                v_turn[j, rows], weights.astype(BF16)
            )

    def tile_row(row, _):
        phase, place_in = row // half, lax.rem(row, half)
        lower = jnp.where(phase == 0, own, 1 - own) * half
        i = jnp.where(phase == 1, half, lower) + place_in
        first = jnp.where(phase == 1, 0, lower)
        last = jnp.where(phase == 1, half, i + 1)
        spread.at_row(row, 3 * half)

        @pl.when(phase == 0)
        def _():
            got(0, i)
            got_keys(i)

        @pl.when((row == half) & (own == 0))
        def _():
            lax.fori_loop(half, parts, lambda block, _: got(0, block) or 0, 0)

        @pl.when((row == half) & (own == 1))
        def _():
            sent_cross((0,))
            start_cross((1, 2))
            lax.fori_loop(0, half, lambda block, _: got_keys(block) or 0, 0)

        @pl.when((row == 2 * half) & (own == 0))
        def _():
            sent_cross((1, 2))
            start_cross((0,))

        @pl.when((phase == 2) & (own == 0))
        def _():
            got_keys(i)

        @pl.when((phase == 2) & (own == 1))
        def _():
            got(0, i)

        @pl.when((phase == 0) | ((phase == 1) & (own == 0)) | ((phase == 2) & (own == 1)))
        def _():
            lse_all[i] = jnp.full(lse_all.shape[1:], NEG, F32)
            total[i] = jnp.zeros(total.shape[1:], F32)
            o_all[i] = jnp.zeros(o_all.shape[1:], F32)

        def key_block(j, _):
            masked = (j == 0) | (j == i) | (i == parts - 1)
            pl.when(masked)(lambda: tile(i, j, True))
            pl.when(jnp.logical_not(masked))(lambda: tile(i, j, False))
            return 0

        lax.fori_loop(first, last, key_block, 0)

        @pl.when(((phase == 0) & (own == 0)) | ((phase == 1) & (own == 1)) | (phase == 2))
        def _():
            for head in range(heads):
                rows = slice(head * HEAD_DIM, (head + 1) * HEAD_DIM)
                o_all[i, rows] = o_all[i, rows] / total[i, head]
                lse_all[i, head] = lse_all[i, head] + jnp.log(total[i, head])
            o_send[i] = o_all[i].T.astype(BF16)

            @pl.when(i == me)
            def _():
                pltpu.make_async_copy(o_send.at[i], attended.at[me], o_in.at[me]).start()

            @pl.when(i != me)
            def _():
                send(o_send.at[i], attended.at[me], o_out.at[i], o_in.at[me], i).start()

        return 0

    lax.fori_loop(0, 3 * half, tile_row, 0)
    spread.finish()
    pl.when(own == 0)(lambda: sent_cross((0,)))
    pl.when(own == 1)(lambda: sent_cross((1, 2)))

    def sent_near(peer):
        @pl.when(peer != me)
        def _():
            for index in range(3):
                moved(index, peer).wait_send()

    over(own * half, sent_near)

    def finish(step, _):
        peer = lax.rem(me + step, parts)
        arrive(o_send.at[peer], o_out.at[peer])
        arrive(attended.at[peer], o_in.at[peer])
        return 0

    lax.fori_loop(1, parts, finish, 0)
    arrive(attended.at[me], o_in.at[me])


def attend(q, k, v, start, late, ready):
    parts, tokens, width = q.shape
    heads = width // HEAD_DIM
    place = Place()
    whole = pl.BlockSpec(memory_space=VMEM)
    far = pl.BlockSpec(memory_space=pl.ANY)
    split = jax.ShapeDtypeStruct(q.shape, BF16)
    flops = 4 * parts * parts * tokens * tokens * width // 2
    held = jax.ShapeDtypeStruct((place.as_, *late.shape), late.dtype)
    shapes = [late.shape] + [value.shape[1:] for value in ready]
    fulls = [
        jax.ShapeDtypeStruct((place.xs, 2, place.as_, place.bs, *shape), BF16) for shape in shapes
    ]
    plan = WeightSpread.plan(shapes)
    results = pl.pallas_call(
        functools.partial(forward_kernel, parts, heads, plan, len(shapes)),
        in_specs=[whole] * 4 + [far] * len(shapes),
        out_specs=[whole] * 6 + [far] * (len(shapes) + 1),
        out_shape=[
            split,
            split,
            split,
            jax.ShapeDtypeStruct((parts, width, tokens), F32),
            jax.ShapeDtypeStruct((parts, heads, 1, tokens), F32),
            split,
            *fulls,
            held,
        ],
        scratch_shapes=[
            VMEM((parts, width, tokens), BF16),
            VMEM((parts, heads, 1, tokens), F32),
            VMEM((parts, tokens, width), BF16),
            pltpu.SemaphoreType.DMA((3, parts)),
            pltpu.SemaphoreType.DMA((3, parts)),
            pltpu.SemaphoreType.DMA((parts,)),
            pltpu.SemaphoreType.DMA((parts,)),
            *WeightSpread.semaphores(place, plan),
        ],
        compiler_params=pltpu.CompilerParams(
            collective_id=1, has_side_effects=True, vmem_limit_bytes=48 * MIB
        ),
        cost_estimate=pl.CostEstimate(
            flops=4 * flops, bytes_accessed=16 * q.size, transcendentals=flops // 256
        ),
        name="attend",
    )(q, k, v, start, late, *ready)
    devices = place.xs * 2 * place.as_ * place.bs
    weights = [value.reshape(devices, *value.shape[4:]) for value in results[6:-1]]
    return results[:6], weights


def backward_kernel(
    parts, heads, plan, count,
    d_in, q_all, k_all, v_all, o_all, lse_all, start, *refs,
):
    grads = refs[:count]
    dq_got, dk_got, dv_got = refs[count : count + 3]
    results = refs[count + 3 : 2 * count + 3]
    refs = refs[2 * count + 3 :]
    d_all, k_turn, delta, dq_turn, dk_sum, dv_sum, dq_send, dk_send, dv_send = refs[:9]
    in_send, in_recv, out_send, out_recv, *buffers = refs[9:]
    place = Place()
    _, tokens, width = d_in.shape
    half = parts // 2
    me = lax.axis_index("seq")
    own = me // half
    place.greet(greet(parts, me))
    adding = GradSums(place, plan, grads, results, buffers)

    def over(first, action):
        def body(step, _):
            action(first + lax.rem(me + step, half))
            return 0

        lax.fori_loop(0, half, body, 0)

    def moved(peer):
        return send(d_in.at[peer], d_all.at[me], in_send.at[peer], in_recv.at[me], peer)

    over((1 - own) * half, lambda peer: moved(peer).start())
    pltpu.make_async_copy(d_in.at[me], d_all.at[me], in_recv.at[me]).start()

    def start_near(peer):
        pl.when(peer != me)(lambda: moved(peer).start())

    over(own * half, start_near)
    sends = ((dq_send, dq_got), (dk_send, dk_got), (dv_send, dv_got))

    def give(index, block):
        source, target = sends[index]

        @pl.when(block == me)
        def _():
            pltpu.make_async_copy(
                source.at[block], target.at[me], out_recv.at[index, me]
            ).start()

        @pl.when(block != me)
        def _():
            send(
                source.at[block], target.at[me],
                out_send.at[index, block], out_recv.at[index, me], block,
            ).start()

    def give_query(i):
        dq_send[i] = (dq_turn[i] * HEAD_DIM**-0.5).T.astype(BF16)
        give(0, i)

    def give_keys(j):
        dk_send[j] = dk_sum[j].astype(BF16)
        dv_send[j] = dv_sum[j].astype(BF16)
        give(1, j)
        give(2, j)

    def tile(i, j, masked):
        if masked:
            allowed = allowed_tile(i, j, tokens, start)
        queries, grads_out, keys, mixed = q_all[i], d_all[i], k_all[j], v_all[j]
        for head in range(heads):
            rows = slice(head * HEAD_DIM, (head + 1) * HEAD_DIM)
            query, grad = own_head(queries, head, width), own_head(grads_out, head, width)
            scores = against(keys, query)
            if masked:
                scores = jnp.where(allowed, scores, NEG)
            weights = jnp.exp(scores - lse_all[i, head])
            dv_sum[j] += dot(weights.astype(BF16), grad)
            slope = against(mixed, grad) - delta[i, head]
            d_scores = (weights * slope).astype(BF16)
            dk_sum[j] += dot(d_scores, query)
            dq_turn[i, rows] += dot(k_turn[j, rows], d_scores)

    def prepare(block):
        arrive(d_all.at[block], in_recv.at[block])
        product = d_all[block].astype(F32).T * o_all[block]
        for head in range(heads):
            rows = slice(head * HEAD_DIM, (head + 1) * HEAD_DIM)
            delta[block, head] = jnp.sum(product[rows], axis=0, keepdims=True)
        k_turn[block] = k_all[block].T
        dq_turn[block] = jnp.zeros(dq_turn.shape[1:], F32)
        dk_sum[block] = jnp.zeros(dk_sum.shape[1:], F32)
        dv_sum[block] = jnp.zeros(dv_sum.shape[1:], F32)

    def tile_row(row, _):
        phase, place_in = row // half, lax.rem(row, half)
        adding.at_row(row, 3 * half)

        @pl.when(row == 0)
        def _():
            lax.fori_loop(0, half, lambda n, _: prepare(own * half + n) or 0, 0)

        @pl.when(row == half)
        def _():
            lax.fori_loop(0, half, lambda n, _: prepare((1 - own) * half + n) or 0, 0)

        by_query = jnp.where(phase == 1, own == 1, own == 0)
        lower = jnp.where(phase == 0, own, 1 - own) * half
        outer = jnp.where(
            phase == 2, jnp.where(by_query, half, 0), lower
        ) + place_in
        first = jnp.where(phase == 2, jnp.where(by_query, 0, half), jnp.where(by_query, lower, outer))
        last = jnp.where(
            phase == 2,
            jnp.where(by_query, half, parts),
            jnp.where(by_query, outer + 1, lower + half),
        )

        def inner_block(inner, _):
            i, j = jnp.where(by_query, outer, inner), jnp.where(by_query, inner, outer)
            masked = (j == 0) | (j == i) | (i == parts - 1)
            pl.when(masked)(lambda: tile(i, j, True))
            pl.when(jnp.logical_not(masked))(lambda: tile(i, j, False))
            return 0

        lax.fori_loop(first, last, inner_block, 0)
        pl.when(by_query)(lambda: give_query(outer))
        pl.when(jnp.logical_not(by_query))(lambda: give_keys(outer))
        return 0

    lax.fori_loop(0, 3 * half, tile_row, 0)
    pl.when(own == 0)(lambda: over(0, give_keys))
    pl.when(own == 1)(lambda: over(half, give_query))
    adding.finish()

    def finish(step, _):
        peer = lax.rem(me + step, parts)
        moved(peer).wait_send()
        for index, (source, target) in enumerate(sends):
            arrive(source.at[peer], out_send.at[index, peer])
            arrive(target.at[peer], out_recv.at[index, peer])
        return 0

    lax.fori_loop(1, parts, finish, 0)
    for index, (_, target) in enumerate(sends):
        arrive(target.at[me], out_recv.at[index, me])


def attend_back(d_att, q, k, v, o, lse, start, grads):
    parts, tokens, width = q.shape
    heads = width // HEAD_DIM
    place = Place()
    whole = pl.BlockSpec(memory_space=VMEM)
    far = pl.BlockSpec(memory_space=pl.ANY)
    split = jax.ShapeDtypeStruct(q.shape, BF16)
    flops = 10 * parts * parts * tokens * tokens * width // 2
    plan, sum_shapes, sum_scratch = GradSums.plan(place, grads)
    grads = [placed(place, grad) for grad in grads]
    results = pl.pallas_call(
        functools.partial(backward_kernel, parts, heads, plan, len(grads)),
        in_specs=[far] + [whole] * 6 + [far] * len(grads),
        out_specs=[far] * 3 + [whole] * len(grads),
        out_shape=[split] * 3 + sum_shapes,
        scratch_shapes=[
            VMEM((parts, tokens, width), BF16),
            VMEM((parts, width, tokens), BF16),
            VMEM((parts, heads, 1, tokens), F32),
            VMEM((parts, width, tokens), F32),
            VMEM((parts, tokens, width), F32),
            VMEM((parts, tokens, width), F32),
            VMEM((parts, tokens, width), BF16),
            VMEM((parts, tokens, width), BF16),
            VMEM((parts, tokens, width), BF16),
            pltpu.SemaphoreType.DMA((parts,)),
            pltpu.SemaphoreType.DMA((parts,)),
            pltpu.SemaphoreType.DMA((3, parts)),
            pltpu.SemaphoreType.DMA((3, parts)),
            *sum_scratch,
        ],
        compiler_params=pltpu.CompilerParams(
            collective_id=2, has_side_effects=True, vmem_limit_bytes=60 * MIB
        ),
        cost_estimate=pl.CostEstimate(
            flops=4 * flops, bytes_accessed=20 * q.size, transcendentals=flops // 640
        ),
        name="attend_back",
    )(d_att, q, k, v, o, lse, start, *grads)
    return results[:3], results[3:]


class Place:
    def __init__(self):
        self.xs = lax.axis_size("dp") // 2
        seq = lax.axis_size("seq")
        self.bs = 2 if seq <= 8 else 4
        self.as_ = seq // self.bs
        dp, rank = lax.axis_index("dp"), lax.axis_index("seq")
        self.x, self.core = dp // 2, lax.rem(dp, 2)
        self.a, self.b = rank // self.bs, lax.rem(rank, self.bs)

    def device(self, x=None, core=None, a=None, b=None):
        x, core = (self.x if x is None else x), (self.core if core is None else core)
        a, b = (self.a if a is None else a), (self.b if b is None else b)
        return (x * 2 + core, a * self.bs + b)

    def peers(self, axis):
        size = {"x": self.xs, "a": self.as_, "b": self.bs}[axis]
        own = getattr(self, axis)
        return [(step - 1, lax.rem(own + step, size)) for step in range(1, size)]

    def greet(self, greeted=0):
        barrier = pltpu.get_barrier_semaphore()
        others = [self.device(core=1 - self.core)]
        for axis in "x" if greeted else "xab":
            others += [self.device(**{axis: index}) for _, index in self.peers(axis)]
        for other in others:
            pl.semaphore_signal(barrier, 1, device_id=other, device_id_type=MESH)
        pl.semaphore_wait(barrier, len(others) + greeted)

    @property
    def inner(self):
        return (self.a == 1) | (self.a == 2)

    @property
    def beside(self):
        return self.a + 1 - 2 * lax.rem(self.a, 2)


def column_pieces(columns, wanted):
    tiles = columns // 128
    wanted = min(wanted, tiles)
    edges = [tiles * n // wanted * 128 for n in range(wanted)] + [columns]
    return [(edges[n], edges[n + 1] - edges[n]) for n in range(wanted)]


def placed(place, value):
    return value.reshape(place.xs, 2, place.as_, place.bs, *value.shape[1:])


def remote(source, target, send_sem, recv_sem, device):
    return pltpu.make_async_remote_copy(
        src_ref=source,
        dst_ref=target,
        send_sem=send_sem,
        recv_sem=recv_sem,
        device_id=device,
        device_id_type=MESH,
    )


def flat(ref):
    rows, columns = ref.shape[-2:]
    return ref.reshape(ref.size // (rows * columns), rows, columns)


class Relay:
    def __init__(self, place, source, target, sems):
        self.p, self.source, self.target, self.sems = place, source, target, sems
        assert place.as_ == 4

    def near(self):
        p = self.p
        return remote(
            self.source, self.target.at[p.a],
            self.sems.at[0, 0], self.sems.at[1, 0], p.device(a=p.beside),
        )

    def middle(self):
        p = self.p
        held = self.target.at[pl.ds(p.a // 2 * 2, 2)]
        return remote(
            held, held, self.sems.at[0, 1], self.sems.at[1, 1], p.device(a=3 - p.a)
        )

    def outward(self):
        p = self.p
        held = self.target.at[pl.ds((1 - p.a // 2) * 2, 2)]
        return remote(
            held, held, self.sems.at[0, 2], self.sems.at[1, 1], p.device(a=p.beside)
        )

    def local(self):
        return pltpu.make_async_copy(self.source, self.target.at[self.p.a], self.sems.at[1, 2])

    def step(self, number):
        if number == 0:
            self.local().start()
            self.near().start()
        elif number == 1:
            self.local().wait()
            self.near().wait_recv()
            pl.when(self.p.inner)(lambda: self.middle().start())
        elif number == 2:

            @pl.when(self.p.inner)
            def _():
                self.middle().wait_recv()
                self.outward().start()
        else:

            @pl.when(jnp.logical_not(self.p.inner))
            def _():
                self.middle().wait_recv()

            @pl.when(self.p.inner)
            def _():
                self.middle().wait_send()
                self.outward().wait_send()

            self.near().wait_send()


class Spread:
    def __init__(self, place, source, full, order, sems, copied):
        self.place, self.order, self.sems, self.copied = place, order, sems, copied
        self.source, self.full = source, full

    def moves(self, number):
        p, full = self.place, self.full
        if number == 2:
            held = full.at[:, p.core]
            return [(held, held, 0, p.device(core=1 - p.core))]
        held = full.at[p.x, p.core, :, p.b]
        source = self.source if number == 0 and self.copied else held
        if number == 1:
            source = held = full.at[:, p.core, :, p.b] if self.order == "xb" else full.at[p.x, p.core]
        axis = self.order[number]
        return [(source, held, s, p.device(**{axis: index})) for s, index in p.peers(axis)]

    def copies(self, number):
        base = sum([len(self.place.peers(axis)) for axis in self.order][:number])
        return [
            remote(source, target, self.sems.at[0, base + s], self.sems.at[1, base + s], device)
            for source, target, s, device in self.moves(number)
        ]

    def local(self):
        p = self.place
        return pltpu.make_async_copy(
            self.source, self.full.at[p.x, p.core, :, p.b], self.sems.at[2, 0]
        )

    def start(self, number):
        if number == 0 and self.copied:
            self.local().start()
        for copy in self.copies(number):
            copy.start()

    def finish(self, number):
        if number == 0 and self.copied:
            self.local().wait()
        for copy in self.copies(number):
            copy.wait_recv()
            copy.wait_send()


def spread_semaphores(place):
    return pltpu.SemaphoreType.DMA((3, place.xs + place.bs - 1))


RELAY_SEMAPHORES = (2, 3)


class WeightSpread:
    def __init__(self, place, plan, late, late_held, ready, fulls, sems):
        self.relays = []
        self.units = []
        for number, (array, start, size, order) in enumerate(plan):
            columns = (slice(None),) * 4 + (slice(None), pl.ds(start, size))
            full = fulls[array].at[columns]
            if array == 0:
                held = late_held.at[:, :, pl.ds(start, size)]
                relay = Relay(place, late[0].at[:, pl.ds(start, size)], held, sems[0].at[number])
                self.relays.append(relay)
            else:
                held = ready[array - 1].at[:, :, pl.ds(start, size)]
            self.units.append(Spread(place, held, full, order, sems[1 + number], True))

    @staticmethod
    def plan(shapes):
        plan = []
        for array, shape in enumerate(shapes):
            small = array == 1
            for start, size in column_pieces(shape[1], 1 if small else 2):
                plan.append((array, start, size, "xb" if small else "bx"))
        return plan

    @staticmethod
    def semaphores(place, plan):
        return [pltpu.SemaphoreType.DMA((len(plan), *RELAY_SEMAPHORES))] + [
            spread_semaphores(place) for _ in plan
        ]

    def actions(self):
        late, ready = self.units[: len(self.relays)], self.units[len(self.relays) :]
        ready = sorted(ready, key=lambda unit: unit.order != "xb")
        done = [(0, functools.partial(unit.start, 0)) for unit in ready]
        relay = lambda number: [functools.partial(r.step, number) for r in self.relays]
        next_step = lambda unit, number: (
            lambda: (unit.finish(number), unit.start(number + 1)) if number < 2 else unit.finish(2)
        )
        done += [(0, action) for action in relay(0)]
        done += [(1, action) for action in relay(1)]
        done += [(2, next_step(ready[0], 0))]
        done += [(3, action) for action in relay(2)]
        done += [(4, next_step(unit, 0)) for unit in ready[1:3]]
        done += [(5, action) for action in relay(3)]
        done += [(5, functools.partial(unit.start, 0)) for unit in late]
        done += [(6, next_step(unit, 0)) for unit in ready[3:]]
        done += [(8, next_step(unit, 0)) for unit in late]
        done += [(9, next_step(unit, 1)) for unit in ready[:2]]
        done += [(10, next_step(unit, 1)) for unit in ready[2:3]]
        done += [(12, next_step(unit, 1)) for unit in ready[3:] + late]
        done += [(12, next_step(unit, 2)) for unit in ready + late]
        return done

    def at_row(self, row, count):
        rows = sorted({at for at, _ in self.actions() if at < 12})
        for at in rows:

            @pl.when(row == at * count // 12)
            def _():
                for own_row, action in self.actions():
                    if own_row == at:
                        action()

    def finish(self):
        for at, action in self.actions():
            if at >= 12:
                action()


def gather_kernel(plan, count, halves, *refs):
    place = Place()
    total = count + halves
    sources, results = refs[:total], refs[total : 2 * total]
    relay_sems, *sems = refs[2 * total :]
    place.greet()
    units, relays = [], []
    for number, (array, start, size, order) in enumerate(plan):
        source = sources[array].at[:, pl.ds(start, size)]
        if array < count:
            full = results[array].at[:, :, :, :, :, pl.ds(start, size)]
            held = full.at[place.x, place.core, :, place.b]
            units.append(Spread(place, None, full, order, sems[number], False))
        else:
            held = results[array].at[:, :, pl.ds(start, size)]
        relays.append(Relay(place, source, held, relay_sems.at[number]))
    first = len(units)

    def act(index, number):
        if number < 4:
            relays[index].step(number)
            if number == 3:
                units[index].start(0)
        else:
            units[index].finish(number - 4)
            if number < 6:
                units[index].start(number - 3)

    for relay in relays[:first]:
        relay.step(0)
    for number in (1, 2, 3):
        for index in range(first):
            act(index, number)
        for relay in relays[first:] if number == 3 else []:
            relay.step(0)
    for index in range(first):
        act(index, 4)
    for relay in relays[first:]:
        relay.step(1)
    for index in range(first):
        act(index, 5)
    for relay in relays[first:]:
        relay.step(2)
    for index in range(first):
        act(index, 6)
    for relay in relays[first:]:
        relay.step(3)


def gathered(arrays, partly, collective_id):
    place = Place()
    xs, as_, bs = place.xs, place.as_, place.bs
    both = [*arrays, *partly]
    plan = []
    for number, array in enumerate(both):
        pieces = column_pieces(array.shape[1], 2)
        for place_in, (start, size) in enumerate(pieces):
            plan.append((number, start, size, "xb" if place_in == 0 else "bx"))
    full = [jax.ShapeDtypeStruct((xs, 2, as_, bs, *array.shape), array.dtype) for array in arrays]
    full += [jax.ShapeDtypeStruct((as_, *array.shape), array.dtype) for array in partly]
    count = len([piece for piece in plan if piece[0] < len(arrays)])
    results = pl.pallas_call(
        functools.partial(gather_kernel, plan, len(arrays), len(partly)),
        in_specs=[pl.BlockSpec(memory_space=pl.ANY)] * len(both),
        out_specs=[pl.BlockSpec(memory_space=pl.ANY)] * len(both),
        out_shape=full,
        scratch_shapes=[
            pltpu.SemaphoreType.DMA((len(plan), *RELAY_SEMAPHORES)),
            *[spread_semaphores(place)] * count,
        ],
        compiler_params=pltpu.CompilerParams(collective_id=collective_id, has_side_effects=True),
        cost_estimate=pl.CostEstimate(
            flops=0, bytes_accessed=sum(array.size for array in arrays) * 64, transcendentals=0
        ),
        name="gathered",
    )(*both)
    devices = xs * 2 * as_ * bs
    return [
        result.reshape(devices, *result.shape[4:]) for result in results[: len(arrays)]
    ] + list(results[len(arrays) :])


def add_up(mine, others):
    lead = mine.shape[:-2]

    def at(ref, step):
        index = []
        for size in reversed(lead):
            index.insert(0, lax.rem(step, size))
            step = step // size
        return ref.at[tuple(index)]

    def body(step, _):
        total = at(mine, step)[...].astype(F32)
        for other in others:
            total += at(other, step)[...].astype(F32)
        at(mine, step)[...] = total.astype(mine.dtype)
        return 0

    count = 1
    for size in lead:
        count *= size
    lax.fori_loop(0, count, body, 0)


class RelaySum:
    def __init__(self, place, own, inward, middle, last, sems, result):
        self.p, self.own, self.sems, self.result = place, own, sems, result
        self.inward, self.middle, self.last = inward, middle, last
        assert place.as_ == 4

    def move(self, number):
        p = self.p
        far = self.own.at[pl.ds((1 - p.a // 2) * 2, 2)]
        if number == 0:
            source, target, device = far, self.inward, p.beside
        elif number == 1:
            source, target, device = far, self.middle, 3 - p.a
        else:
            source, target, device = self.own.at[p.beside], self.last, p.beside
        return remote(
            source, target, self.sems.at[0, number], self.sems.at[1, number], p.device(a=device)
        )

    def step(self, number):
        p, inner = self.p, self.p.inner
        outer = jnp.logical_not(inner)
        if number == 0:
            pl.when(outer)(lambda: self.move(0).start())
            pl.when(outer)(lambda: self.move(2).start())
        elif number == 1:

            @pl.when(inner)
            def _():
                self.move(0).wait_recv()
                add_up(self.own.at[pl.ds((1 - p.a // 2) * 2, 2)], [self.inward])
                self.move(1).start()
        elif number == 2:

            @pl.when(inner)
            def _():
                self.move(1).wait_recv()
                add_up(self.own.at[pl.ds(p.a // 2 * 2, 2)], [self.middle])
                self.move(2).start()
        else:
            self.move(2).wait_recv()
            self.result[...] = self.own[p.a].astype(F32) + self.last[...].astype(F32)
            pl.when(outer)(lambda: self.move(0).wait_send())
            pl.when(inner)(lambda: self.move(1).wait_send())
            self.move(2).wait_send()

    @staticmethod
    def scratch(rows, columns, dtype):
        return [
            VMEM((2, rows, columns), dtype),
            VMEM((2, rows, columns), dtype),
            VMEM((rows, columns), dtype),
            pltpu.SemaphoreType.DMA((2, 3)),
        ]


class Sum:
    def __init__(self, place, source, order, buffers):
        self.place, self.order, self.source = place, order, source
        self.own, self.got0, self.got1, self.got2, self.sems = buffers

    @property
    def held(self):
        return self.own.at[self.place.x, :, self.place.b]

    def moves(self, number):
        p = self.place
        if number == 0:
            return [(self.source.at[:, 1 - p.core], self.got0, 0, p.device(core=1 - p.core))]
        axis = self.order[number - 1]
        got = self.got1 if number == 1 else self.got2
        moves = []
        for slot, index in p.peers(axis):
            if axis == "x":
                piece = self.own.at[index] if number == 1 else self.own.at[index, :, p.b]
            else:
                piece = self.own.at[:, :, index] if number == 1 else self.own.at[p.x, :, index]
            moves.append((piece, got.at[slot], slot, p.device(**{axis: index})))
        return moves

    def copies(self, number):
        base = sum(([1] + [len(self.place.peers(axis)) for axis in self.order])[:number])
        return [
            remote(source, target, self.sems.at[0, base + s], self.sems.at[1, base + s], device)
            for source, target, s, device in self.moves(number)
        ]

    def local(self):
        return pltpu.make_async_copy(
            self.source.at[:, self.place.core], self.own, self.sems.at[2, 0]
        )

    def start(self, number):
        for copy in self.copies(number):
            copy.start()
        if number == 0:
            self.local().start()

    def finish(self, number):
        p = self.place
        if number == 0:
            self.local().wait()
        for copy in self.copies(number):
            copy.wait_recv()
            copy.wait_send()
        if number == 0:
            add_up(self.own, [self.got0])
        else:
            if number == 2:
                mine = self.held
            else:
                mine = self.own.at[p.x] if self.order[0] == "x" else self.own.at[:, :, p.b]
            got = self.got1 if number == 1 else self.got2
            add_up(mine, [got.at[slot] for slot in range(len(p.peers(self.order[number - 1])))])

    @staticmethod
    def scratch(place, rows, size, order, dtype):
        xs, as_, bs = place.xs, place.as_, place.bs
        shapes = {
            "x": ((xs - 1, as_, bs, rows, size), (xs - 1, as_, rows, size)),
            "b": ((bs - 1, xs, as_, rows, size), (bs - 1, as_, rows, size)),
        }
        return [
            VMEM((xs, as_, bs, rows, size), dtype),
            VMEM((xs, as_, bs, rows, size), dtype),
            VMEM(shapes[order[0]][0], dtype),
            VMEM(shapes[order[1]][1], dtype),
            pltpu.SemaphoreType.DMA((3, xs + bs - 1)),
        ]


class GradSums:
    WHOLE = 2

    def __init__(self, place, plan, grads, results, buffers):
        self.place = place
        self.units, self.relays, self.results = [], [], []
        for array, start, size, order in plan:
            source = grads[array].at[:, :, :, :, :, pl.ds(start, size)]
            unit, buffers = Sum(place, source, order, buffers[:5]), buffers[5:]
            self.units.append(unit)
            if array < self.WHOLE:
                result = results[array].at[:, pl.ds(start, size)]
                self.relays.append(RelaySum(place, unit.held, *buffers[:4], result))
                buffers = buffers[4:]
            else:
                self.relays.append(None)
                self.results.append((unit, results[array], start, size))

    @classmethod
    def plan(cls, place, grads):
        plan, scratch, shapes = [], [], []
        for array, grad in enumerate(grads):
            rows, columns = grad.shape[1:]
            small = array == len(grads) - 1
            order = "bx" if small else "xb"
            for start, size in column_pieces(columns, 1 if small else 2):
                plan.append((array, start, size, order))
                scratch += Sum.scratch(place, rows, size, order, grad.dtype)
                if array < cls.WHOLE:
                    scratch += RelaySum.scratch(rows, size, grad.dtype)
            whole = array < cls.WHOLE
            shape = (rows, columns) if whole else (place.as_, rows, columns)
            shapes.append(jax.ShapeDtypeStruct(shape, F32 if whole else grad.dtype))
        return plan, shapes, scratch

    def actions(self):
        units = self.units
        count = len(units)

        def step(index, number):
            def action():
                units[index].finish(number)
                if number < 2:
                    units[index].start(number + 1)
                elif self.relays[index]:
                    self.relays[index].step(0)

            return action

        def relay(index, number):
            return lambda: self.relays[index].step(number)

        done = [(0, functools.partial(unit.start, 0)) for unit in units]
        first = [(0, 0), (1, 1), (1, 2), (2, 3), (2, 4), (3, 5), (3, 6)]
        done += [(row, step(index, 0)) for row, index in first]
        done += [(4, step(count - 1, 1)), (5, step(0, 1)), (7, step(1, 1)), (8, step(0, 2))]
        done += [(9, step(2, 1)), (9, relay(0, 1)), (9, step(1, 2)), (10, relay(0, 2))]
        done += [(10, relay(1, 1)), (11, step(3, 1)), (11, step(2, 2)), (11, relay(0, 3))]
        done += [(11, relay(1, 2)), (11, step(count - 1, 2))]
        done += [(12, step(3, 2)), (12, relay(2, 1)), (12, relay(3, 1)), (12, relay(1, 3))]
        done += [(12, relay(2, 2)), (12, relay(3, 2))]
        done += [(12, step(index, 1)) for index in range(4, count - 1)]
        done += [(12, relay(2, 3)), (12, relay(3, 3))]
        done += [(12, step(index, 2)) for index in range(4, count - 1)]
        return done

    def at_row(self, row, count):
        rows = sorted({at for at, _ in self.actions() if at < 12})
        for at in rows:

            @pl.when(row == at * count // 12)
            def _():
                for own_row, action in self.actions():
                    if own_row == at:
                        action()

    def finish(self):
        for at, action in self.actions():
            if at >= 12:
                action()
        for unit, result, start, size in self.results:
            result[:, :, pl.ds(start, size)] = unit.held[...]


def sums_kernel(plan, count, relayed, *refs):
    place = Place()
    total = count + relayed
    sources, results, buffers = refs[:total], refs[total : 2 * total], refs[2 * total :]
    place.greet()
    units, relays = [], []
    for array, start, size, order in plan:
        result = results[array].at[:, pl.ds(start, size)]
        if array < count:
            source = sources[array].at[:, :, :, :, :, pl.ds(start, size)]
            unit, buffers = Sum(place, source, order, buffers[:5]), buffers[5:]
            units.append(unit)
            own = unit.held
        else:
            own, buffers = buffers[0], buffers[1:]
            own[...] = sources[array][:, :, pl.ds(start, size)]
        relays.append(RelaySum(place, own, *buffers[:4], result))
        buffers = buffers[4:]
    first = len(units)
    for unit in units:
        unit.start(0)
    for relay in relays[first:]:
        relay.step(0)
    for unit in units:
        unit.finish(0)
        unit.start(1)
    for relay in relays[first:]:
        relay.step(1)
    for number in (1, 2):
        for unit, relay in zip(units, relays):
            unit.finish(number)
            if number == 1:
                unit.start(2)
            else:
                relay.step(0)
        for relay in relays[first:]:
            relay.step(number + 1)
    for number in (1, 2, 3):
        for relay in relays[:first]:
            relay.step(number)


def sums(arrays, partly, collective_id):
    place = Place()
    plan, scratch = [], []
    for number, array in enumerate([*arrays, *partly]):
        rows, columns = array.shape[1:]
        for place_in, (start, size) in enumerate(column_pieces(columns, 2)):
            order = "xb" if place_in == 0 else "bx"
            plan.append((number, start, size, order))
            if number < len(arrays):
                scratch += Sum.scratch(place, rows, size, order, array.dtype)
            else:
                scratch.append(VMEM((place.as_, rows, size), array.dtype))
            scratch += RelaySum.scratch(rows, size, array.dtype)
    both = [placed(place, array) for array in arrays] + list(partly)
    far, whole = pl.BlockSpec(memory_space=pl.ANY), pl.BlockSpec(memory_space=VMEM)
    return pl.pallas_call(
        functools.partial(sums_kernel, plan, len(arrays), len(partly)),
        in_specs=[far] * len(arrays) + [whole] * len(partly),
        out_specs=[whole] * len(both),
        out_shape=[jax.ShapeDtypeStruct(array.shape[-2:], F32) for array in both],
        scratch_shapes=scratch,
        compiler_params=pltpu.CompilerParams(
            collective_id=collective_id, has_side_effects=True, vmem_limit_bytes=48 * MIB
        ),
        cost_estimate=pl.CostEstimate(
            flops=0, bytes_accessed=sum(array.size for array in arrays) * 4, transcendentals=0
        ),
        name="sums",
    )(*both)


def stacked(value, devices):
    rows, columns = value.shape[0] // devices, value.shape[1]
    fold = 1
    while rows * fold % 16:
        fold *= 2
    value = value.reshape(devices, rows, fold, columns // fold)
    return value.transpose(0, 2, 1, 3).reshape(devices, rows * fold, columns // fold)


def unstacked(value, rows):
    devices, high, columns = value.shape
    value = value.reshape(devices, high // rows, rows, columns).transpose(0, 2, 1, 3)
    return value.reshape(devices * rows, high // rows * columns)


def shards(
    inputs, first_values, lengths, w_query, w_key, w_value, w_out, gain_attn,
    w_gate, w_up, w_down, gain_mlp, cotangent,
):
    row_count, tokens, width = inputs.shape
    assert row_count == 1
    parts = lax.axis_size("seq")
    rank = lax.axis_index("seq")
    devices = lax.axis_size("dp") * parts
    rows, down_rows = w_query.shape[0], w_down.shape[0]
    multiple = 16 if down_rows >= 64 else 8
    down_padded = -(-down_rows // multiple) * multiple

    def spaced(value):
        value = value.reshape(rows, devices, down_rows)
        value = jnp.pad(value, ((0, 0), (0, 0), (0, down_padded - down_rows)))
        return value.reshape(rows, devices * down_padded)

    gains = jnp.pad(jnp.stack([gain_attn, gain_mlp]), ((0, 14), (0, 128 - rows)))
    wide = lambda value: stacked(value, 1)[0]
    query_full, key_full, value_full, gains, *ready = gathered(
        [wide(w_query), wide(w_key), wide(w_value), gains],
        [wide(w_out), wide(spaced(w_gate)), wide(spaced(w_up))],
        3,
    )
    late = wide(jnp.pad(w_down, ((0, down_padded - down_rows), (0, 0))))
    tall = lambda value: unstacked(value, rows)
    query_full, key_full, value_full = tall(query_full), tall(key_full), tall(value_full)
    gain_one, gain_two = (gains[:, n, :rows].reshape(width).astype(F32) for n in range(2))

    ends = jnp.cumsum(lengths[0])
    begins = ends - lengths[0]
    time = jnp.arange(tokens * parts, dtype=jnp.int32)
    inside = (time[:, None] >= begins[None, :]) & (time[:, None] < ends[None, :])
    start_all = jnp.sum(jnp.where(inside, begins[None, :], 0), axis=1)
    own_start = lax.dynamic_slice_in_dim(start_all, rank * tokens, tokens)
    position = (rank * tokens + jnp.arange(tokens, dtype=jnp.int32) - own_start).astype(F32)
    half = HEAD_DIM // 2
    angles = position[:, None] * THETA ** (-jnp.arange(half, dtype=F32) * 2.0 / HEAD_DIM)
    cosine = jnp.tile(jnp.cos(angles), (1, 4))
    sine = jnp.sin(angles)
    sine = jnp.tile(jnp.concatenate([-sine, sine], axis=1), (1, 2))
    start = start_all.reshape(parts, 1, tokens)

    x_low = inputs.reshape(tokens, width)
    q, k, v, hidden_in = project(
        x_low, gain_one[None], query_full, key_full, value_full,
        first_values.reshape(tokens, width), cosine, sine, parts,
    )
    (q_all, k_all, v_all, o_all, lse_all, attended), (down_full, *weights) = attend(
        q, k, v, start, late, ready
    )
    out_full, gate_full, up_full = (tall(value) for value in weights)
    down_full = unstacked(down_full, down_padded)
    attended = attended.transpose(1, 0, 2).reshape(tokens, width)

    x_in = x_low.astype(F32)
    middle = x_in + dot(attended, out_full)
    scale = lax.rsqrt(jnp.mean(middle * middle, axis=-1, keepdims=True) + EPS)
    hidden_mlp = (middle * scale * gain_two).astype(BF16)
    gate = dot(hidden_mlp, gate_full)
    upward = dot(hidden_mlp, up_full)
    sigma = jax.nn.sigmoid(gate)
    silu_gate = gate * sigma
    inner = (silu_gate * upward).astype(BF16)
    output = (middle + dot(inner, down_full)).astype(BF16).reshape(inputs.shape)
    grad_y = cotangent.reshape(tokens, width)
    grad_down = across(inner, grad_y)
    grad_inner = against(grad_y, down_full)
    grad_gate_low = (grad_inner * upward * sigma * (1.0 + gate * (1.0 - sigma))).astype(BF16)
    grad_up_low = (grad_inner * silu_gate).astype(BF16)
    grad_gate = across(hidden_mlp, grad_gate_low)
    grad_up = across(hidden_mlp, grad_up_low)
    grad_hidden_mlp = against(grad_gate_low, gate_full) + against(grad_up_low, up_full)
    grad_middle, grad_gain_two = norm_back(grad_hidden_mlp, middle, gain_two)
    grad_middle = grad_middle + grad_y.astype(F32)
    grad_branch = grad_middle.astype(BF16)
    grad_out = across(attended, grad_branch)
    d_att = against(grad_branch, out_full).astype(BF16)
    d_att = d_att.reshape(tokens, parts, width // parts).transpose(1, 0, 2)

    share = lambda grad: stacked(grad.astype(BF16), devices)
    (dq, dk, dv), (total_gate, total_up, part_down, part_out) = attend_back(
        d_att, q_all, k_all, v_all, o_all, lse_all, start,
        [share(grad_gate), share(grad_up), share(grad_down), share(grad_out)],
    )
    dq, dk, dv, grad_first = unproject(dq, dk, dv, cosine, sine)
    grad_query_w = across(hidden_in, dq)
    grad_key_w = across(hidden_in, dk)
    grad_value_w = across(hidden_in, dv)
    grad_hidden_in = against(dq, query_full) + against(dk, key_full) + against(dv, value_full)
    grad_x, grad_gain_one = norm_back(grad_hidden_in, x_in, gain_one)
    grad_x = grad_x + grad_middle
    gains_grad = jnp.stack([grad_gain_one, grad_gain_two]).reshape(2, devices, rows)
    gains_grad = jnp.pad(gains_grad.transpose(1, 0, 2), ((0, 0), (0, 6), (0, 128 - rows)))
    total_query, total_key, total_value, gains_total, total_down, total_out = sums(
        [share(grad_query_w), share(grad_key_w), share(grad_value_w), gains_grad],
        [part_down, part_out],
        4,
    )
    low = lambda total: unstacked(total[None], rows)

    def close(total):
        total = low(total).reshape(rows, devices, down_padded)
        return total[:, :, :down_rows].reshape(rows, devices * down_rows)

    return (
        output,
        grad_x.reshape(inputs.shape),
        grad_first.reshape(inputs.shape),
        low(total_query),
        low(total_key),
        low(total_value),
        low(total_out),
        gains_total[0, :rows],
        close(total_gate),
        close(total_up),
        unstacked(total_down[None], down_padded)[:down_rows],
        gains_total[1, :rows],
    )


def solution(mesh):
    tokens = P("dp", "seq", None)
    matrix = P(("dp", "seq"), None)
    vector = P(("dp", "seq"))
    return jax.shard_map(
        shards,
        mesh=mesh,
        in_specs=(
            tokens, tokens, P("dp", None), matrix, matrix, matrix, matrix, vector,
            matrix, matrix, matrix, vector, tokens,
        ),
        out_specs=(
            tokens, tokens, tokens, matrix, matrix, matrix, matrix, vector,
            matrix, matrix, matrix, vector,
        ),
        check_vma=False,
    )
```

```python
import functools

import jax
import jax.numpy as jnp
from jax import lax
from jax.experimental import pallas as pl
from jax.experimental.pallas import tpu as pltpu
from jax.sharding import PartitionSpec as P

HEAD_DIM = 64
EPS = 1e-06
THETA = 10000.0
NEG = -1e30
MESH = pl.DeviceIdType.MESH
BF16 = jnp.bfloat16
F32 = jnp.float32
VMEM = pltpu.VMEM
MIB = 1 << 20


def dot(left, right, left_dim=1, right_dim=0):
    return lax.dot_general(
        left, right, (((left_dim,), (right_dim,)), ((), ())), preferred_element_type=F32
    )


def across(left, right):
    return dot(left, right, 0, 0)


def against(left, right):
    return dot(left, right, 1, 1)


def norm_back(grad_normed, values, gain):
    scale_inv = lax.rsqrt(jnp.mean(values * values, axis=-1, keepdims=True) + EPS)
    normed = values * scale_inv
    grad_scaled = grad_normed * gain
    grad_values = scale_inv * (
        grad_scaled - normed * jnp.mean(grad_scaled * normed, axis=-1, keepdims=True)
    )
    grad_gain = jnp.sum(grad_normed * normed, axis=0)
    return (grad_values, grad_gain)


def turned(values, cosine, sine):
    lane = lax.broadcasted_iota(jnp.int32, values.shape, 1) % HEAD_DIM
    other = jnp.where(
        lane < HEAD_DIM // 2,
        pltpu.roll(values, 128 - HEAD_DIM // 2, 1),
        pltpu.roll(values, HEAD_DIM // 2, 1),
    )
    return values * cosine + other * sine


def project_kernel(width, x, gain, wq, wk, wv, first, cosine, sine, q_out, k_out, v_out, h_out):
    @pl.when(pl.program_id(0) == 0)
    def _():
        values = x[...].astype(F32)
        scale = lax.rsqrt(jnp.mean(values * values, axis=-1, keepdims=True) + EPS)
        h_out[...] = (values * scale * gain[...]).astype(BF16)

    hidden = h_out[...]
    cos, sin = cosine[...], sine[...]
    for weight, out, scale in ((wq, q_out, HEAD_DIM**-0.5), (wk, k_out, 1.0)):
        raw = dot(hidden, weight[...])
        for part in range(2):
            done = turned(raw[:, part * 128 : part * 128 + 128], cos, sin) * scale
            for piece in range(128 // width):
                out[part * (128 // width) + piece] = done[
                    :, piece * width : (piece + 1) * width
                ].astype(BF16)
    mixed = (0.5 * dot(hidden, wv[...]) + 0.5 * first[...].astype(F32)).astype(BF16)
    for piece in range(256 // width):
        v_out[piece] = mixed[:, piece * width : (piece + 1) * width]


def project(x, gain, wq, wk, wv, first, cosine, sine, parts):
    tokens, dim = x.shape
    width = dim // parts
    whole = lambda shape: pl.BlockSpec(shape, lambda g: (0,) * len(shape))
    cols = lambda rows: pl.BlockSpec((rows, 256), lambda g: (0, g))
    out = pl.BlockSpec((256 // width, tokens, width), lambda g: (g, 0, 0))
    split = jax.ShapeDtypeStruct((parts, tokens, width), BF16)
    return pl.pallas_call(
        functools.partial(project_kernel, width),
        grid=(dim // 256,),
        in_specs=[
            whole((tokens, dim)),
            whole((1, dim)),
            cols(dim),
            cols(dim),
            cols(dim),
            cols(tokens),
            whole((tokens, 128)),
            whole((tokens, 128)),
        ],
        out_specs=[out, out, out, whole((tokens, dim))],
        out_shape=[split, split, split, jax.ShapeDtypeStruct((tokens, dim), BF16)],
        compiler_params=pltpu.CompilerParams(vmem_limit_bytes=40 * MIB),
        cost_estimate=pl.CostEstimate(
            flops=6 * tokens * dim * dim, bytes_accessed=16 * tokens * dim, transcendentals=0
        ),
        name="project",
    )(x, gain, wq, wk, wv, first, cosine, sine)


def unproject_kernel(width, dq, dk, dv, cosine, sine, q_out, k_out, v_out, first_out):
    cos, sin = cosine[...], sine[...]
    for part in range(2):
        lanes = slice(part * 128, part * 128 + 128)
        picks = range(part * (128 // width), (part + 1) * (128 // width))
        join = lambda ref: jnp.concatenate([ref[p] for p in picks], axis=1).astype(F32)
        q_out[:, lanes] = turned(join(dq), cos, -sin).astype(BF16)
        k_out[:, lanes] = turned(join(dk), cos, -sin).astype(BF16)
        value = 0.5 * join(dv)
        first_out[:, lanes] = value
        v_out[:, lanes] = value.astype(BF16)


def unproject(dq, dk, dv, cosine, sine):
    parts, tokens, width = dq.shape
    dim = parts * width
    split = pl.BlockSpec((256 // width, tokens, width), lambda g: (g, 0, 0))
    table = pl.BlockSpec((tokens, 128), lambda g: (0, 0))
    cols = pl.BlockSpec((tokens, 256), lambda g: (0, g))
    low = jax.ShapeDtypeStruct((tokens, dim), BF16)
    return pl.pallas_call(
        functools.partial(unproject_kernel, width),
        grid=(dim // 256,),
        in_specs=[split, split, split, table, table],
        out_specs=[cols, cols, cols, cols],
        out_shape=[low, low, low, jax.ShapeDtypeStruct((tokens, dim), F32)],
        compiler_params=pltpu.CompilerParams(vmem_limit_bytes=40 * MIB),
        name="unproject",
    )(dq, dk, dv, cosine, sine)


def greet(parts, me):
    barrier = pltpu.get_barrier_semaphore()
    for step in range(1, parts):
        pl.semaphore_signal(
            barrier, 1, device_id={"seq": lax.rem(me + step, parts)}, device_id_type=MESH
        )
    return parts - 1


def send(source, target, send_sem, recv_sem, peer):
    return pltpu.make_async_remote_copy(
        src_ref=source,
        dst_ref=target,
        send_sem=send_sem,
        recv_sem=recv_sem,
        device_id={"seq": peer},
        device_id_type=MESH,
    )


def arrive(ref, sem):
    pltpu.make_async_copy(ref, ref, sem).wait()


def own_head(values, head, width):
    if width == HEAD_DIM:
        return values
    lane = lax.broadcasted_iota(jnp.int32, values.shape, 1)
    return jnp.where(lane // HEAD_DIM == head, values, jnp.zeros_like(values))


def allowed_tile(i, j, tokens, start):
    key = j * tokens + lax.broadcasted_iota(jnp.int32, (tokens, tokens), 0)
    query = i * tokens + lax.broadcasted_iota(jnp.int32, (tokens, tokens), 1)
    return (key <= query) & (key >= start[i])


def forward_kernel(
    parts, heads, pieces, count,
    q_in, k_in, v_in, start, *refs,
):
    helds, refs = refs[: len(pieces)], refs[len(pieces) :]
    q_all, k_all, v_all, o_all, lse_all, attended = refs[:6]
    fulls, refs = refs[6 : 6 + count], refs[6 + count :]
    v_turn, total, o_send, in_send, in_recv, o_out, o_in, *sems = refs
    place = Place()
    _, tokens, width = q_in.shape
    half = parts // 2
    me = lax.axis_index("seq")
    own = me // half
    place.greet(greet(parts, me))
    spread = WeightSpread(place, pieces, helds, fulls, sems)
    pairs = ((q_in, q_all), (k_in, k_all), (v_in, v_all))

    def moved(index, peer):
        source, target = pairs[index]
        return send(
            source.at[peer], target.at[me], in_send.at[index, peer], in_recv.at[index, me], peer
        )

    def over(first, action):
        def body(step, _):
            action(first + lax.rem(me + step, half))
            return 0

        lax.fori_loop(0, half, body, 0)

    def start_cross(indices):
        over((1 - own) * half, lambda peer: [moved(index, peer).start() for index in indices])

    def sent_cross(indices):
        over((1 - own) * half, lambda peer: [moved(index, peer).wait_send() for index in indices])

    for index, (source, target) in enumerate(pairs):
        pltpu.make_async_copy(source.at[me], target.at[me], in_recv.at[index, me]).start()
    pl.when(own == 0)(lambda: start_cross((1, 2)))
    pl.when(own == 1)(lambda: start_cross((0,)))

    def start_near(peer):
        @pl.when(peer != me)
        def _():
            for index in range(3):
                moved(index, peer).start()

    over(own * half, start_near)

    def got(index, block):
        arrive(pairs[index][1].at[block], in_recv.at[index, block])

    def got_keys(block):
        got(1, block)
        got(2, block)
        v_turn[block] = v_all[block].T

    def tile(i, j, masked):
        if masked:
            allowed = allowed_tile(i, j, tokens, start)
        queries, keys = q_all[i], k_all[j]
        for head in range(heads):
            rows = slice(head * HEAD_DIM, (head + 1) * HEAD_DIM)
            scores = against(keys, own_head(queries, head, width))
            if masked:
                scores = jnp.where(allowed, scores, NEG)
            old = lse_all[i, head]
            new = jnp.maximum(old, jnp.max(scores, axis=0, keepdims=True))
            weights = jnp.exp(scores - new)
            factor = jnp.exp(old - new)
            lse_all[i, head] = new
            total[i, head] = total[i, head] * factor + jnp.sum(weights, axis=0, keepdims=True)
            o_all[i, rows] = o_all[i, rows] * factor + dot(
                v_turn[j, rows], weights.astype(BF16)
            )

    def tile_row(row, _):
        phase, place_in = row // half, lax.rem(row, half)
        lower = jnp.where(phase == 0, own, 1 - own) * half
        i = jnp.where(phase == 1, half, lower) + place_in
        first = jnp.where(phase == 1, 0, lower)
        last = jnp.where(phase == 1, half, i + 1)
        spread.at_row(row, 3 * half)

        @pl.when(phase == 0)
        def _():
            got(0, i)
            got_keys(i)

        @pl.when((row == half) & (own == 0))
        def _():
            lax.fori_loop(half, parts, lambda block, _: got(0, block) or 0, 0)

        @pl.when((row == half) & (own == 1))
        def _():
            sent_cross((0,))
            start_cross((1, 2))
            lax.fori_loop(0, half, lambda block, _: got_keys(block) or 0, 0)

        @pl.when((row == 2 * half) & (own == 0))
        def _():
            sent_cross((1, 2))
            start_cross((0,))

        @pl.when((phase == 2) & (own == 0))
        def _():
            got_keys(i)

        @pl.when((phase == 2) & (own == 1))
        def _():
            got(0, i)

        @pl.when((phase == 0) | ((phase == 1) & (own == 0)) | ((phase == 2) & (own == 1)))
        def _():
            lse_all[i] = jnp.full(lse_all.shape[1:], NEG, F32)
            total[i] = jnp.zeros(total.shape[1:], F32)
            o_all[i] = jnp.zeros(o_all.shape[1:], F32)

        def key_block(j, _):
            masked = (j == 0) | (j == i) | (i == parts - 1)
            pl.when(masked)(lambda: tile(i, j, True))
            pl.when(jnp.logical_not(masked))(lambda: tile(i, j, False))
            return 0

        lax.fori_loop(first, last, key_block, 0)

        @pl.when(((phase == 0) & (own == 0)) | ((phase == 1) & (own == 1)) | (phase == 2))
        def _():
            for head in range(heads):
                rows = slice(head * HEAD_DIM, (head + 1) * HEAD_DIM)
                o_all[i, rows] = o_all[i, rows] / total[i, head]
                lse_all[i, head] = lse_all[i, head] + jnp.log(total[i, head])
            o_send[i] = o_all[i].T.astype(BF16)

            @pl.when(i == me)
            def _():
                pltpu.make_async_copy(o_send.at[i], attended.at[me], o_in.at[me]).start()

            @pl.when(i != me)
            def _():
                send(o_send.at[i], attended.at[me], o_out.at[i], o_in.at[me], i).start()

        return 0

    lax.fori_loop(0, 3 * half, tile_row, 0)
    spread.finish()
    pl.when(own == 0)(lambda: sent_cross((0,)))
    pl.when(own == 1)(lambda: sent_cross((1, 2)))

    def sent_near(peer):
        @pl.when(peer != me)
        def _():
            for index in range(3):
                moved(index, peer).wait_send()

    over(own * half, sent_near)

    def finish(step, _):
        peer = lax.rem(me + step, parts)
        arrive(o_send.at[peer], o_out.at[peer])
        arrive(attended.at[peer], o_in.at[peer])
        return 0

    lax.fori_loop(1, parts, finish, 0)
    arrive(attended.at[me], o_in.at[me])


def attend(q, k, v, start, helds, pieces, shapes):
    parts, tokens, width = q.shape
    heads = width // HEAD_DIM
    place = Place()
    whole = pl.BlockSpec(memory_space=VMEM)
    far = pl.BlockSpec(memory_space=pl.ANY)
    split = jax.ShapeDtypeStruct(q.shape, BF16)
    flops = 4 * parts * parts * tokens * tokens * width // 2
    fulls = [
        jax.ShapeDtypeStruct((place.xs, 2, place.as_, place.bs, *shape), BF16) for shape in shapes
    ]
    results = pl.pallas_call(
        functools.partial(forward_kernel, parts, heads, pieces, len(shapes)),
        in_specs=[whole] * 4 + [far] * len(pieces),
        out_specs=[whole] * 6 + [far] * len(shapes),
        out_shape=[
            split,
            split,
            split,
            jax.ShapeDtypeStruct((parts, width, tokens), F32),
            jax.ShapeDtypeStruct((parts, heads, 1, tokens), F32),
            split,
            *fulls,
        ],
        scratch_shapes=[
            VMEM((parts, width, tokens), BF16),
            VMEM((parts, heads, 1, tokens), F32),
            VMEM((parts, tokens, width), BF16),
            pltpu.SemaphoreType.DMA((3, parts)),
            pltpu.SemaphoreType.DMA((3, parts)),
            pltpu.SemaphoreType.DMA((parts,)),
            pltpu.SemaphoreType.DMA((parts,)),
            *[spread_semaphores(place)] * len(pieces),
        ],
        compiler_params=pltpu.CompilerParams(
            collective_id=1, has_side_effects=True, vmem_limit_bytes=48 * MIB
        ),
        cost_estimate=pl.CostEstimate(
            flops=4 * flops, bytes_accessed=16 * q.size, transcendentals=flops // 256
        ),
        name="attend",
    )(q, k, v, start, *helds)
    devices = place.xs * 2 * place.as_ * place.bs
    weights = [value.reshape(devices, *value.shape[4:]) for value in results[6:]]
    return results[:6], weights


def backward_kernel(
    parts, heads, pieces, count,
    d_in, q_all, k_all, v_all, o_all, lse_all, start, *refs,
):
    grads, refs = refs[:count], refs[count:]
    (dq_got, dk_got, dv_got), refs = refs[:3], refs[3:]
    results, refs = refs[: len(pieces)], refs[len(pieces) :]
    d_all, k_turn, delta, dq_turn, dk_sum, dv_sum, dq_send, dk_send, dv_send = refs[:9]
    in_send, in_recv, out_send, out_recv, *buffers = refs[9:]
    place = Place()
    _, tokens, width = d_in.shape
    half = parts // 2
    me = lax.axis_index("seq")
    own = me // half
    place.greet(greet(parts, me))
    adding = GradSums(place, pieces, grads, results, buffers)

    def over(first, action):
        def body(step, _):
            action(first + lax.rem(me + step, half))
            return 0

        lax.fori_loop(0, half, body, 0)

    def moved(peer):
        return send(d_in.at[peer], d_all.at[me], in_send.at[peer], in_recv.at[me], peer)

    over((1 - own) * half, lambda peer: moved(peer).start())
    pltpu.make_async_copy(d_in.at[me], d_all.at[me], in_recv.at[me]).start()

    def start_near(peer):
        pl.when(peer != me)(lambda: moved(peer).start())

    over(own * half, start_near)
    sends = ((dq_send, dq_got), (dk_send, dk_got), (dv_send, dv_got))

    def give(index, block):
        source, target = sends[index]

        @pl.when(block == me)
        def _():
            pltpu.make_async_copy(
                source.at[block], target.at[me], out_recv.at[index, me]
            ).start()

        @pl.when(block != me)
        def _():
            send(
                source.at[block], target.at[me],
                out_send.at[index, block], out_recv.at[index, me], block,
            ).start()

    def give_query(i):
        dq_send[i] = (dq_turn[i] * HEAD_DIM**-0.5).T.astype(BF16)
        give(0, i)

    def give_keys(j):
        dk_send[j] = dk_sum[j].astype(BF16)
        dv_send[j] = dv_sum[j].astype(BF16)
        give(1, j)
        give(2, j)

    def tile(i, j, masked):
        if masked:
            allowed = allowed_tile(i, j, tokens, start)
        queries, grads_out, keys, mixed = q_all[i], d_all[i], k_all[j], v_all[j]
        for head in range(heads):
            rows = slice(head * HEAD_DIM, (head + 1) * HEAD_DIM)
            query, grad = own_head(queries, head, width), own_head(grads_out, head, width)
            scores = against(keys, query)
            if masked:
                scores = jnp.where(allowed, scores, NEG)
            weights = jnp.exp(scores - lse_all[i, head])
            dv_sum[j] += dot(weights.astype(BF16), grad)
            slope = against(mixed, grad) - delta[i, head]
            d_scores = (weights * slope).astype(BF16)
            dk_sum[j] += dot(d_scores, query)
            dq_turn[i, rows] += dot(k_turn[j, rows], d_scores)

    def prepare(block):
        arrive(d_all.at[block], in_recv.at[block])
        product = d_all[block].astype(F32).T * o_all[block]
        for head in range(heads):
            rows = slice(head * HEAD_DIM, (head + 1) * HEAD_DIM)
            delta[block, head] = jnp.sum(product[rows], axis=0, keepdims=True)
        k_turn[block] = k_all[block].T
        dq_turn[block] = jnp.zeros(dq_turn.shape[1:], F32)
        dk_sum[block] = jnp.zeros(dk_sum.shape[1:], F32)
        dv_sum[block] = jnp.zeros(dv_sum.shape[1:], F32)

    def tile_row(row, _):
        phase, place_in = row // half, lax.rem(row, half)
        adding.at_row(row, 3 * half)

        @pl.when(row == 0)
        def _():
            lax.fori_loop(0, half, lambda n, _: prepare(own * half + n) or 0, 0)

        @pl.when(row == half)
        def _():
            lax.fori_loop(0, half, lambda n, _: prepare((1 - own) * half + n) or 0, 0)

        by_query = jnp.where(phase == 1, own == 1, own == 0)
        lower = jnp.where(phase == 0, own, 1 - own) * half
        outer = jnp.where(
            phase == 2, jnp.where(by_query, half, 0), lower
        ) + place_in
        first = jnp.where(phase == 2, jnp.where(by_query, 0, half), jnp.where(by_query, lower, outer))
        last = jnp.where(
            phase == 2,
            jnp.where(by_query, half, parts),
            jnp.where(by_query, outer + 1, lower + half),
        )

        def inner_block(inner, _):
            i, j = jnp.where(by_query, outer, inner), jnp.where(by_query, inner, outer)
            masked = (j == 0) | (j == i) | (i == parts - 1)
            pl.when(masked)(lambda: tile(i, j, True))
            pl.when(jnp.logical_not(masked))(lambda: tile(i, j, False))
            return 0

        lax.fori_loop(first, last, inner_block, 0)
        pl.when(by_query)(lambda: give_query(outer))
        pl.when(jnp.logical_not(by_query))(lambda: give_keys(outer))
        return 0

    lax.fori_loop(0, 3 * half, tile_row, 0)
    pl.when(own == 0)(lambda: over(0, give_keys))
    pl.when(own == 1)(lambda: over(half, give_query))
    adding.finish()

    def finish(step, _):
        peer = lax.rem(me + step, parts)
        moved(peer).wait_send()
        for index, (source, target) in enumerate(sends):
            arrive(source.at[peer], out_send.at[index, peer])
            arrive(target.at[peer], out_recv.at[index, peer])
        return 0

    lax.fori_loop(1, parts, finish, 0)
    for index, (_, target) in enumerate(sends):
        arrive(target.at[me], out_recv.at[index, me])


def attend_back(d_att, q, k, v, o, lse, start, grads, pieces):
    parts, tokens, width = q.shape
    heads = width // HEAD_DIM
    place = Place()
    whole = pl.BlockSpec(memory_space=VMEM)
    far = pl.BlockSpec(memory_space=pl.ANY)
    split = jax.ShapeDtypeStruct(q.shape, BF16)
    flops = 10 * parts * parts * tokens * tokens * width // 2
    sum_shapes = [piece.held(place, grads[piece.array].shape[1]) for piece in pieces]
    sum_scratch = GradSums.scratch(place, pieces, grads)
    grads = [placed(place, grad) for grad in grads]
    results = pl.pallas_call(
        functools.partial(backward_kernel, parts, heads, pieces, len(grads)),
        in_specs=[far] + [whole] * 6 + [far] * len(grads),
        out_specs=[far] * 3 + [far] * len(pieces),
        out_shape=[split] * 3 + sum_shapes,
        scratch_shapes=[
            VMEM((parts, tokens, width), BF16),
            VMEM((parts, width, tokens), BF16),
            VMEM((parts, heads, 1, tokens), F32),
            VMEM((parts, width, tokens), F32),
            VMEM((parts, tokens, width), F32),
            VMEM((parts, tokens, width), F32),
            VMEM((parts, tokens, width), BF16),
            VMEM((parts, tokens, width), BF16),
            VMEM((parts, tokens, width), BF16),
            pltpu.SemaphoreType.DMA((parts,)),
            pltpu.SemaphoreType.DMA((parts,)),
            pltpu.SemaphoreType.DMA((3, parts)),
            pltpu.SemaphoreType.DMA((3, parts)),
            *sum_scratch,
        ],
        compiler_params=pltpu.CompilerParams(
            collective_id=2, has_side_effects=True, vmem_limit_bytes=60 * MIB
        ),
        cost_estimate=pl.CostEstimate(
            flops=4 * flops, bytes_accessed=20 * q.size, transcendentals=flops // 640
        ),
        name="attend_back",
    )(d_att, q, k, v, o, lse, start, *grads)
    return results[:3], results[3:]


class Place:
    def __init__(self):
        self.xs = lax.axis_size("dp") // 2
        seq = lax.axis_size("seq")
        self.bs = 2 if seq <= 8 else 4
        self.as_ = seq // self.bs
        dp, rank = lax.axis_index("dp"), lax.axis_index("seq")
        self.x, self.core = dp // 2, lax.rem(dp, 2)
        self.a, self.b = rank // self.bs, lax.rem(rank, self.bs)

    def device(self, x=None, core=None, a=None, b=None):
        x, core = (self.x if x is None else x), (self.core if core is None else core)
        a, b = (self.a if a is None else a), (self.b if b is None else b)
        return (x * 2 + core, a * self.bs + b)

    def peers(self, axis):
        size = {"x": self.xs, "a": self.as_, "b": self.bs}[axis]
        own = getattr(self, axis)
        return [(step - 1, lax.rem(own + step, size)) for step in range(1, size)]

    def greet(self, greeted=0):
        barrier = pltpu.get_barrier_semaphore()
        others = [self.device(core=1 - self.core)]
        for axis in "x" if greeted else "xab":
            others += [self.device(**{axis: index}) for _, index in self.peers(axis)]
        for other in others:
            pl.semaphore_signal(barrier, 1, device_id=other, device_id_type=MESH)
        pl.semaphore_wait(barrier, len(others) + greeted)

    @property
    def inner(self):
        return (self.a == 1) | (self.a == 2)

    @property
    def beside(self):
        return self.a + 1 - 2 * lax.rem(self.a, 2)


def column_pieces(columns, wanted):
    tiles = columns // 128
    wanted = min(wanted, tiles)
    edges = [tiles * n // wanted * 128 for n in range(wanted)] + [columns]
    return [(edges[n], edges[n + 1] - edges[n]) for n in range(wanted)]


def placed(place, value):
    return value.reshape(place.xs, 2, place.as_, place.bs, *value.shape[1:])


def remote(source, target, send_sem, recv_sem, device):
    return pltpu.make_async_remote_copy(
        src_ref=source,
        dst_ref=target,
        send_sem=send_sem,
        recv_sem=recv_sem,
        device_id=device,
        device_id_type=MESH,
    )


def flat(ref):
    rows, columns = ref.shape[-2:]
    return ref.reshape(ref.size // (rows * columns), rows, columns)


class Relay:
    def __init__(self, place, source, target, sems):
        self.p, self.source, self.target, self.sems = place, source, target, sems
        assert place.as_ == 4

    def near(self):
        p = self.p
        return remote(
            self.source, self.target.at[p.a],
            self.sems.at[0, 0], self.sems.at[1, 0], p.device(a=p.beside),
        )

    def middle(self):
        p = self.p
        held = self.target.at[pl.ds(p.a // 2 * 2, 2)]
        return remote(
            held, held, self.sems.at[0, 1], self.sems.at[1, 1], p.device(a=3 - p.a)
        )

    def outward(self):
        p = self.p
        held = self.target.at[pl.ds((1 - p.a // 2) * 2, 2)]
        return remote(
            held, held, self.sems.at[0, 2], self.sems.at[1, 1], p.device(a=p.beside)
        )

    def local(self):
        return pltpu.make_async_copy(self.source, self.target.at[self.p.a], self.sems.at[1, 2])

    def step(self, number):
        if number == 0:
            self.local().start()
            self.near().start()
        elif number == 1:
            self.local().wait()
            self.near().wait_recv()
            pl.when(self.p.inner)(lambda: self.middle().start())
        elif number == 2:

            @pl.when(self.p.inner)
            def _():
                self.middle().wait_recv()
                self.outward().start()
        else:

            @pl.when(jnp.logical_not(self.p.inner))
            def _():
                self.middle().wait_recv()

            @pl.when(self.p.inner)
            def _():
                self.middle().wait_send()
                self.outward().wait_send()

            self.near().wait_send()


class Piece:
    def __init__(self, array, start, size, order, deep):
        self.array, self.start, self.size, self.order, self.deep = array, start, size, order, deep

    @staticmethod
    def all(shapes):
        pieces = []
        for array, kinds in enumerate(
            ([("bx", 0)], [("bx", 1)] * 2, [("xb", 1), ("bx", 1)], [("bx", 0)] * 2)
        ):
            for (start, size), kind in zip(column_pieces(shapes[array][1], len(kinds)), kinds):
                pieces.append(Piece(array, start, size, *kind))
        return pieces

    def held(self, place, rows):
        lead = {"": (), "b": (place.bs,), "x": (place.xs,)}[self.order[0] if self.deep else ""]
        lead = (*lead, place.as_) if self.order[0] == "x" else (place.as_, *lead)
        return jax.ShapeDtypeStruct((*lead, rows, self.size), BF16)

    def along_a(self, place, held):
        if not self.deep:
            return held
        return held.at[place.x] if self.order[0] == "x" else held.at[:, place.b]

    def columns(self, ref):
        return ref.at[(slice(None),) * (len(ref.shape) - 1) + (pl.ds(self.start, self.size),)]


class Spread:
    def __init__(self, place, views, order, sems, source=None, first=0):
        self.place, self.views, self.order, self.sems = place, views, order, sems
        self.source, self.first = source, first

    @staticmethod
    def views_of(place, full, order):
        p = place
        middle = full.at[:, p.core, :, p.b] if order == "xb" else full.at[p.x, p.core]
        return full.at[p.x, p.core, :, p.b], middle, full.at[:, p.core]

    def copies(self, number):
        p, view = self.place, self.views[number]
        source = self.source if self.source is not None and number == self.first else view
        base = sum([len(p.peers(axis)) for axis in self.order][:number])
        if number == 2:
            devices = [(0, p.device(core=1 - p.core))]
        else:
            axis = self.order[number]
            devices = [(s, p.device(**{axis: index})) for s, index in p.peers(axis)]
        return [
            remote(source, view, self.sems.at[0, base + s], self.sems.at[1, base + s], device)
            for s, device in devices
        ]

    def local(self):
        return pltpu.make_async_copy(self.source, self.views[self.first], self.sems.at[2, 0])

    def start(self, number):
        if self.source is not None and number == self.first:
            self.local().start()
        for copy in self.copies(number):
            copy.start()

    def finish(self, number):
        if self.source is not None and number == self.first:
            self.local().wait()
        for copy in self.copies(number):
            copy.wait_recv()
            copy.wait_send()

    def then(self, number):
        self.finish(number)
        if number < 2:
            self.start(number + 1)


def spread_semaphores(place):
    return pltpu.SemaphoreType.DMA((3, place.xs + place.bs - 1))


RELAY_SEMAPHORES = (2, 3)


class InRows:
    def at_row(self, row, count):
        for at in sorted({at for at, _ in self.actions() if at < 12}):

            @pl.when(row == at * count // 12)
            def _():
                for own_row, action in self.actions():
                    if own_row == at:
                        action()

    def finish(self):
        for at, action in self.actions():
            if at >= 12:
                action()


class WeightSpread(InRows):
    def __init__(self, place, pieces, sources, fulls, sems):
        self.units = []
        for piece, source, own_sems in zip(pieces, sources, sems):
            full = piece.columns(fulls[piece.array])
            views = Spread.views_of(place, full, piece.order)
            self.units.append(Spread(place, views, piece.order, own_sems, source, piece.deep))

    def actions(self):
        out, gate0, gate1, up0, up1, down0, down1 = self.units
        start = lambda unit: functools.partial(unit.start, unit.first)
        then = lambda unit, number: functools.partial(unit.then, number)
        done = [(0, start(unit)) for unit in (gate0, down0, gate1, down1, up1, out, up0)]
        done += [(4, then(down0, 0)), (5, then(down1, 0)), (6, then(out, 0))]
        done += [(7, then(gate0, 1)), (8, then(gate1, 1)), (9, then(up0, 1)), (10, then(up1, 1))]
        done += [(12, then(unit, 1)) for unit in (down0, down1, out)]
        done += [(12, then(unit, 2)) for unit in (gate0, gate1, up0, up1, down0, down1, out)]
        return done


def gather_kernel(plan, pieces, arrays, parted, *refs):
    place = Place()
    total = arrays + parted
    sources, refs = refs[:total], refs[total:]
    fulls, helds, (relay_sems, *sems) = (
        refs[:arrays], refs[arrays : arrays + len(pieces)], refs[arrays + len(pieces) :]
    )
    place.greet()
    whole, relays = [], []
    for number, (array, start, size, order) in enumerate(plan):
        views = Spread.views_of(place, fulls[array].at[:, :, :, :, :, pl.ds(start, size)], order)
        relays.append(
            Relay(place, sources[array].at[:, pl.ds(start, size)], views[0], relay_sems.at[number])
        )
        whole.append(Spread(place, views, order, sems[number]))
    deep, flat_relays, deep_relays = [], [], []
    for number, (piece, held) in enumerate(zip(pieces, helds)):
        view = piece.along_a(place, held)
        index = len(plan) + number
        source = piece.columns(sources[arrays + piece.array])
        relay = Relay(place, source, view, relay_sems.at[index])
        (deep_relays if piece.deep else flat_relays).append(relay)
        if piece.deep:
            deep.append(Spread(place, [view], piece.order, sems[index]))

    def step(group, number):
        for relay in group:
            relay.step(number)

    step(relays, 0)
    step(relays, 1)
    step(deep_relays, 0)
    step(relays, 2)
    for relay, unit in zip(relays, whole):
        relay.step(3)
        unit.start(0)
    step(deep_relays, 1)
    step(flat_relays, 0)
    for unit in whole:
        unit.then(0)
    step(deep_relays, 2)
    for relay, unit in zip(deep_relays, deep):
        relay.step(3)
        unit.start(0)
    step(flat_relays, 1)
    for unit in whole:
        unit.then(1)
    step(flat_relays, 2)
    for unit in whole:
        unit.then(2)
    step(flat_relays, 3)
    for unit in deep:
        unit.finish(0)


def gathered(arrays, parted, pieces, collective_id):
    place = Place()
    xs, as_, bs = place.xs, place.as_, place.bs
    plan = []
    for number, array in enumerate(arrays):
        for place_in, (start, size) in enumerate(column_pieces(array.shape[1], 2)):
            plan.append((number, start, size, "xb" if place_in == 0 else "bx"))
    full = [jax.ShapeDtypeStruct((xs, 2, as_, bs, *array.shape), array.dtype) for array in arrays]
    full += [piece.held(place, parted[piece.array].shape[0]) for piece in pieces]
    far = pl.BlockSpec(memory_space=pl.ANY)
    count = len(plan) + len(pieces)
    results = pl.pallas_call(
        functools.partial(gather_kernel, plan, pieces, len(arrays), len(parted)),
        in_specs=[far] * (len(arrays) + len(parted)),
        out_specs=[far] * len(full),
        out_shape=full,
        scratch_shapes=[
            pltpu.SemaphoreType.DMA((count, *RELAY_SEMAPHORES)),
            *[spread_semaphores(place)] * count,
        ],
        compiler_params=pltpu.CompilerParams(collective_id=collective_id, has_side_effects=True),
        cost_estimate=pl.CostEstimate(
            flops=0, bytes_accessed=sum(array.size for array in arrays) * 64, transcendentals=0
        ),
        name="gathered",
    )(*arrays, *parted)
    devices = xs * 2 * as_ * bs
    gives = [result.reshape(devices, *result.shape[4:]) for result in results[: len(arrays)]]
    return gives, results[len(arrays) :]


def add_up(mine, others):
    lead = mine.shape[:-2]

    def at(ref, step):
        index = []
        for size in reversed(lead):
            index.insert(0, lax.rem(step, size))
            step = step // size
        return ref.at[tuple(index)]

    def body(step, _):
        total = at(mine, step)[...].astype(F32)
        for other in others:
            total += at(other, step)[...].astype(F32)
        at(mine, step)[...] = total.astype(mine.dtype)
        return 0

    count = 1
    for size in lead:
        count *= size
    lax.fori_loop(0, count, body, 0)


class RelaySum:
    def __init__(self, place, own, inward, middle, last, sems, result):
        self.p, self.own, self.sems, self.result = place, own, sems, result
        self.inward, self.middle, self.last = inward, middle, last
        assert place.as_ == 4

    def move(self, number):
        p = self.p
        far = self.own.at[pl.ds((1 - p.a // 2) * 2, 2)]
        if number == 0:
            source, target, device = far, self.inward, p.beside
        elif number == 1:
            source, target, device = far, self.middle, 3 - p.a
        else:
            source, target, device = self.own.at[p.beside], self.last, p.beside
        return remote(
            source, target, self.sems.at[0, number], self.sems.at[1, number], p.device(a=device)
        )

    def step(self, number):
        p, inner = self.p, self.p.inner
        outer = jnp.logical_not(inner)
        if number == 0:
            pl.when(outer)(lambda: self.move(0).start())
            pl.when(outer)(lambda: self.move(2).start())
        elif number == 1:

            @pl.when(inner)
            def _():
                self.move(0).wait_recv()
                add_up(self.own.at[pl.ds((1 - p.a // 2) * 2, 2)], [self.inward])
                self.move(1).start()
        elif number == 2:

            @pl.when(inner)
            def _():
                self.move(1).wait_recv()
                add_up(self.own.at[pl.ds(p.a // 2 * 2, 2)], [self.middle])
                self.move(2).start()
        else:
            self.move(2).wait_recv()
            self.result[...] = self.own[p.a].astype(F32) + self.last[...].astype(F32)
            pl.when(outer)(lambda: self.move(0).wait_send())
            pl.when(inner)(lambda: self.move(1).wait_send())
            self.move(2).wait_send()

    @staticmethod
    def scratch(rows, columns, dtype):
        return [
            VMEM((2, rows, columns), dtype),
            VMEM((2, rows, columns), dtype),
            VMEM((rows, columns), dtype),
            pltpu.SemaphoreType.DMA((2, 3)),
        ]


class Sum:
    def __init__(self, place, source, order, buffers):
        self.place, self.order, self.source = place, order, source
        self.own, self.got0, self.got1, self.got2, self.sems = buffers

    @property
    def held(self):
        return self.own.at[self.place.x, :, self.place.b]

    @property
    def part(self):
        p = self.place
        return self.own.at[p.x] if self.order[0] == "x" else self.own.at[:, :, p.b]

    def moves(self, number):
        p = self.place
        if number == 0:
            return [(self.source.at[:, 1 - p.core], self.got0, 0, p.device(core=1 - p.core))]
        axis = self.order[number - 1]
        got = self.got1 if number == 1 else self.got2
        moves = []
        for slot, index in p.peers(axis):
            if axis == "x":
                piece = self.own.at[index] if number == 1 else self.own.at[index, :, p.b]
            else:
                piece = self.own.at[:, :, index] if number == 1 else self.own.at[p.x, :, index]
            moves.append((piece, got.at[slot], slot, p.device(**{axis: index})))
        return moves

    def copies(self, number):
        base = sum(([1] + [len(self.place.peers(axis)) for axis in self.order])[:number])
        return [
            remote(source, target, self.sems.at[0, base + s], self.sems.at[1, base + s], device)
            for source, target, s, device in self.moves(number)
        ]

    def local(self):
        return pltpu.make_async_copy(
            self.source.at[:, self.place.core], self.own, self.sems.at[2, 0]
        )

    def start(self, number):
        for copy in self.copies(number):
            copy.start()
        if number == 0:
            self.local().start()

    def finish(self, number):
        p = self.place
        if number == 0:
            self.local().wait()
        for copy in self.copies(number):
            copy.wait_recv()
            copy.wait_send()
        if number == 0:
            add_up(self.own, [self.got0])
        else:
            mine = self.held if number == 2 else self.part
            got = self.got1 if number == 1 else self.got2
            add_up(mine, [got.at[slot] for slot in range(len(p.peers(self.order[number - 1])))])

    @staticmethod
    def scratch(place, rows, size, order, dtype):
        xs, as_, bs = place.xs, place.as_, place.bs
        shapes = {
            "x": ((xs - 1, as_, bs, rows, size), (xs - 1, as_, rows, size)),
            "b": ((bs - 1, xs, as_, rows, size), (bs - 1, as_, rows, size)),
        }
        return [
            VMEM((xs, as_, bs, rows, size), dtype),
            VMEM((xs, as_, bs, rows, size), dtype),
            VMEM(shapes[order[0]][0], dtype),
            VMEM(shapes[order[1]][1], dtype),
            pltpu.SemaphoreType.DMA((3, xs + bs - 1)),
        ]


class GradSums(InRows):
    def __init__(self, place, pieces, grads, results, buffers):
        self.units, self.outs = [], []
        for piece, result in zip(pieces, results):
            source = piece.columns(grads[piece.array])
            unit, buffers = Sum(place, source, piece.order[::-1], buffers[:5]), buffers[5:]
            self.units.append(unit)
            self.outs.append((unit.part if piece.deep else unit.held, result))

    @staticmethod
    def scratch(place, pieces, grads):
        return [
            item
            for piece in pieces
            for item in Sum.scratch(
                place, grads[piece.array].shape[1], piece.size, piece.order[::-1], BF16
            )
        ]

    def actions(self):
        out, gate0, gate1, up0, up1, down0, down1 = self.units

        def copy_of(unit):
            source, result = self.outs[self.units.index(unit)]
            return pltpu.make_async_copy(source, result, unit.sems.at[2, 1])

        def then(unit, number):
            def action():
                unit.finish(number)
                if number < (1 if unit in (gate0, gate1, up0, up1) else 2):
                    unit.start(number + 1)
                else:
                    copy_of(unit).start()

            return action

        order = (down0, down1, out, up0, gate0, gate1, up1)
        done = [(0, functools.partial(unit.start, 0)) for unit in order]
        done += [(row, then(unit, 0)) for row, unit in zip((0, 1, 1, 2, 2, 3, 3), order)]
        done += [(6, then(down0, 1)), (7, then(down1, 1)), (8, then(out, 1)), (9, then(up0, 1))]
        done += [(10, then(gate0, 1)), (11, then(down0, 2))]
        done += [(12, then(down1, 2)), (12, then(out, 2)), (12, then(gate1, 1)), (12, then(up1, 1))]
        done += [(12, lambda unit=unit: copy_of(unit).wait()) for unit in order]
        return done


class HeldSum:
    def __init__(self, place, piece, source, buffers, result):
        self.place, self.piece, self.source = place, piece, source
        self.own, self.got, self.sems, *relay = buffers
        self.relay = RelaySum(place, self.own, *relay, result)
        self.axis = piece.order[0]

    def copies(self):
        if not self.piece.deep:
            return []
        p = self.place
        at = lambda index: self.source.at[index] if self.axis == "x" else self.source.at[:, index]
        return [
            remote(
                at(index), self.got.at[s], self.sems.at[0, s], self.sems.at[1, s],
                p.device(**{self.axis: index}),
            )
            for s, index in p.peers(self.axis)
        ]

    def local(self):
        mine = self.piece.along_a(self.place, self.source)
        return pltpu.make_async_copy(mine, self.own, self.sems.at[2, 0])

    def start(self):
        self.local().start()
        for copy in self.copies():
            copy.start()

    def finish(self):
        self.local().wait()
        copies = self.copies()
        for copy in copies:
            copy.wait_recv()
            copy.wait_send()
        if copies:
            add_up(self.own, [self.got.at[slot] for slot in range(len(copies))])
        self.relay.step(0)

    @staticmethod
    def scratch(place, piece, rows):
        count = len(place.peers(piece.order[0])) if piece.deep else 1
        got = (count, place.as_, rows, piece.size) if piece.deep else (1, 1, 16, 128)
        return [
            VMEM((place.as_, rows, piece.size), BF16),
            VMEM(got, BF16),
            pltpu.SemaphoreType.DMA((3, count)),
            *RelaySum.scratch(rows, piece.size, BF16),
        ]


def sums_kernel(plan, pieces, arrays, parted, *refs):
    place = Place()
    sources, helds, refs = refs[:arrays], refs[arrays : arrays + len(pieces)], refs[arrays + len(pieces) :]
    results, buffers = refs[: arrays + parted], refs[arrays + parted :]
    place.greet()
    units, relays, rest = [], [], []
    for array, start, size, order in plan:
        source = sources[array].at[:, :, :, :, :, pl.ds(start, size)]
        unit = Sum(place, source, order, buffers[:5])
        result = results[array].at[:, pl.ds(start, size)]
        relays.append(RelaySum(place, unit.held, *buffers[5:9], result))
        units.append(unit)
        buffers = buffers[9:]
    for piece, held in zip(pieces, helds):
        result = piece.columns(results[arrays + piece.array])
        rest.append(HeldSum(place, piece, held, buffers[:7], result))
        buffers = buffers[7:]
    deep = [unit for unit in rest if unit.piece.deep]
    simple = [unit for unit in rest if not unit.piece.deep]

    def step(group, number):
        for item in group:
            (item if isinstance(item, RelaySum) else item.relay).step(number)

    for unit in units + simple + deep:
        unit.start(*((0,) if isinstance(unit, Sum) else ()))
    for unit in simple:
        unit.finish()
    for unit in units:
        unit.finish(0)
        unit.start(1)
    step(simple, 1)
    for unit in deep:
        unit.finish()
    step(simple, 2)
    for unit in units:
        unit.finish(1)
        unit.start(2)
    step(deep, 1)
    step(simple, 3)
    for unit, relay in zip(units, relays):
        unit.finish(2)
        relay.step(0)
    step(deep, 2)
    step(relays, 1)
    step(deep, 3)
    step(relays, 2)
    step(relays, 3)


def sums(arrays, helds, pieces, shapes, collective_id):
    place = Place()
    plan, scratch = [], []
    for number, array in enumerate(arrays):
        rows, columns = array.shape[1:]
        for place_in, (start, size) in enumerate(column_pieces(columns, 2)):
            order = "xb" if place_in == 0 else "bx"
            plan.append((number, start, size, order))
            scratch += Sum.scratch(place, rows, size, order, array.dtype)
            scratch += RelaySum.scratch(rows, size, array.dtype)
    for piece in pieces:
        scratch += HeldSum.scratch(place, piece, shapes[piece.array][0])
    both = [placed(place, array) for array in arrays] + list(helds)
    far, whole = pl.BlockSpec(memory_space=pl.ANY), pl.BlockSpec(memory_space=VMEM)
    out = [jax.ShapeDtypeStruct(array.shape[1:], F32) for array in arrays]
    out += [jax.ShapeDtypeStruct(shape, F32) for shape in shapes]
    return pl.pallas_call(
        functools.partial(sums_kernel, plan, pieces, len(arrays), len(shapes)),
        in_specs=[far] * len(both),
        out_specs=[whole] * len(out),
        out_shape=out,
        scratch_shapes=scratch,
        compiler_params=pltpu.CompilerParams(
            collective_id=collective_id, has_side_effects=True, vmem_limit_bytes=48 * MIB
        ),
        cost_estimate=pl.CostEstimate(
            flops=0, bytes_accessed=sum(array.size for array in arrays) * 4, transcendentals=0
        ),
        name="sums",
    )(*both)


def stacked(value, devices):
    rows, columns = value.shape[0] // devices, value.shape[1]
    fold = 1
    while rows * fold % 16:
        fold *= 2
    value = value.reshape(devices, rows, fold, columns // fold)
    return value.transpose(0, 2, 1, 3).reshape(devices, rows * fold, columns // fold)


def unstacked(value, rows):
    devices, high, columns = value.shape
    value = value.reshape(devices, high // rows, rows, columns).transpose(0, 2, 1, 3)
    return value.reshape(devices * rows, high // rows * columns)


def middle_kernel(
    steps, x, att, dy, w_out, gain, w_gate, w_up, w_down,
    out, d_middle, d_att, g_out, g_gate, g_up, g_down, g_gain,
    attended, middle, hidden, hidden_turn, result, d_hidden,
):
    step = pl.program_id(0)
    parts, _, width = att.shape

    @pl.when(step == 0)
    def _():
        for part in range(parts):
            attended[:, part * width : (part + 1) * width] = att[part]
        total = x[...].astype(F32) + dot(attended[...], w_out[...])
        scale = lax.rsqrt(jnp.mean(total * total, axis=-1, keepdims=True) + EPS)
        normed = (total * scale * gain[...]).astype(BF16)
        middle[...] = total
        result[...] = total
        hidden[...] = normed
        hidden_turn[...] = normed.T
        d_hidden[...] = jnp.zeros_like(d_hidden)

    grad = dy[...]
    gate = dot(hidden[...], w_gate[...])
    up = dot(hidden[...], w_up[...])
    d_inner = against(grad, w_down[...])
    sigma = jax.nn.sigmoid(gate)
    silu = gate * sigma
    inner = (silu * up).astype(BF16)
    d_gate = (d_inner * up * sigma * (1.0 + gate * (1.0 - sigma))).astype(BF16)
    d_up = (d_inner * silu).astype(BF16)
    result[...] += dot(inner, w_down[...])
    g_down[...] = across(inner, grad).astype(BF16)
    g_gate[...] = dot(hidden_turn[...], d_gate).astype(BF16)
    g_up[...] = dot(hidden_turn[...], d_up).astype(BF16)
    d_hidden[...] += against(d_gate, w_gate[...]) + against(d_up, w_up[...])

    @pl.when(step == steps - 1)
    def _():
        out[...] = result[...].astype(BF16)
        grad_values, grad_gain = norm_back(d_hidden[...], middle[...], gain[...])
        total = grad_values + dy[...].astype(F32)
        d_middle[...] = total
        g_gain[...] = grad_gain[None]
        d_branch = total.astype(BF16)
        g_out[...] = across(attended[...], d_branch).astype(BF16)
        back = against(d_branch, w_out[...]).astype(BF16)
        for part in range(parts):
            d_att[part] = back[:, part * width : (part + 1) * width]


def between(x, att, dy, w_out, gain, w_gate, w_up, w_down):
    tokens, dim = x.shape
    units = w_gate.shape[1]
    chunk = 512 if units % 512 == 0 else 128
    whole = lambda value: pl.BlockSpec(value.shape, lambda g: (0,) * len(value.shape))
    wide = pl.BlockSpec((dim, chunk), lambda g: (0, g))
    tall = pl.BlockSpec((chunk, dim), lambda g: (g, 0))
    shape = jax.ShapeDtypeStruct
    outs = [
        shape((tokens, dim), BF16),
        shape((tokens, dim), F32),
        shape(att.shape, BF16),
        shape(w_out.shape, BF16),
        shape(w_gate.shape, BF16),
        shape(w_up.shape, BF16),
        shape(w_down.shape, BF16),
        shape((1, dim), F32),
    ]
    return pl.pallas_call(
        functools.partial(middle_kernel, units // chunk),
        grid=(units // chunk,),
        in_specs=[whole(v) for v in (x, att, dy, w_out, gain)] + [wide, wide, tall],
        out_specs=[whole(v) for v in outs[:4]] + [wide, wide, tall, whole(outs[7])],
        out_shape=outs,
        scratch_shapes=[
            VMEM((tokens, dim), BF16),
            VMEM((tokens, dim), F32),
            VMEM((tokens, dim), BF16),
            VMEM((dim, tokens), BF16),
            VMEM((tokens, dim), F32),
            VMEM((tokens, dim), F32),
        ],
        compiler_params=pltpu.CompilerParams(vmem_limit_bytes=56 * MIB),
        cost_estimate=pl.CostEstimate(
            flops=18 * tokens * dim * units, bytes_accessed=12 * dim * units, transcendentals=0
        ),
        name="between",
    )(x, att, dy, w_out, gain, w_gate, w_up, w_down)


def shards(
    inputs, first_values, lengths, w_query, w_key, w_value, w_out, gain_attn,
    w_gate, w_up, w_down, gain_mlp, cotangent,
):
    row_count, tokens, width = inputs.shape
    assert row_count == 1
    parts = lax.axis_size("seq")
    rank = lax.axis_index("seq")
    devices = lax.axis_size("dp") * parts
    rows, down_rows = w_query.shape[0], w_down.shape[0]
    multiple = 16 if down_rows >= 64 else 8
    down_padded = -(-down_rows // multiple) * multiple

    def spaced(value):
        value = value.reshape(rows, devices, down_rows)
        value = jnp.pad(value, ((0, 0), (0, 0), (0, down_padded - down_rows)))
        return value.reshape(rows, devices * down_padded)

    gains = jnp.pad(jnp.stack([gain_attn, gain_mlp]), ((0, 14), (0, 128 - rows)))
    wide = lambda value: stacked(value, 1)[0]
    padded_down = jnp.pad(w_down, ((0, down_padded - down_rows), (0, 0)))
    parted = [wide(w_out), wide(spaced(w_gate)), wide(spaced(w_up)), wide(padded_down)]
    shapes = [value.shape for value in parted]
    pieces = Piece.all(shapes)
    (query_full, key_full, value_full, gains), helds = gathered(
        [wide(w_query), wide(w_key), wide(w_value), gains], parted, pieces, 3
    )
    tall = lambda value: unstacked(value, rows)
    query_full, key_full, value_full = tall(query_full), tall(key_full), tall(value_full)
    gain_one, gain_two = (gains[:, n, :rows].reshape(width).astype(F32) for n in range(2))

    ends = jnp.cumsum(lengths[0])
    begins = ends - lengths[0]
    time = jnp.arange(tokens * parts, dtype=jnp.int32)
    inside = (time[:, None] >= begins[None, :]) & (time[:, None] < ends[None, :])
    start_all = jnp.sum(jnp.where(inside, begins[None, :], 0), axis=1)
    own_start = lax.dynamic_slice_in_dim(start_all, rank * tokens, tokens)
    position = (rank * tokens + jnp.arange(tokens, dtype=jnp.int32) - own_start).astype(F32)
    half = HEAD_DIM // 2
    angles = position[:, None] * THETA ** (-jnp.arange(half, dtype=F32) * 2.0 / HEAD_DIM)
    cosine = jnp.tile(jnp.cos(angles), (1, 4))
    sine = jnp.sin(angles)
    sine = jnp.tile(jnp.concatenate([-sine, sine], axis=1), (1, 2))
    start = start_all.reshape(parts, 1, tokens)

    x_low = inputs.reshape(tokens, width)
    q, k, v, hidden_in = project(
        x_low, gain_one[None], query_full, key_full, value_full,
        first_values.reshape(tokens, width), cosine, sine, parts,
    )
    (q_all, k_all, v_all, o_all, lse_all, attended), (*weights, down_full) = attend(
        q, k, v, start, helds, pieces, shapes
    )
    out_full, gate_full, up_full = (tall(value) for value in weights)
    down_full = unstacked(down_full, down_padded)
    output, grad_middle, d_att, grad_out, grad_gate, grad_up, grad_down, grad_gain_two = between(
        x_low, attended, cotangent.reshape(tokens, width), out_full, gain_two[None],
        gate_full, up_full, down_full,
    )
    grad_gain_two = grad_gain_two[0]
    x_in = x_low.astype(F32)

    share = lambda grad: stacked(grad.astype(BF16), devices)
    (dq, dk, dv), helds = attend_back(
        d_att, q_all, k_all, v_all, o_all, lse_all, start,
        [share(grad_out), share(grad_gate), share(grad_up), share(grad_down)], pieces,
    )
    dq, dk, dv, grad_first = unproject(dq, dk, dv, cosine, sine)
    grad_query_w = across(hidden_in, dq)
    grad_key_w = across(hidden_in, dk)
    grad_value_w = across(hidden_in, dv)
    grad_hidden_in = against(dq, query_full) + against(dk, key_full) + against(dv, value_full)
    grad_x, grad_gain_one = norm_back(grad_hidden_in, x_in, gain_one)
    grad_x = grad_x + grad_middle
    gains_grad = jnp.stack([grad_gain_one, grad_gain_two]).reshape(2, devices, rows)
    gains_grad = jnp.pad(gains_grad.transpose(1, 0, 2), ((0, 0), (0, 6), (0, 128 - rows)))
    (
        total_query, total_key, total_value, gains_total,
        total_out, total_gate, total_up, total_down,
    ) = sums(
        [share(grad_query_w), share(grad_key_w), share(grad_value_w), gains_grad],
        helds, pieces, shapes, 4,
    )
    low = lambda total: unstacked(total[None], rows)

    def close(total):
        total = low(total).reshape(rows, devices, down_padded)
        return total[:, :, :down_rows].reshape(rows, devices * down_rows)

    return (
        output.reshape(inputs.shape),
        grad_x.reshape(inputs.shape),
        grad_first.reshape(inputs.shape),
        low(total_query),
        low(total_key),
        low(total_value),
        low(total_out),
        gains_total[0, :rows],
        close(total_gate),
        close(total_up),
        unstacked(total_down[None], down_padded)[:down_rows],
        gains_total[1, :rows],
    )


def solution(mesh):
    tokens = P("dp", "seq", None)
    matrix = P(("dp", "seq"), None)
    vector = P(("dp", "seq"))
    return jax.shard_map(
        shards,
        mesh=mesh,
        in_specs=(
            tokens, tokens, P("dp", None), matrix, matrix, matrix, matrix, vector,
            matrix, matrix, matrix, vector, tokens,
        ),
        out_specs=(
            tokens, tokens, tokens, matrix, matrix, matrix, matrix, vector,
            matrix, matrix, matrix, vector,
        ),
        check_vma=False,
    )
```

```python
import functools

import jax
import jax.numpy as jnp
from jax import lax
from jax.experimental import pallas as pl
from jax.experimental.pallas import tpu as pltpu
from jax.sharding import PartitionSpec as P

HEAD_DIM = 64
EPS = 1e-06
THETA = 10000.0
NEG = -1e30
MESH = pl.DeviceIdType.MESH
BF16 = jnp.bfloat16
F32 = jnp.float32
VMEM = pltpu.VMEM
MIB = 1 << 20


def dot(left, right, left_dim=1, right_dim=0):
    return lax.dot_general(
        left, right, (((left_dim,), (right_dim,)), ((), ())), preferred_element_type=F32
    )


def across(left, right):
    return dot(left, right, 0, 0)


def against(left, right):
    return dot(left, right, 1, 1)


def norm_back(grad_normed, values, gain):
    scale_inv = lax.rsqrt(jnp.mean(values * values, axis=-1, keepdims=True) + EPS)
    normed = values * scale_inv
    grad_scaled = grad_normed * gain
    grad_values = scale_inv * (
        grad_scaled - normed * jnp.mean(grad_scaled * normed, axis=-1, keepdims=True)
    )
    grad_gain = jnp.sum(grad_normed * normed, axis=0)
    return (grad_values, grad_gain)


def turned(values, cosine, sine):
    lane = lax.broadcasted_iota(jnp.int32, values.shape, 1) % HEAD_DIM
    other = jnp.where(
        lane < HEAD_DIM // 2,
        pltpu.roll(values, 128 - HEAD_DIM // 2, 1),
        pltpu.roll(values, HEAD_DIM // 2, 1),
    )
    return values * cosine + other * sine


def greet(parts, me):
    barrier = pltpu.get_barrier_semaphore()
    for step in range(1, parts):
        pl.semaphore_signal(
            barrier, 1, device_id={"seq": lax.rem(me + step, parts)}, device_id_type=MESH
        )
    return parts - 1


def send(source, target, send_sem, recv_sem, peer):
    return pltpu.make_async_remote_copy(
        src_ref=source,
        dst_ref=target,
        send_sem=send_sem,
        recv_sem=recv_sem,
        device_id={"seq": peer},
        device_id_type=MESH,
    )


def arrive(ref, sem):
    pltpu.make_async_copy(ref, ref, sem).wait()


def own_head(values, head, width):
    if width == HEAD_DIM:
        return values
    lane = lax.broadcasted_iota(jnp.int32, values.shape, 1)
    return jnp.where(lane // HEAD_DIM == head, values, jnp.zeros_like(values))


def allowed_tile(i, j, tokens, start):
    key = j * tokens + lax.broadcasted_iota(jnp.int32, (tokens, tokens), 0)
    query = i * tokens + lax.broadcasted_iota(jnp.int32, (tokens, tokens), 1)
    return (key <= query) & (key >= start[i])


def forward_kernel(
    parts, heads, pieces, count,
    q_in, k_in, v_in, start, *refs,
):
    helds, refs = refs[: len(pieces)], refs[len(pieces) :]
    q_all, k_all, v_all, o_all, lse_all, attended = refs[:6]
    fulls, refs = refs[6 : 6 + count], refs[6 + count :]
    v_turn, total, o_send, in_send, in_recv, o_out, o_in, *sems = refs
    place = Place()
    _, tokens, width = q_in.shape
    half = parts // 2
    me = lax.axis_index("seq")
    own = me // half
    place.greet(greet(parts, me))
    spread = WeightSpread(place, pieces, helds, fulls, sems)
    pairs = ((q_in, q_all), (k_in, k_all), (v_in, v_all))

    def moved(index, peer):
        source, target = pairs[index]
        return send(
            source.at[peer], target.at[me], in_send.at[index, peer], in_recv.at[index, me], peer
        )

    def over(first, action):
        def body(step, _):
            action(first + lax.rem(me + step, half))
            return 0

        lax.fori_loop(0, half, body, 0)

    def start_cross(indices):
        over((1 - own) * half, lambda peer: [moved(index, peer).start() for index in indices])

    def sent_cross(indices):
        over((1 - own) * half, lambda peer: [moved(index, peer).wait_send() for index in indices])

    for index, (source, target) in enumerate(pairs):
        pltpu.make_async_copy(source.at[me], target.at[me], in_recv.at[index, me]).start()
    def start_near(peer):
        @pl.when(peer != me)
        def _():
            for index in range(3):
                moved(index, peer).start()

    over(own * half, start_near)
    pl.when(own == 0)(lambda: start_cross((1, 2)))
    pl.when(own == 1)(lambda: start_cross((0,)))

    def got(index, block):
        arrive(pairs[index][1].at[block], in_recv.at[index, block])

    def got_keys(block):
        got(1, block)
        got(2, block)
        v_turn[block] = v_all[block].T

    def tile(i, j, masked):
        if masked:
            allowed = allowed_tile(i, j, tokens, start)
        queries, keys = q_all[i], k_all[j]
        for head in range(heads):
            rows = slice(head * HEAD_DIM, (head + 1) * HEAD_DIM)
            scores = against(keys, own_head(queries, head, width))
            if masked:
                scores = jnp.where(allowed, scores, NEG)
            old = lse_all[i, head]
            new = jnp.maximum(old, jnp.max(scores, axis=0, keepdims=True))
            weights = jnp.exp(scores - new)
            factor = jnp.exp(old - new)
            lse_all[i, head] = new
            total[i, head] = total[i, head] * factor + jnp.sum(weights, axis=0, keepdims=True)
            o_all[i, rows] = o_all[i, rows] * factor + dot(
                v_turn[j, rows], weights.astype(BF16)
            )

    def tile_row(row, _):
        phase, place_in = row // half, lax.rem(row, half)
        lower = jnp.where(phase == 0, own, 1 - own) * half
        i = jnp.where(phase == 1, half, lower) + place_in
        first = jnp.where(phase == 1, 0, lower)
        last = jnp.where(phase == 1, half, i + 1)
        spread.at_row(row, 3 * half)

        @pl.when(phase == 0)
        def _():
            got(0, i)
            got_keys(i)

        @pl.when((row == half) & (own == 0))
        def _():
            lax.fori_loop(half, parts, lambda block, _: got(0, block) or 0, 0)

        @pl.when((row == half) & (own == 1))
        def _():
            lax.fori_loop(0, half, lambda block, _: got_keys(block) or 0, 0)

        @pl.when((row == half * 3 // 4) & (own == 1))
        def _():
            sent_cross((0,))
            start_cross((1, 2))

        @pl.when((row == half + half // 2) & (own == 0))
        def _():
            sent_cross((1, 2))
            start_cross((0,))

        @pl.when((phase == 2) & (own == 0))
        def _():
            got_keys(i)

        @pl.when((phase == 2) & (own == 1))
        def _():
            got(0, i)

        @pl.when((phase == 0) | ((phase == 1) & (own == 0)) | ((phase == 2) & (own == 1)))
        def _():
            lse_all[i] = jnp.full(lse_all.shape[1:], NEG, F32)
            total[i] = jnp.zeros(total.shape[1:], F32)
            o_all[i] = jnp.zeros(o_all.shape[1:], F32)

        def key_block(j, _):
            masked = (j == 0) | (j == i) | (i == parts - 1)
            pl.when(masked)(lambda: tile(i, j, True))
            pl.when(jnp.logical_not(masked))(lambda: tile(i, j, False))
            return 0

        lax.fori_loop(first, last, key_block, 0)

        @pl.when(((phase == 0) & (own == 0)) | ((phase == 1) & (own == 1)) | (phase == 2))
        def _():
            for head in range(heads):
                rows = slice(head * HEAD_DIM, (head + 1) * HEAD_DIM)
                o_all[i, rows] = o_all[i, rows] / total[i, head]
                lse_all[i, head] = lse_all[i, head] + jnp.log(total[i, head])
            o_send[i] = o_all[i].T.astype(BF16)

            @pl.when(i == me)
            def _():
                pltpu.make_async_copy(o_send.at[i], attended.at[me], o_in.at[me]).start()

            @pl.when(i != me)
            def _():
                send(o_send.at[i], attended.at[me], o_out.at[i], o_in.at[me], i).start()

        return 0

    lax.fori_loop(0, 3 * half, tile_row, 0)
    spread.finish()
    pl.when(own == 0)(lambda: sent_cross((0,)))
    pl.when(own == 1)(lambda: sent_cross((1, 2)))

    def sent_near(peer):
        @pl.when(peer != me)
        def _():
            for index in range(3):
                moved(index, peer).wait_send()

    over(own * half, sent_near)

    def finish(step, _):
        peer = lax.rem(me + step, parts)
        arrive(o_send.at[peer], o_out.at[peer])
        arrive(attended.at[peer], o_in.at[peer])
        return 0

    lax.fori_loop(1, parts, finish, 0)
    arrive(attended.at[me], o_in.at[me])


def attend(q, k, v, start, helds, pieces, shapes):
    parts, tokens, width = q.shape
    heads = width // HEAD_DIM
    place = Place()
    whole = pl.BlockSpec(memory_space=VMEM)
    far = pl.BlockSpec(memory_space=pl.ANY)
    split = jax.ShapeDtypeStruct(q.shape, BF16)
    flops = 4 * parts * parts * tokens * tokens * width // 2
    fulls = [
        jax.ShapeDtypeStruct((place.xs, 2, place.as_, place.bs, *shape), BF16) for shape in shapes
    ]
    results = pl.pallas_call(
        functools.partial(forward_kernel, parts, heads, pieces, len(shapes)),
        in_specs=[whole] * 4 + [far] * len(pieces),
        out_specs=[whole] * 6 + [far] * len(shapes),
        out_shape=[
            split,
            split,
            split,
            jax.ShapeDtypeStruct((parts, width, tokens), F32),
            jax.ShapeDtypeStruct((parts, heads, 1, tokens), F32),
            split,
            *fulls,
        ],
        scratch_shapes=[
            VMEM((parts, width, tokens), BF16),
            VMEM((parts, heads, 1, tokens), F32),
            VMEM((parts, tokens, width), BF16),
            pltpu.SemaphoreType.DMA((3, parts)),
            pltpu.SemaphoreType.DMA((3, parts)),
            pltpu.SemaphoreType.DMA((parts,)),
            pltpu.SemaphoreType.DMA((parts,)),
            *[spread_semaphores(place)] * len(pieces),
        ],
        compiler_params=pltpu.CompilerParams(
            collective_id=1, has_side_effects=True, vmem_limit_bytes=48 * MIB
        ),
        cost_estimate=pl.CostEstimate(
            flops=4 * flops, bytes_accessed=16 * q.size, transcendentals=flops // 256
        ),
        name="attend",
    )(q, k, v, start, *helds)
    devices = place.xs * 2 * place.as_ * place.bs
    weights = [value.reshape(devices, *value.shape[4:]) for value in results[6:]]
    return results[:6], weights


def backward_kernel(
    parts, heads, pieces, count,
    d_in, q_all, k_all, v_all, o_all, lse_all, start, *refs,
):
    grads, refs = refs[:count], refs[count:]
    (dq_got, dk_got, dv_got), refs = refs[:3], refs[3:]
    results, refs = refs[: len(pieces)], refs[len(pieces) :]
    d_all, k_turn, delta, dq_turn, dk_sum, dv_sum, dq_send, dk_send, dv_send = refs[:9]
    in_send, in_recv, out_send, out_recv, *buffers = refs[9:]
    place = Place()
    _, tokens, width = d_in.shape
    half = parts // 2
    me = lax.axis_index("seq")
    own = me // half
    place.greet(greet(parts, me))
    adding = GradSums(place, pieces, grads, results, buffers)

    def over(first, action):
        def body(step, _):
            action(first + lax.rem(me + step, half))
            return 0

        lax.fori_loop(0, half, body, 0)

    def moved(peer):
        return send(d_in.at[peer], d_all.at[me], in_send.at[peer], in_recv.at[me], peer)

    pltpu.make_async_copy(d_in.at[me], d_all.at[me], in_recv.at[me]).start()

    def start_near(peer):
        pl.when(peer != me)(lambda: moved(peer).start())

    over(own * half, start_near)
    over((1 - own) * half, lambda peer: moved(peer).start())
    sends = ((dq_send, dq_got), (dk_send, dk_got), (dv_send, dv_got))

    def give(index, block):
        source, target = sends[index]

        @pl.when(block == me)
        def _():
            pltpu.make_async_copy(
                source.at[block], target.at[me], out_recv.at[index, me]
            ).start()

        @pl.when(block != me)
        def _():
            send(
                source.at[block], target.at[me],
                out_send.at[index, block], out_recv.at[index, me], block,
            ).start()

    def give_query(i):
        dq_send[i] = (dq_turn[i] * HEAD_DIM**-0.5).T.astype(BF16)
        give(0, i)

    def give_keys(j):
        dk_send[j] = dk_sum[j].astype(BF16)
        dv_send[j] = dv_sum[j].astype(BF16)
        give(1, j)
        give(2, j)

    def tile(i, j, masked):
        if masked:
            allowed = allowed_tile(i, j, tokens, start)
        queries, grads_out, keys, mixed = q_all[i], d_all[i], k_all[j], v_all[j]
        for head in range(heads):
            rows = slice(head * HEAD_DIM, (head + 1) * HEAD_DIM)
            query, grad = own_head(queries, head, width), own_head(grads_out, head, width)
            scores = against(keys, query)
            if masked:
                scores = jnp.where(allowed, scores, NEG)
            weights = jnp.exp(scores - lse_all[i, head])
            dv_sum[j] += dot(weights.astype(BF16), grad)
            slope = against(mixed, grad) - delta[i, head]
            d_scores = (weights * slope).astype(BF16)
            dk_sum[j] += dot(d_scores, query)
            dq_turn[i, rows] += dot(k_turn[j, rows], d_scores)

    def prepare(block):
        arrive(d_all.at[block], in_recv.at[block])
        product = d_all[block].astype(F32).T * o_all[block]
        for head in range(heads):
            rows = slice(head * HEAD_DIM, (head + 1) * HEAD_DIM)
            delta[block, head] = jnp.sum(product[rows], axis=0, keepdims=True)
        k_turn[block] = k_all[block].T
        dq_turn[block] = jnp.zeros(dq_turn.shape[1:], F32)
        dk_sum[block] = jnp.zeros(dk_sum.shape[1:], F32)
        dv_sum[block] = jnp.zeros(dv_sum.shape[1:], F32)

    def tile_row(row, _):
        phase, place_in = row // half, lax.rem(row, half)
        adding.at_row(row, 3 * half)

        @pl.when(row == 0)
        def _():
            lax.fori_loop(0, half, lambda n, _: prepare(own * half + n) or 0, 0)

        @pl.when(row == half)
        def _():
            lax.fori_loop(0, half, lambda n, _: prepare((1 - own) * half + n) or 0, 0)

        by_query = jnp.where(phase == 1, own == 1, own == 0)
        lower = jnp.where(phase == 0, own, 1 - own) * half
        outer = jnp.where(
            phase == 2, jnp.where(by_query, half, 0), lower
        ) + place_in
        first = jnp.where(phase == 2, jnp.where(by_query, 0, half), jnp.where(by_query, lower, outer))
        last = jnp.where(
            phase == 2,
            jnp.where(by_query, half, parts),
            jnp.where(by_query, outer + 1, lower + half),
        )

        def inner_block(inner, _):
            i, j = jnp.where(by_query, outer, inner), jnp.where(by_query, inner, outer)
            masked = (j == 0) | (j == i) | (i == parts - 1)
            pl.when(masked)(lambda: tile(i, j, True))
            pl.when(jnp.logical_not(masked))(lambda: tile(i, j, False))
            return 0

        lax.fori_loop(first, last, inner_block, 0)
        pl.when(by_query)(lambda: give_query(outer))
        pl.when(jnp.logical_not(by_query))(lambda: give_keys(outer))
        return 0

    lax.fori_loop(0, 3 * half, tile_row, 0)
    pl.when(own == 0)(lambda: over(0, give_keys))
    pl.when(own == 1)(lambda: over(half, give_query))
    adding.finish()

    def finish(step, _):
        peer = lax.rem(me + step, parts)
        moved(peer).wait_send()
        for index, (source, target) in enumerate(sends):
            arrive(source.at[peer], out_send.at[index, peer])
            arrive(target.at[peer], out_recv.at[index, peer])
        return 0

    lax.fori_loop(1, parts, finish, 0)
    for index, (_, target) in enumerate(sends):
        arrive(target.at[me], out_recv.at[index, me])


def attend_back(d_att, q, k, v, o, lse, start, grads, pieces):
    parts, tokens, width = q.shape
    heads = width // HEAD_DIM
    place = Place()
    whole = pl.BlockSpec(memory_space=VMEM)
    far = pl.BlockSpec(memory_space=pl.ANY)
    split = jax.ShapeDtypeStruct(q.shape, BF16)
    flops = 10 * parts * parts * tokens * tokens * width // 2
    sum_shapes = [piece.held(place, grads[piece.array].shape[1]) for piece in pieces]
    sum_scratch = GradSums.scratch(place, pieces, grads)
    grads = [placed(place, grad) for grad in grads]
    results = pl.pallas_call(
        functools.partial(backward_kernel, parts, heads, pieces, len(grads)),
        in_specs=[far] + [whole] * 6 + [far] * len(grads),
        out_specs=[far] * 3 + [far] * len(pieces),
        out_shape=[split] * 3 + sum_shapes,
        scratch_shapes=[
            VMEM((parts, tokens, width), BF16),
            VMEM((parts, width, tokens), BF16),
            VMEM((parts, heads, 1, tokens), F32),
            VMEM((parts, width, tokens), F32),
            VMEM((parts, tokens, width), F32),
            VMEM((parts, tokens, width), F32),
            VMEM((parts, tokens, width), BF16),
            VMEM((parts, tokens, width), BF16),
            VMEM((parts, tokens, width), BF16),
            pltpu.SemaphoreType.DMA((parts,)),
            pltpu.SemaphoreType.DMA((parts,)),
            pltpu.SemaphoreType.DMA((3, parts)),
            pltpu.SemaphoreType.DMA((3, parts)),
            *sum_scratch,
        ],
        compiler_params=pltpu.CompilerParams(
            collective_id=2, has_side_effects=True, vmem_limit_bytes=60 * MIB
        ),
        cost_estimate=pl.CostEstimate(
            flops=4 * flops, bytes_accessed=20 * q.size, transcendentals=flops // 640
        ),
        name="attend_back",
    )(d_att, q, k, v, o, lse, start, *grads)
    return results[:3], results[3:]


class Place:
    def __init__(self):
        self.xs = lax.axis_size("dp") // 2
        seq = lax.axis_size("seq")
        self.bs = 2 if seq <= 8 else 4
        self.as_ = seq // self.bs
        dp, rank = lax.axis_index("dp"), lax.axis_index("seq")
        self.x, self.core = dp // 2, lax.rem(dp, 2)
        self.a, self.b = rank // self.bs, lax.rem(rank, self.bs)

    def device(self, x=None, core=None, a=None, b=None):
        x, core = (self.x if x is None else x), (self.core if core is None else core)
        a, b = (self.a if a is None else a), (self.b if b is None else b)
        return (x * 2 + core, a * self.bs + b)

    def peers(self, axis):
        size = {"x": self.xs, "a": self.as_, "b": self.bs}[axis]
        own = getattr(self, axis)
        return [(step - 1, lax.rem(own + step, size)) for step in range(1, size)]

    def greet(self, greeted=0):
        barrier = pltpu.get_barrier_semaphore()
        others = [self.device(core=1 - self.core)]
        for axis in "x" if greeted else "xab":
            others += [self.device(**{axis: index}) for _, index in self.peers(axis)]
        for other in others:
            pl.semaphore_signal(barrier, 1, device_id=other, device_id_type=MESH)
        pl.semaphore_wait(barrier, len(others) + greeted)

    @property
    def inner(self):
        return (self.a == 1) | (self.a == 2)

    @property
    def beside(self):
        return self.a + 1 - 2 * lax.rem(self.a, 2)


def column_pieces(columns, wanted):
    tiles = columns // 128
    wanted = min(wanted, tiles)
    edges = [tiles * n // wanted * 128 for n in range(wanted)] + [columns]
    return [(edges[n], edges[n + 1] - edges[n]) for n in range(wanted)]


def placed(place, value):
    return value.reshape(place.xs, 2, place.as_, place.bs, *value.shape[1:])


def remote(source, target, send_sem, recv_sem, device):
    return pltpu.make_async_remote_copy(
        src_ref=source,
        dst_ref=target,
        send_sem=send_sem,
        recv_sem=recv_sem,
        device_id=device,
        device_id_type=MESH,
    )


def flat(ref):
    rows, columns = ref.shape[-2:]
    return ref.reshape(ref.size // (rows * columns), rows, columns)


class Relay:
    def __init__(self, place, source, target, sems):
        self.p, self.source, self.target, self.sems = place, source, target, sems
        assert place.as_ == 4

    def near(self):
        p = self.p
        return remote(
            self.source, self.target.at[p.a],
            self.sems.at[0, 0], self.sems.at[1, 0], p.device(a=p.beside),
        )

    def middle(self):
        p = self.p
        held = self.target.at[pl.ds(p.a // 2 * 2, 2)]
        return remote(
            held, held, self.sems.at[0, 1], self.sems.at[1, 1], p.device(a=3 - p.a)
        )

    def outward(self):
        p = self.p
        held = self.target.at[pl.ds((1 - p.a // 2) * 2, 2)]
        return remote(
            held, held, self.sems.at[0, 2], self.sems.at[1, 1], p.device(a=p.beside)
        )

    def local(self):
        return pltpu.make_async_copy(self.source, self.target.at[self.p.a], self.sems.at[1, 2])

    def step(self, number):
        if number == 0:
            self.local().start()
            self.near().start()
        elif number == 1:
            self.local().wait()
            self.near().wait_recv()
            pl.when(self.p.inner)(lambda: self.middle().start())
        elif number == 2:

            @pl.when(self.p.inner)
            def _():
                self.middle().wait_recv()
                self.outward().start()
        else:

            @pl.when(jnp.logical_not(self.p.inner))
            def _():
                self.middle().wait_recv()

            @pl.when(self.p.inner)
            def _():
                self.middle().wait_send()
                self.outward().wait_send()

            self.near().wait_send()


class Direct:
    def __init__(self, place, source, target, sems):
        self.p, self.source, self.target, self.sems = place, source, target, sems

    def copies(self):
        p = self.p
        return [
            remote(
                self.source, self.target.at[p.a],
                self.sems.at[0, s], self.sems.at[1, s], p.device(a=index),
            )
            for s, index in p.peers("a")
        ]

    def local(self):
        return pltpu.make_async_copy(self.source, self.target.at[self.p.a], self.sems.at[0, 3])

    def step(self, number):
        if number == 0:
            self.local().start()
            for copy in self.copies():
                copy.start()
        elif number == 3:
            self.local().wait()
            for copy in self.copies():
                copy.wait()


class Piece:
    def __init__(self, array, start, size, order, deep):
        self.array, self.start, self.size, self.order, self.deep = array, start, size, order, deep

    @staticmethod
    def all(shapes):
        pieces = []
        for array, kinds in enumerate(
            ([("bx", 0)], [("bx", 1)] * 2, [("xb", 1), ("bx", 1)], [("bx", 0)] * 2)
        ):
            for (start, size), kind in zip(column_pieces(shapes[array][1], len(kinds)), kinds):
                pieces.append(Piece(array, start, size, *kind))
        return pieces

    def held(self, place, rows):
        lead = {"": (), "b": (place.bs,), "x": (place.xs,)}[self.order[0] if self.deep else ""]
        lead = (*lead, place.as_) if self.order[0] == "x" else (place.as_, *lead)
        return jax.ShapeDtypeStruct((*lead, rows, self.size), BF16)

    def along_a(self, place, held):
        if not self.deep:
            return held
        return held.at[place.x] if self.order[0] == "x" else held.at[:, place.b]

    def columns(self, ref):
        return ref.at[(slice(None),) * (len(ref.shape) - 1) + (pl.ds(self.start, self.size),)]


class Spread:
    def __init__(self, place, views, order, sems, source=None, first=0):
        self.place, self.views, self.order, self.sems = place, views, order, sems
        self.source, self.first = source, first

    @staticmethod
    def views_of(place, full, order):
        p = place
        middle = full.at[:, p.core, :, p.b] if order == "xb" else full.at[p.x, p.core]
        return full.at[p.x, p.core, :, p.b], middle, full.at[:, p.core]

    def copies(self, number):
        p, view = self.place, self.views[number]
        source = self.source if self.source is not None and number == self.first else view
        base = sum([len(p.peers(axis)) for axis in self.order][:number])
        if number == 2:
            devices = [(0, p.device(core=1 - p.core))]
        else:
            axis = self.order[number]
            devices = [(s, p.device(**{axis: index})) for s, index in p.peers(axis)]
        return [
            remote(source, view, self.sems.at[0, base + s], self.sems.at[1, base + s], device)
            for s, device in devices
        ]

    def local(self):
        return pltpu.make_async_copy(self.source, self.views[self.first], self.sems.at[2, 0])

    def start(self, number):
        if self.source is not None and number == self.first:
            self.local().start()
        for copy in self.copies(number):
            copy.start()

    def finish(self, number):
        if self.source is not None and number == self.first:
            self.local().wait()
        for copy in self.copies(number):
            copy.wait_recv()
            copy.wait_send()

    def then(self, number):
        self.finish(number)
        if number < 2:
            self.start(number + 1)


def spread_semaphores(place):
    return pltpu.SemaphoreType.DMA((3, place.xs + place.bs - 1))


RELAY_SEMAPHORES = (2, 4)


class InRows:
    def at_row(self, row, count):
        for at in sorted({at for at, _ in self.actions() if at < 12}):

            @pl.when(row == at * count // 12)
            def _():
                for own_row, action in self.actions():
                    if own_row == at:
                        action()

    def finish(self):
        for at, action in self.actions():
            if at >= 12:
                action()


class WeightSpread(InRows):
    def __init__(self, place, pieces, sources, fulls, sems):
        self.units = []
        for piece, source, own_sems in zip(pieces, sources, sems):
            full = piece.columns(fulls[piece.array])
            views = Spread.views_of(place, full, piece.order)
            self.units.append(Spread(place, views, piece.order, own_sems, source, piece.deep))

    def actions(self):
        out, gate0, gate1, up0, up1, down0, down1 = self.units
        start = lambda unit: functools.partial(unit.start, unit.first)
        then = lambda unit, number: functools.partial(unit.then, number)
        done = [(0, start(unit)) for unit in (gate0, down0, gate1, down1, up1, out, up0)]
        done += [(4, then(down0, 0)), (5, then(down1, 0)), (6, then(out, 0))]
        done += [(7, then(gate0, 1)), (8, then(gate1, 1)), (9, then(up0, 1)), (10, then(up1, 1))]
        done += [(12, then(unit, 1)) for unit in (down0, down1, out)]
        done += [(12, then(unit, 2)) for unit in (gate0, gate1, up0, up1, down0, down1, out)]
        return done


class TotalSum:
    def __init__(self, place, mine, got, sems):
        self.place, self.mine, self.got, self.sems = place, mine, got, sems

    def slots(self, number):
        p = self.place
        devices = [[p.device(core=1 - p.core)]]
        devices += [[p.device(**{axis: index}) for _, index in p.peers(axis)] for axis in "xba"]
        return sum(len(some) for some in devices[:number]), devices[number]

    def copies(self, number):
        base, devices = self.slots(number)
        return [
            remote(
                self.mine, self.got.at[base + n],
                self.sems.at[0, base + n], self.sems.at[1, base + n], device,
            )
            for n, device in enumerate(devices)
        ]

    def start(self, number):
        for copy in self.copies(number):
            copy.start()

    def then(self, number):
        for copy in self.copies(number):
            copy.wait()
        base, devices = self.slots(number)
        for slot in range(len(devices)):
            self.mine[...] += self.got[base + slot]
        if number < 3:
            self.start(number + 1)


def opening_kernel(
    plan, pieces, parted,
    x, first, cosine, sine, gains, w_query, w_key, w_value, *refs,
):
    shares, refs = refs[:parted], refs[parted:]
    q_out, k_out, v_out, hidden, gains_total, *fulls = refs[:8]
    helds, refs = refs[8 : 8 + len(pieces)], refs[8 + len(pieces) :]
    got_gains, gain_sems, relay_sems, *sems = refs
    place = Place()
    parts, tokens, width = q_out.shape
    dim = parts * width
    place.greet()
    gains_total[...] = gains[...]
    total = TotalSum(place, gains_total, got_gains, gain_sems)
    units, relays = [], []
    sources = (w_query, w_key, w_value)
    for number, (array, start, size, order) in enumerate(plan):
        views = Spread.views_of(place, fulls[array].at[:, :, :, :, :, pl.ds(start, size)], order)
        relays.append(
            Direct(place, sources[array].at[:, pl.ds(start, size)], views[0], relay_sems.at[number])
        )
        units.append(Spread(place, views, order, sems[number]))
    deep, flat_relays, deep_relays = [], [], []
    for number, (piece, held) in enumerate(zip(pieces, helds)):
        view = piece.along_a(place, held)
        index = len(plan) + number
        relay = Relay(place, piece.columns(shares[piece.array]), view, relay_sems.at[index])
        (deep_relays if piece.deep else flat_relays).append(relay)
        if piece.deep:
            deep.append(Spread(place, [view], piece.order, sems[index]))

    def step(group, number):
        for relay in group:
            relay.step(number)

    def then(some, number):
        for unit in some:
            unit.then(number)

    def weight(array, start, size):
        full = fulls[array]
        rows, columns = full.shape[-2:]
        fold = dim // columns
        value = full[:, :, :, :, :, start % columns : start % columns + size]
        if fold > 1:
            share = rows // fold
            part = start // columns * share
            value = value.astype(F32)[:, :, :, :, part : part + share]
        return value.reshape(dim, size).astype(BF16)

    def project(array):
        for start in range(0, dim, 256):
            raw = dot(hidden[...], weight(array, start, 256))
            if array == 2:
                raw = 0.5 * raw + 0.5 * first[:, start : start + 256].astype(F32)
            for begin in range(0, 256, 128):
                value = raw[:, begin : begin + 128]
                if array < 2:
                    value = turned(value, cosine[...], sine[...])
                if array == 0:
                    value = value * HEAD_DIM**-0.5
                for lane in range(0, 128, width):
                    out = (q_out, k_out, v_out)[array]
                    out[(start + begin + lane) // width] = value[:, lane : lane + width].astype(BF16)

    half = len(units) // 2
    line = deep_relays + flat_relays

    def tick(number):
        for back in (3, 2, 1, 0):
            index = number - back
            if 0 <= index < len(line):
                line[index].step(back)
                if back == 3 and index < len(deep):
                    deep[index].start(0)

    step(relays, 0)
    total.start(0)
    step(relays, 1)
    tick(0)
    step(relays, 2)
    total.then(0)
    for relay, unit in zip(relays, units):
        relay.step(3)
        unit.start(0)
    tick(1)
    total.then(1)
    then(units[:half], 0)
    tick(2)
    then(units[half:], 0)
    total.then(2)
    tick(3)
    total.then(3)
    values = x[...].astype(F32)
    scale = lax.rsqrt(jnp.mean(values * values, axis=-1, keepdims=True) + EPS)
    hidden[...] = (values * scale * gains_total[0:1]).astype(BF16)
    tick(4)
    then(units[:half], 1)
    tick(5)
    then(units[half:], 1)
    for array in range(3):
        then([unit for unit, piece in zip(units, plan) if piece[0] == array], 2)
        project(array)
        tick(6 + array)
    for number in range(9, len(line) + 3):
        tick(number)
    for unit in deep:
        unit.finish(0)


def opening(x, first, cosine, sine, gains, weights, parted, pieces, parts, collective_id):
    place = Place()
    xs, as_, bs = place.xs, place.as_, place.bs
    tokens, dim = x.shape
    plan = []
    for number, array in enumerate(weights):
        for start, size in column_pieces(array.shape[1], 2):
            plan.append((number, start, size, "xb" if len(plan) % 2 == 1 else "bx"))
    shape = jax.ShapeDtypeStruct
    near = [shape((parts, tokens, dim // parts), BF16)] * 3
    near += [shape((tokens, dim), BF16), shape(gains.shape, F32)]
    near += [shape((xs, 2, as_, bs, *array.shape), array.dtype) for array in weights]
    held = [piece.held(place, parted[piece.array].shape[0]) for piece in pieces]
    far, whole = pl.BlockSpec(memory_space=pl.ANY), pl.BlockSpec(memory_space=VMEM)
    count = len(plan) + len(pieces)
    peers = 1 + (xs - 1) + (bs - 1) + (as_ - 1)
    results = pl.pallas_call(
        functools.partial(opening_kernel, plan, pieces, len(parted)),
        in_specs=[whole] * 5 + [far] * (3 + len(parted)),
        out_specs=[whole] * len(near) + [far] * len(held),
        out_shape=near + held,
        scratch_shapes=[
            VMEM((peers, *gains.shape), F32),
            pltpu.SemaphoreType.DMA((2, peers)),
            pltpu.SemaphoreType.DMA((count, *RELAY_SEMAPHORES)),
            *[spread_semaphores(place)] * count,
        ],
        compiler_params=pltpu.CompilerParams(
            collective_id=collective_id, has_side_effects=True, vmem_limit_bytes=48 * MIB
        ),
        cost_estimate=pl.CostEstimate(
            flops=6 * tokens * dim * dim, bytes_accessed=20 * dim * dim, transcendentals=0
        ),
        name="opening",
    )(x, first, cosine, sine, gains, *weights, *parted)
    devices = xs * 2 * as_ * bs
    fulls = [value.reshape(devices, *value.shape[4:]) for value in results[5:8]]
    return results[:4], results[4], fulls, results[8:]


def add_up(mine, others):
    lead = mine.shape[:-2]

    def at(ref, step):
        index = []
        for size in reversed(lead):
            index.insert(0, lax.rem(step, size))
            step = step // size
        return ref.at[tuple(index)]

    def body(step, _):
        total = at(mine, step)[...].astype(F32)
        for other in others:
            total += at(other, step)[...].astype(F32)
        at(mine, step)[...] = total.astype(mine.dtype)
        return 0

    count = 1
    for size in lead:
        count *= size
    lax.fori_loop(0, count, body, 0)


class RelaySum:
    def __init__(self, place, own, inward, middle, last, sems, result):
        self.p, self.own, self.sems, self.result = place, own, sems, result
        self.inward, self.middle, self.last = inward, middle, last
        assert place.as_ == 4

    def move(self, number):
        p = self.p
        far = self.own.at[pl.ds((1 - p.a // 2) * 2, 2)]
        if number == 0:
            source, target, device = far, self.inward, p.beside
        elif number == 1:
            source, target, device = far, self.middle, 3 - p.a
        else:
            source, target, device = self.own.at[p.beside], self.last, p.beside
        return remote(
            source, target, self.sems.at[0, number], self.sems.at[1, number], p.device(a=device)
        )

    def step(self, number):
        p, inner = self.p, self.p.inner
        outer = jnp.logical_not(inner)
        if number == 0:
            pl.when(outer)(lambda: self.move(0).start())
            pl.when(outer)(lambda: self.move(2).start())
        elif number == 1:

            @pl.when(inner)
            def _():
                self.move(0).wait_recv()
                add_up(self.own.at[pl.ds((1 - p.a // 2) * 2, 2)], [self.inward])
                self.move(1).start()
        elif number == 2:

            @pl.when(inner)
            def _():
                self.move(1).wait_recv()
                add_up(self.own.at[pl.ds(p.a // 2 * 2, 2)], [self.middle])
                self.move(2).start()
        else:
            self.move(2).wait_recv()
            self.result[...] = self.own[p.a].astype(F32) + self.last[...].astype(F32)
            pl.when(outer)(lambda: self.move(0).wait_send())
            pl.when(inner)(lambda: self.move(1).wait_send())
            self.move(2).wait_send()

    @staticmethod
    def scratch(rows, columns, dtype):
        return [
            VMEM((2, rows, columns), dtype),
            VMEM((2, rows, columns), dtype),
            VMEM((rows, columns), dtype),
            pltpu.SemaphoreType.DMA((2, 3)),
        ]


class DirectSum:
    def __init__(self, place, own, got, sems, result):
        self.p, self.own, self.got, self.sems, self.result = place, own, got, sems, result

    def copies(self):
        p = self.p
        return [
            remote(
                self.own.at[index], self.got.at[s],
                self.sems.at[0, s], self.sems.at[1, s], p.device(a=index),
            )
            for s, index in p.peers("a")
        ]

    def step(self, number):
        if number == 0:
            for copy in self.copies():
                copy.start()
        elif number == 3:
            total = self.own[self.p.a].astype(F32)
            for slot, copy in enumerate(self.copies()):
                copy.wait()
                total += self.got[slot].astype(F32)
            self.result[...] = total

    @staticmethod
    def scratch(place, rows, columns, dtype):
        return [
            VMEM((place.as_ - 1, rows, columns), dtype),
            pltpu.SemaphoreType.DMA((2, place.as_ - 1)),
        ]


class Sum:
    def __init__(self, place, source, order, buffers):
        self.place, self.order, self.source = place, order, source
        self.own, self.got0, self.got1, self.got2, self.sems = buffers
        self.copied = self.own is not None
        if not self.copied:
            self.own = source.at[:, place.core]

    @property
    def held(self):
        return self.own.at[self.place.x, :, self.place.b]

    @property
    def part(self):
        p = self.place
        return self.own.at[p.x] if self.order[0] == "x" else self.own.at[:, :, p.b]

    def moves(self, number):
        p = self.place
        if number == 0:
            return [(self.source.at[:, 1 - p.core], self.got0, 0, p.device(core=1 - p.core))]
        axis = self.order[number - 1]
        got = self.got1 if number == 1 else self.got2
        moves = []
        for slot, index in p.peers(axis):
            if axis == "x":
                piece = self.own.at[index] if number == 1 else self.own.at[index, :, p.b]
            else:
                piece = self.own.at[:, :, index] if number == 1 else self.own.at[p.x, :, index]
            moves.append((piece, got.at[slot], slot, p.device(**{axis: index})))
        return moves

    def copies(self, number):
        base = sum(([1] + [len(self.place.peers(axis)) for axis in self.order])[:number])
        return [
            remote(source, target, self.sems.at[0, base + s], self.sems.at[1, base + s], device)
            for source, target, s, device in self.moves(number)
        ]

    def local(self):
        return pltpu.make_async_copy(
            self.source.at[:, self.place.core], self.own, self.sems.at[2, 0]
        )

    def start(self, number):
        for copy in self.copies(number):
            copy.start()
        if number == 0 and self.copied:
            self.local().start()

    def finish(self, number):
        p = self.place
        if number == 0 and self.copied:
            self.local().wait()
        for copy in self.copies(number):
            copy.wait_recv()
            copy.wait_send()
        if number == 0:
            add_up(self.own, [self.got0])
        else:
            mine = self.held if number == 2 else self.part
            got = self.got1 if number == 1 else self.got2
            add_up(mine, [got.at[slot] for slot in range(len(p.peers(self.order[number - 1])))])

    @staticmethod
    def scratch(place, rows, size, order, dtype, copied=True):
        xs, as_, bs = place.xs, place.as_, place.bs
        shapes = {
            "x": ((xs - 1, as_, bs, rows, size), (xs - 1, as_, rows, size)),
            "b": ((bs - 1, xs, as_, rows, size), (bs - 1, as_, rows, size)),
        }
        return [VMEM((xs, as_, bs, rows, size), dtype)] * copied + [
            VMEM((xs, as_, bs, rows, size), dtype),
            VMEM(shapes[order[0]][0], dtype),
            VMEM(shapes[order[1]][1], dtype),
            pltpu.SemaphoreType.DMA((3, xs + bs - 1)),
        ]


class GradSums(InRows):
    def __init__(self, place, pieces, grads, results, buffers):
        self.units, self.outs = [], []
        for piece, result in zip(pieces, results):
            source = piece.columns(grads[piece.array])
            unit, buffers = Sum(place, source, piece.order[::-1], buffers[:5]), buffers[5:]
            self.units.append(unit)
            self.outs.append((unit.part if piece.deep else unit.held, result))

    @staticmethod
    def scratch(place, pieces, grads):
        return [
            item
            for piece in pieces
            for item in Sum.scratch(
                place, grads[piece.array].shape[1], piece.size, piece.order[::-1], BF16
            )
        ]

    def actions(self):
        out, gate0, gate1, up0, up1, down0, down1 = self.units

        def copy_of(unit):
            source, result = self.outs[self.units.index(unit)]
            return pltpu.make_async_copy(source, result, unit.sems.at[2, 1])

        def then(unit, number):
            def action():
                unit.finish(number)
                if number < (1 if unit in (gate0, gate1, up0, up1) else 2):
                    unit.start(number + 1)
                else:
                    copy_of(unit).start()

            return action

        order = (down0, down1, out, up0, gate0, gate1, up1)
        done = [(0, functools.partial(unit.start, 0)) for unit in order]
        done += [(row, then(unit, 0)) for row, unit in zip((0, 1, 1, 2, 2, 3, 3), order)]
        done += [(6, then(down0, 1)), (7, then(down1, 1)), (8, then(out, 1)), (9, then(up0, 1))]
        done += [(10, then(gate0, 1)), (11, then(down0, 2))]
        done += [(12, then(down1, 2)), (12, then(out, 2)), (12, then(gate1, 1)), (12, then(up1, 1))]
        done += [(12, lambda unit=unit: copy_of(unit).wait()) for unit in order]
        return done


class HeldSum:
    def __init__(self, place, piece, source, buffers, result):
        self.place, self.piece, self.source = place, piece, source
        self.own, self.got, self.sems, *relay = buffers
        self.relay = RelaySum(place, self.own, *relay, result)
        self.axis = piece.order[0]

    def copies(self):
        if not self.piece.deep:
            return []
        p = self.place
        at = lambda index: self.source.at[index] if self.axis == "x" else self.source.at[:, index]
        return [
            remote(
                at(index), self.got.at[s], self.sems.at[0, s], self.sems.at[1, s],
                p.device(**{self.axis: index}),
            )
            for s, index in p.peers(self.axis)
        ]

    def local(self):
        mine = self.piece.along_a(self.place, self.source)
        return pltpu.make_async_copy(mine, self.own, self.sems.at[2, 0])

    def start(self):
        self.local().start()
        for copy in self.copies():
            copy.start()

    def finish(self):
        self.local().wait()
        copies = self.copies()
        for copy in copies:
            copy.wait_recv()
            copy.wait_send()
        if len(copies):
            add_up(self.own, [self.got.at[slot] for slot in range(len(copies))])
        self.relay.step(0)

    @staticmethod
    def scratch(place, piece, rows):
        count = len(place.peers(piece.order[0])) if piece.deep else 1
        got = (count, place.as_, rows, piece.size) if piece.deep else (1, 1, 16, 128)
        return [
            VMEM((place.as_, rows, piece.size), BF16),
            VMEM(got, BF16),
            pltpu.SemaphoreType.DMA((3, count)),
            *RelaySum.scratch(rows, piece.size, BF16),
        ]


def closing_kernel(
    plan, pieces, rows, fold, parted,
    dq, dk, dv, w_query, w_key, w_value, hidden, x, d_middle, gains, cosine, sine, gain, *refs,
):
    helds, refs = refs[: len(pieces)], refs[len(pieces) :]
    grad_first, grad_x, gains_total, *refs = refs
    results, buffers = refs[: 3 + parted], refs[3 + parted :]
    slopes, weights, hidden_in, x_in, middle, hidden_turn, d_hidden, got_gains, gain_sems = buffers[:9]
    loads, buffers = buffers[9], buffers[10:]
    place = Place()
    parts, tokens, width = dq.shape
    dim = parts * width
    devices = dim // rows
    place.greet()
    copies = [
        pltpu.make_async_copy(source, target, loads.at[n])
        for n, (source, target) in enumerate(
            (
                (hidden, hidden_in), (dq, slopes.at[0]), (w_query, weights.at[0]),
                (dk, slopes.at[1]), (w_key, weights.at[1]), (dv, slopes.at[2]),
                (w_value, weights.at[2]), (x, x_in), (d_middle, middle),
            )
        )
    ]
    for copy in copies:
        copy.start()
    units, relays, grads, rest = [], [], [], []
    for array, start, size, order in plan:
        source = buffers[0]
        unit = Sum(place, source, order, (None, *buffers[1:5]))
        result = results[array].at[:, pl.ds(start, size)]
        relays.append(DirectSum(place, unit.held, *buffers[5:7], result))
        units.append(unit)
        grads.append(source)
        buffers = buffers[7:]
    for piece, held in zip(pieces, helds):
        result = piece.columns(results[3 + piece.array])
        rest.append(HeldSum(place, piece, held, buffers[:7], result))
        buffers = buffers[7:]
    deep = [unit for unit in rest if unit.piece.deep]
    simple = [unit for unit in rest if not unit.piece.deep]
    total = TotalSum(place, gains_total, got_gains, gain_sems)
    for unit in simple + deep:
        unit.start()

    def low(array, first, size):
        done = []
        for start in range(first, first + size, 128):
            picks = range(start // width, (start + 128) // width)
            value = jnp.concatenate([slopes[array, n] for n in picks], axis=1).astype(F32)
            if array < 2:
                value = turned(value, cosine[...], -sine[...])
            else:
                value = 0.5 * value
                grad_first[:, start : start + 128] = value
            done.append(value.astype(BF16))
        return jnp.concatenate(done, axis=1)

    def compute(index):
        array, start, size, _ = plan[index]
        blocks = []
        for part in range(fold):
            first = part * (dim // fold) + start
            slope = low(array, first, size)
            blocks.append(dot(hidden_turn[...], slope).reshape(devices, rows, size))
            d_hidden[...] += against(slope, weights[array, :, first : first + size])
        block = (blocks[0] if fold == 1 else jnp.concatenate(blocks, axis=1)).astype(BF16)
        grads[index][...] = block.reshape(grads[index].shape)

    def step(group, number):
        for unit in group:
            unit.relay.step(number)

    def then(index, number):
        units[index].finish(number)
        if number < 2:
            units[index].start(number + 1)
        else:
            relays[index].step(0)

    copies[0].wait()
    hidden_turn[...] = hidden_in[...].T
    d_hidden[...] = jnp.zeros_like(d_hidden)
    count = len(units)
    for index in range(count):
        array = plan[index][0]
        if index == 0 or plan[index - 1][0] != array:
            copies[1 + 2 * array].wait()
            copies[2 + 2 * array].wait()
        compute(index)
        units[index].start(0)
        if index == 0:
            for unit in simple:
                unit.finish()
        else:
            then(index - 1, 0)
        if index == 2:
            step(simple, 1)
        if index == 4:
            step(simple, 2)
    copies[7].wait()
    copies[8].wait()
    grad_values, grad_gain = norm_back(d_hidden[...], x_in[...].astype(F32), gain[...])
    grad_x[...] = grad_values + middle[...]
    gains_total[...] = gains[...]
    gains_total[0:1] = grad_gain[None]
    total.start(0)
    then(count - 1, 0)
    for unit in deep:
        unit.finish()
    step(simple, 3)
    for index in range(count // 2):
        then(index, 1)
    step(deep, 1)
    total.then(0)
    for index in range(count // 2, count):
        then(index, 1)
    step(deep, 2)
    total.then(1)
    for index in range(count // 2):
        then(index, 2)
    total.then(2)
    for relay in relays[: count // 2]:
        relay.step(1)
    for index in range(count // 2, count):
        then(index, 2)
    step(deep, 3)
    for relay in relays[count // 2 :]:
        relay.step(1)
    total.then(3)
    for relay in relays:
        relay.step(2)
    for relay in relays:
        relay.step(3)


def closing(
    slopes, weights, hidden, x, d_middle, grad_gain, cosine, sine, gain, rows, helds, pieces,
    shapes, collective_id,
):
    place = Place()
    parts, tokens, width = slopes[0].shape
    dim = parts * width
    fold = 1
    while rows * fold % 16:
        fold *= 2
    plan, scratch = [], []
    for array in range(3):
        for start, size in column_pieces(dim // fold, 2):
            order = "bx" if len(plan) % 2 == 1 else "xb"
            plan.append((array, start, size, order))
            lead = (place.xs, 2, place.as_, place.bs)
            scratch.append(VMEM((*lead, rows * fold, size), BF16))
            scratch += Sum.scratch(place, rows * fold, size, order, BF16, False)
            scratch += DirectSum.scratch(place, rows * fold, size, BF16)
    for piece in pieces:
        scratch += HeldSum.scratch(place, piece, shapes[piece.array][0])
    peers = 1 + (place.xs - 1) + (place.bs - 1) + (place.as_ - 1)
    gains = jnp.pad(grad_gain[None], ((1, 6), (0, 0)))
    far, whole = pl.BlockSpec(memory_space=pl.ANY), pl.BlockSpec(memory_space=VMEM)
    shape = jax.ShapeDtypeStruct
    out = [shape((tokens, dim), F32), shape((tokens, dim), F32), shape((8, dim), F32)]
    out += [shape((rows * fold, dim // fold), F32)] * 3
    out += [shape(each, F32) for each in shapes]
    return pl.pallas_call(
        functools.partial(closing_kernel, plan, pieces, rows, fold, len(shapes)),
        in_specs=[far] * 9 + [whole] * 4 + [far] * len(helds),
        out_specs=[whole] * len(out),
        out_shape=out,
        scratch_shapes=[
            VMEM((3, parts, tokens, width), BF16),
            VMEM((3, dim, dim), BF16),
            VMEM((tokens, dim), BF16),
            VMEM((tokens, dim), BF16),
            VMEM((tokens, dim), F32),
            VMEM((dim, tokens), BF16),
            VMEM((tokens, dim), F32),
            VMEM((peers, 8, dim), F32),
            pltpu.SemaphoreType.DMA((2, peers)),
            pltpu.SemaphoreType.DMA((9,)),
            *scratch,
        ],
        compiler_params=pltpu.CompilerParams(
            collective_id=collective_id, has_side_effects=True, vmem_limit_bytes=60 * MIB
        ),
        cost_estimate=pl.CostEstimate(
            flops=12 * tokens * dim * dim, bytes_accessed=20 * dim * dim, transcendentals=0
        ),
        name="closing",
    )(*slopes, *weights, hidden, x, d_middle, gains, cosine, sine, gain, *helds)


def stacked(value, devices):
    rows, columns = value.shape[0] // devices, value.shape[1]
    fold = 1
    while rows * fold % 16:
        fold *= 2
    value = value.reshape(devices, rows, fold, columns // fold)
    return value.transpose(0, 2, 1, 3).reshape(devices, rows * fold, columns // fold)


def unstacked(value, rows):
    devices, high, columns = value.shape
    value = value.reshape(devices, high // rows, rows, columns).transpose(0, 2, 1, 3)
    return value.reshape(devices * rows, high // rows * columns)


def middle_kernel(
    steps, x, att, dy, w_out, gain, w_gate, w_up, w_down,
    out, d_middle, d_att, g_out, g_gate, g_up, g_down, g_gain,
    attended, middle, hidden, hidden_turn, result, d_hidden,
):
    step = pl.program_id(0)
    parts, _, width = att.shape

    @pl.when(step == 0)
    def _():
        for part in range(parts):
            attended[:, part * width : (part + 1) * width] = att[part]
        total = x[...].astype(F32) + dot(attended[...], w_out[...])
        scale = lax.rsqrt(jnp.mean(total * total, axis=-1, keepdims=True) + EPS)
        normed = (total * scale * gain[...]).astype(BF16)
        middle[...] = total
        result[...] = total
        hidden[...] = normed
        hidden_turn[...] = normed.T
        d_hidden[...] = jnp.zeros_like(d_hidden)

    grad = dy[...]
    gate = dot(hidden[...], w_gate[...])
    up = dot(hidden[...], w_up[...])
    d_inner = against(grad, w_down[...])
    sigma = jax.nn.sigmoid(gate)
    silu = gate * sigma
    inner = (silu * up).astype(BF16)
    d_gate = (d_inner * up * sigma * (1.0 + gate * (1.0 - sigma))).astype(BF16)
    d_up = (d_inner * silu).astype(BF16)
    result[...] += dot(inner, w_down[...])
    g_down[...] = across(inner, grad).astype(BF16)
    g_gate[...] = dot(hidden_turn[...], d_gate).astype(BF16)
    g_up[...] = dot(hidden_turn[...], d_up).astype(BF16)
    d_hidden[...] += against(d_gate, w_gate[...]) + against(d_up, w_up[...])

    @pl.when(step == steps - 1)
    def _():
        out[...] = result[...].astype(BF16)
        grad_values, grad_gain = norm_back(d_hidden[...], middle[...], gain[...])
        total = grad_values + dy[...].astype(F32)
        d_middle[...] = total
        g_gain[...] = grad_gain[None]
        d_branch = total.astype(BF16)
        g_out[...] = across(attended[...], d_branch).astype(BF16)
        back = against(d_branch, w_out[...]).astype(BF16)
        for part in range(parts):
            d_att[part] = back[:, part * width : (part + 1) * width]


def between(x, att, dy, w_out, gain, w_gate, w_up, w_down):
    tokens, dim = x.shape
    units = w_gate.shape[1]
    chunk = 512 if units % 512 == 0 else 128
    whole = lambda value: pl.BlockSpec(value.shape, lambda g: (0,) * len(value.shape))
    wide = pl.BlockSpec((dim, chunk), lambda g: (0, g))
    tall = pl.BlockSpec((chunk, dim), lambda g: (g, 0))
    shape = jax.ShapeDtypeStruct
    outs = [
        shape((tokens, dim), BF16),
        shape((tokens, dim), F32),
        shape(att.shape, BF16),
        shape(w_out.shape, BF16),
        shape(w_gate.shape, BF16),
        shape(w_up.shape, BF16),
        shape(w_down.shape, BF16),
        shape((1, dim), F32),
    ]
    return pl.pallas_call(
        functools.partial(middle_kernel, units // chunk),
        grid=(units // chunk,),
        in_specs=[whole(v) for v in (x, att, dy, w_out, gain)] + [wide, wide, tall],
        out_specs=[whole(v) for v in outs[:4]] + [wide, wide, tall, whole(outs[7])],
        out_shape=outs,
        scratch_shapes=[
            VMEM((tokens, dim), BF16),
            VMEM((tokens, dim), F32),
            VMEM((tokens, dim), BF16),
            VMEM((dim, tokens), BF16),
            VMEM((tokens, dim), F32),
            VMEM((tokens, dim), F32),
        ],
        compiler_params=pltpu.CompilerParams(vmem_limit_bytes=56 * MIB),
        cost_estimate=pl.CostEstimate(
            flops=18 * tokens * dim * units, bytes_accessed=12 * dim * units, transcendentals=0
        ),
        name="between",
    )(x, att, dy, w_out, gain, w_gate, w_up, w_down)


def shards(
    inputs, first_values, lengths, w_query, w_key, w_value, w_out, gain_attn,
    w_gate, w_up, w_down, gain_mlp, cotangent,
):
    row_count, tokens, width = inputs.shape
    assert row_count == 1
    parts = lax.axis_size("seq")
    rank = lax.axis_index("seq")
    devices = lax.axis_size("dp") * parts
    rows, down_rows = w_query.shape[0], w_down.shape[0]
    multiple = 16 if down_rows >= 64 else 8
    down_padded = -(-down_rows // multiple) * multiple

    def spaced(value):
        value = value.reshape(rows, devices, down_rows)
        value = jnp.pad(value, ((0, 0), (0, 0), (0, down_padded - down_rows)))
        return value.reshape(rows, devices * down_padded)

    index = lax.axis_index("dp") * parts + rank
    gains = jnp.pad(jnp.stack([gain_attn, gain_mlp]).astype(F32), ((0, 6), (0, width - rows)))
    gains = jnp.roll(gains, index * rows, axis=1)
    wide = lambda value: stacked(value, 1)[0]
    padded_down = jnp.pad(w_down, ((0, down_padded - down_rows), (0, 0)))
    parted = [wide(w_out), wide(spaced(w_gate)), wide(spaced(w_up)), wide(padded_down)]
    shapes = [value.shape for value in parted]
    pieces = Piece.all(shapes)
    ends = jnp.cumsum(lengths[0])
    begins = ends - lengths[0]
    time = jnp.arange(tokens * parts, dtype=jnp.int32)
    inside = (time[:, None] >= begins[None, :]) & (time[:, None] < ends[None, :])
    start_all = jnp.sum(jnp.where(inside, begins[None, :], 0), axis=1)
    own_start = lax.dynamic_slice_in_dim(start_all, rank * tokens, tokens)
    position = (rank * tokens + jnp.arange(tokens, dtype=jnp.int32) - own_start).astype(F32)
    half = HEAD_DIM // 2
    angles = position[:, None] * THETA ** (-jnp.arange(half, dtype=F32) * 2.0 / HEAD_DIM)
    cosine = jnp.tile(jnp.cos(angles), (1, 4))
    sine = jnp.sin(angles)
    sine = jnp.tile(jnp.concatenate([-sine, sine], axis=1), (1, 2))
    start = start_all.reshape(parts, 1, tokens)

    x_low = inputs.reshape(tokens, width)
    (q, k, v, hidden_in), gains, fulls, helds = opening(
        x_low, first_values.reshape(tokens, width), cosine, sine, gains,
        [wide(w_query), wide(w_key), wide(w_value)], parted, pieces, parts, 3,
    )
    tall = lambda value: unstacked(value, rows)
    query_full, key_full, value_full = (tall(value) for value in fulls)
    gain_one, gain_two = gains[0], gains[1]
    (q_all, k_all, v_all, o_all, lse_all, attended), (*weights, down_full) = attend(
        q, k, v, start, helds, pieces, shapes
    )
    out_full, gate_full, up_full = (tall(value) for value in weights)
    down_full = unstacked(down_full, down_padded)
    output, grad_middle, d_att, grad_out, grad_gate, grad_up, grad_down, grad_gain_two = between(
        x_low, attended, cotangent.reshape(tokens, width), out_full, gain_two[None],
        gate_full, up_full, down_full,
    )
    grad_gain_two = grad_gain_two[0]

    share = lambda grad: stacked(grad.astype(BF16), devices)
    (dq, dk, dv), helds = attend_back(
        d_att, q_all, k_all, v_all, o_all, lse_all, start,
        [share(grad_out), share(grad_gate), share(grad_up), share(grad_down)], pieces,
    )
    (
        grad_first, grad_x, gains_total, total_query, total_key, total_value,
        total_out, total_gate, total_up, total_down,
    ) = closing(
        (dq, dk, dv), (query_full, key_full, value_full), hidden_in, x_low, grad_middle,
        grad_gain_two, cosine, sine, gain_one[None], rows, helds, pieces, shapes, 4,
    )
    own_gain = lambda n: lax.dynamic_slice_in_dim(gains_total[n], index * rows, rows)
    low = lambda total: unstacked(total[None], rows)

    def close(total):
        total = low(total).reshape(rows, devices, down_padded)
        return total[:, :, :down_rows].reshape(rows, devices * down_rows)

    return (
        output.reshape(inputs.shape),
        grad_x.reshape(inputs.shape),
        grad_first.reshape(inputs.shape),
        low(total_query),
        low(total_key),
        low(total_value),
        low(total_out),
        own_gain(0),
        close(total_gate),
        close(total_up),
        unstacked(total_down[None], down_padded)[:down_rows],
        own_gain(1),
    )


def solution(mesh):
    tokens = P("dp", "seq", None)
    matrix = P(("dp", "seq"), None)
    vector = P(("dp", "seq"))
    return jax.shard_map(
        shards,
        mesh=mesh,
        in_specs=(
            tokens, tokens, P("dp", None), matrix, matrix, matrix, matrix, vector,
            matrix, matrix, matrix, vector, tokens,
        ),
        out_specs=(
            tokens, tokens, tokens, matrix, matrix, matrix, matrix, vector,
            matrix, matrix, matrix, vector,
        ),
        check_vma=False,
    )
```

```python
import functools

import jax
import jax.numpy as jnp
from jax import lax
from jax.experimental import pallas as pl
from jax.experimental.pallas import tpu as pltpu
from jax.sharding import PartitionSpec as P

HEAD_DIM = 64
EPS = 1e-06
THETA = 10000.0
NEG = -1e30
MESH = pl.DeviceIdType.MESH
BF16 = jnp.bfloat16
F32 = jnp.float32
VMEM = pltpu.VMEM
MIB = 1 << 20


def dot(left, right, left_dim=1, right_dim=0):
    return lax.dot_general(
        left, right, (((left_dim,), (right_dim,)), ((), ())), preferred_element_type=F32
    )


def across(left, right):
    return dot(left, right, 0, 0)


def against(left, right):
    return dot(left, right, 1, 1)


def norm_back(grad_normed, values, gain):
    scale_inv = lax.rsqrt(jnp.mean(values * values, axis=-1, keepdims=True) + EPS)
    normed = values * scale_inv
    grad_scaled = grad_normed * gain
    grad_values = scale_inv * (
        grad_scaled - normed * jnp.mean(grad_scaled * normed, axis=-1, keepdims=True)
    )
    grad_gain = jnp.sum(grad_normed * normed, axis=0)
    return (grad_values, grad_gain)


def turned(values, cosine, sine):
    lane = lax.broadcasted_iota(jnp.int32, values.shape, 1) % HEAD_DIM
    other = jnp.where(
        lane < HEAD_DIM // 2,
        pltpu.roll(values, 128 - HEAD_DIM // 2, 1),
        pltpu.roll(values, HEAD_DIM // 2, 1),
    )
    return values * cosine + other * sine


def greet(parts, me):
    barrier = pltpu.get_barrier_semaphore()
    for step in range(1, parts):
        pl.semaphore_signal(
            barrier, 1, device_id={"seq": lax.rem(me + step, parts)}, device_id_type=MESH
        )
    return parts - 1


def send(source, target, send_sem, recv_sem, peer):
    return pltpu.make_async_remote_copy(
        src_ref=source,
        dst_ref=target,
        send_sem=send_sem,
        recv_sem=recv_sem,
        device_id={"seq": peer},
        device_id_type=MESH,
    )


def arrive(ref, sem):
    pltpu.make_async_copy(ref, ref, sem).wait()


def own_head(values, head, width):
    if width == HEAD_DIM:
        return values
    lane = lax.broadcasted_iota(jnp.int32, values.shape, 1)
    return jnp.where(lane // HEAD_DIM == head, values, jnp.zeros_like(values))


def allowed_tile(i, j, tokens, start):
    key = j * tokens + lax.broadcasted_iota(jnp.int32, (tokens, tokens), 0)
    query = i * tokens + lax.broadcasted_iota(jnp.int32, (tokens, tokens), 1)
    return (key <= query) & (key >= start[i])


def forward_kernel(
    parts, heads, pieces, count,
    q_in, k_in, v_in, start, *refs,
):
    helds, refs = refs[: len(pieces)], refs[len(pieces) :]
    q_all, k_all, v_all, o_all, lse_all, attended = refs[:6]
    fulls, refs = refs[6 : 6 + count], refs[6 + count :]
    v_turn, total, o_send, in_send, in_recv, o_out, o_in, *sems = refs
    place = Place()
    _, tokens, width = q_in.shape
    half = parts // 2
    me = lax.axis_index("seq")
    own = me // half
    place.greet(greet(parts, me))
    spread = WeightSpread(place, pieces, helds, fulls, sems)
    pairs = ((q_in, q_all), (k_in, k_all), (v_in, v_all))

    def moved(index, peer):
        source, target = pairs[index]
        return send(
            source.at[peer], target.at[me], in_send.at[index, peer], in_recv.at[index, me], peer
        )

    def over(first, action):
        def body(step, _):
            action(first + lax.rem(me + step, half))
            return 0

        lax.fori_loop(0, half, body, 0)

    def start_cross(indices):
        over((1 - own) * half, lambda peer: [moved(index, peer).start() for index in indices])

    def sent_cross(indices):
        over((1 - own) * half, lambda peer: [moved(index, peer).wait_send() for index in indices])

    for index, (source, target) in enumerate(pairs):
        pltpu.make_async_copy(source.at[me], target.at[me], in_recv.at[index, me]).start()
    def start_near(peer):
        @pl.when(peer != me)
        def _():
            for index in range(3):
                moved(index, peer).start()

    over(own * half, start_near)
    pl.when(own == 0)(lambda: start_cross((1, 2)))
    pl.when(own == 1)(lambda: start_cross((0,)))

    def got(index, block):
        arrive(pairs[index][1].at[block], in_recv.at[index, block])

    def got_keys(block):
        got(1, block)
        got(2, block)
        v_turn[block] = v_all[block].T

    def tile(i, j, masked):
        if masked:
            allowed = allowed_tile(i, j, tokens, start)
        queries, keys = q_all[i], k_all[j]
        for head in range(heads):
            rows = slice(head * HEAD_DIM, (head + 1) * HEAD_DIM)
            scores = against(keys, own_head(queries, head, width))
            if masked:
                scores = jnp.where(allowed, scores, NEG)
            old = lse_all[i, head]
            new = jnp.maximum(old, jnp.max(scores, axis=0, keepdims=True))
            weights = jnp.exp(scores - new)
            factor = jnp.exp(old - new)
            lse_all[i, head] = new
            total[i, head] = total[i, head] * factor + jnp.sum(weights, axis=0, keepdims=True)
            o_all[i, rows] = o_all[i, rows] * factor + dot(
                v_turn[j, rows], weights.astype(BF16)
            )

    def tile_row(row, _):
        phase, place_in = row // half, lax.rem(row, half)
        lower = jnp.where(phase == 0, own, 1 - own) * half
        i = jnp.where(phase == 1, half, lower) + place_in
        first = jnp.where(phase == 1, 0, lower)
        last = jnp.where(phase == 1, half, i + 1)
        spread.at_row(row, 3 * half)

        @pl.when(phase == 0)
        def _():
            got(0, i)
            got_keys(i)

        @pl.when((row == half) & (own == 0))
        def _():
            lax.fori_loop(half, parts, lambda block, _: got(0, block) or 0, 0)

        @pl.when((row == half) & (own == 1))
        def _():
            lax.fori_loop(0, half, lambda block, _: got_keys(block) or 0, 0)

        @pl.when((row == half * 3 // 4) & (own == 1))
        def _():
            sent_cross((0,))
            start_cross((1, 2))

        @pl.when((row == half + half // 2) & (own == 0))
        def _():
            sent_cross((1, 2))
            start_cross((0,))

        @pl.when((phase == 2) & (own == 0))
        def _():
            got_keys(i)

        @pl.when((phase == 2) & (own == 1))
        def _():
            got(0, i)

        @pl.when((phase == 0) | ((phase == 1) & (own == 0)) | ((phase == 2) & (own == 1)))
        def _():
            lse_all[i] = jnp.full(lse_all.shape[1:], NEG, F32)
            total[i] = jnp.zeros(total.shape[1:], F32)
            o_all[i] = jnp.zeros(o_all.shape[1:], F32)

        def key_block(j, _):
            masked = (j == 0) | (j == i) | (i == parts - 1)
            pl.when(masked)(lambda: tile(i, j, True))
            pl.when(jnp.logical_not(masked))(lambda: tile(i, j, False))
            return 0

        lax.fori_loop(first, last, key_block, 0)

        @pl.when(((phase == 0) & (own == 0)) | ((phase == 1) & (own == 1)) | (phase == 2))
        def _():
            for head in range(heads):
                rows = slice(head * HEAD_DIM, (head + 1) * HEAD_DIM)
                o_all[i, rows] = o_all[i, rows] / total[i, head]
                lse_all[i, head] = lse_all[i, head] + jnp.log(total[i, head])
            o_send[i] = o_all[i].T.astype(BF16)

            @pl.when(i == me)
            def _():
                pltpu.make_async_copy(o_send.at[i], attended.at[me], o_in.at[me]).start()

            @pl.when(i != me)
            def _():
                send(o_send.at[i], attended.at[me], o_out.at[i], o_in.at[me], i).start()

        return 0

    lax.fori_loop(0, 3 * half, tile_row, 0)
    spread.finish()
    pl.when(own == 0)(lambda: sent_cross((0,)))
    pl.when(own == 1)(lambda: sent_cross((1, 2)))

    def sent_near(peer):
        @pl.when(peer != me)
        def _():
            for index in range(3):
                moved(index, peer).wait_send()

    over(own * half, sent_near)

    def finish(step, _):
        peer = lax.rem(me + step, parts)
        arrive(o_send.at[peer], o_out.at[peer])
        arrive(attended.at[peer], o_in.at[peer])
        return 0

    lax.fori_loop(1, parts, finish, 0)
    arrive(attended.at[me], o_in.at[me])


def attend(q, k, v, start, helds, pieces, shapes):
    parts, tokens, width = q.shape
    heads = width // HEAD_DIM
    place = Place()
    whole = pl.BlockSpec(memory_space=VMEM)
    far = pl.BlockSpec(memory_space=pl.ANY)
    split = jax.ShapeDtypeStruct(q.shape, BF16)
    flops = 4 * parts * parts * tokens * tokens * width // 2
    fulls = [
        jax.ShapeDtypeStruct((place.xs, 2, place.as_, place.bs, *shape), BF16) for shape in shapes
    ]
    results = pl.pallas_call(
        functools.partial(forward_kernel, parts, heads, pieces, len(shapes)),
        in_specs=[whole] * (4 + len(pieces)),
        out_specs=[whole] * 6 + [far] * len(shapes),
        out_shape=[
            split,
            split,
            split,
            jax.ShapeDtypeStruct((parts, width, tokens), F32),
            jax.ShapeDtypeStruct((parts, heads, 1, tokens), F32),
            split,
            *fulls,
        ],
        scratch_shapes=[
            VMEM((parts, width, tokens), BF16),
            VMEM((parts, heads, 1, tokens), F32),
            VMEM((parts, tokens, width), BF16),
            pltpu.SemaphoreType.DMA((3, parts)),
            pltpu.SemaphoreType.DMA((3, parts)),
            pltpu.SemaphoreType.DMA((parts,)),
            pltpu.SemaphoreType.DMA((parts,)),
            *[spread_semaphores(place)] * len(pieces),
        ],
        compiler_params=pltpu.CompilerParams(
            collective_id=1, has_side_effects=True, vmem_limit_bytes=48 * MIB
        ),
        cost_estimate=pl.CostEstimate(
            flops=4 * flops, bytes_accessed=16 * q.size, transcendentals=flops // 256
        ),
        name="attend",
    )(q, k, v, start, *helds)
    devices = place.xs * 2 * place.as_ * place.bs
    weights = [value.reshape(devices, *value.shape[4:]) for value in results[6:]]
    return results[:6], weights


def backward_kernel(
    parts, heads, pieces, count,
    d_in, q_all, k_all, v_all, o_all, lse_all, start, *refs,
):
    grads, refs = refs[:count], refs[count:]
    (dq_got, dk_got, dv_got), refs = refs[:3], refs[3:]
    results, refs = refs[: len(pieces)], refs[len(pieces) :]
    d_all, k_turn, delta, dq_turn, dk_sum, dv_sum, dq_send, dk_send, dv_send = refs[:9]
    in_send, in_recv, out_send, out_recv, *buffers = refs[9:]
    place = Place()
    _, tokens, width = d_in.shape
    half = parts // 2
    me = lax.axis_index("seq")
    own = me // half
    place.greet(greet(parts, me))
    adding = GradSums(place, pieces, grads, results, buffers)

    def over(first, action):
        def body(step, _):
            action(first + lax.rem(me + step, half))
            return 0

        lax.fori_loop(0, half, body, 0)

    def moved(peer):
        return send(d_in.at[peer], d_all.at[me], in_send.at[peer], in_recv.at[me], peer)

    pltpu.make_async_copy(d_in.at[me], d_all.at[me], in_recv.at[me]).start()

    def start_near(peer):
        pl.when(peer != me)(lambda: moved(peer).start())

    over(own * half, start_near)
    over((1 - own) * half, lambda peer: moved(peer).start())
    sends = ((dq_send, dq_got), (dk_send, dk_got), (dv_send, dv_got))

    def give(index, block):
        source, target = sends[index]

        @pl.when(block == me)
        def _():
            pltpu.make_async_copy(
                source.at[block], target.at[me], out_recv.at[index, me]
            ).start()

        @pl.when(block != me)
        def _():
            send(
                source.at[block], target.at[me],
                out_send.at[index, block], out_recv.at[index, me], block,
            ).start()

    def give_query(i):
        dq_send[i] = (dq_turn[i] * HEAD_DIM**-0.5).T.astype(BF16)
        give(0, i)

    def give_keys(j):
        dk_send[j] = dk_sum[j].astype(BF16)
        dv_send[j] = dv_sum[j].astype(BF16)
        give(1, j)
        give(2, j)

    def tile(i, j, masked):
        if masked:
            allowed = allowed_tile(i, j, tokens, start)
        queries, grads_out, keys, mixed = q_all[i], d_all[i], k_all[j], v_all[j]
        for head in range(heads):
            rows = slice(head * HEAD_DIM, (head + 1) * HEAD_DIM)
            query, grad = own_head(queries, head, width), own_head(grads_out, head, width)
            scores = against(keys, query)
            if masked:
                scores = jnp.where(allowed, scores, NEG)
            weights = jnp.exp(scores - lse_all[i, head])
            dv_sum[j] += dot(weights.astype(BF16), grad)
            slope = against(mixed, grad) - delta[i, head]
            d_scores = (weights * slope).astype(BF16)
            dk_sum[j] += dot(d_scores, query)
            dq_turn[i, rows] += dot(k_turn[j, rows], d_scores)

    def prepare(block):
        arrive(d_all.at[block], in_recv.at[block])
        product = d_all[block].astype(F32).T * o_all[block]
        for head in range(heads):
            rows = slice(head * HEAD_DIM, (head + 1) * HEAD_DIM)
            delta[block, head] = jnp.sum(product[rows], axis=0, keepdims=True)
        k_turn[block] = k_all[block].T
        dq_turn[block] = jnp.zeros(dq_turn.shape[1:], F32)
        dk_sum[block] = jnp.zeros(dk_sum.shape[1:], F32)
        dv_sum[block] = jnp.zeros(dv_sum.shape[1:], F32)

    def tile_row(row, _):
        phase, place_in = row // half, lax.rem(row, half)
        adding.at_row(row, 3 * half)

        @pl.when(row == 0)
        def _():
            lax.fori_loop(0, half, lambda n, _: prepare(own * half + n) or 0, 0)

        @pl.when(row == half)
        def _():
            lax.fori_loop(0, half, lambda n, _: prepare((1 - own) * half + n) or 0, 0)

        by_query = jnp.where(phase == 1, own == 1, own == 0)
        lower = jnp.where(phase == 0, own, 1 - own) * half
        outer = jnp.where(
            phase == 2, jnp.where(by_query, half, 0), lower
        ) + place_in
        first = jnp.where(phase == 2, jnp.where(by_query, 0, half), jnp.where(by_query, lower, outer))
        last = jnp.where(
            phase == 2,
            jnp.where(by_query, half, parts),
            jnp.where(by_query, outer + 1, lower + half),
        )

        def inner_block(inner, _):
            i, j = jnp.where(by_query, outer, inner), jnp.where(by_query, inner, outer)
            masked = (j == 0) | (j == i) | (i == parts - 1)
            pl.when(masked)(lambda: tile(i, j, True))
            pl.when(jnp.logical_not(masked))(lambda: tile(i, j, False))
            return 0

        lax.fori_loop(first, last, inner_block, 0)
        pl.when(by_query)(lambda: give_query(outer))
        pl.when(jnp.logical_not(by_query))(lambda: give_keys(outer))
        return 0

    lax.fori_loop(0, 3 * half, tile_row, 0)
    pl.when(own == 0)(lambda: over(0, give_keys))
    pl.when(own == 1)(lambda: over(half, give_query))
    adding.finish()

    def finish(step, _):
        peer = lax.rem(me + step, parts)
        moved(peer).wait_send()
        for index, (source, target) in enumerate(sends):
            arrive(source.at[peer], out_send.at[index, peer])
            arrive(target.at[peer], out_recv.at[index, peer])
        return 0

    lax.fori_loop(1, parts, finish, 0)
    for index, (_, target) in enumerate(sends):
        arrive(target.at[me], out_recv.at[index, me])


def attend_back(d_att, q, k, v, o, lse, start, grads, pieces):
    parts, tokens, width = q.shape
    heads = width // HEAD_DIM
    place = Place()
    whole = pl.BlockSpec(memory_space=VMEM)
    far = pl.BlockSpec(memory_space=pl.ANY)
    split = jax.ShapeDtypeStruct(q.shape, BF16)
    flops = 10 * parts * parts * tokens * tokens * width // 2
    sum_shapes = [piece.held(place, grads[piece.array].shape[1]) for piece in pieces]
    sum_scratch = GradSums.scratch(place, pieces, grads)
    grads = [placed(place, grad) for grad in grads]
    results = pl.pallas_call(
        functools.partial(backward_kernel, parts, heads, pieces, len(grads)),
        in_specs=[far] + [whole] * 6 + [far] * len(grads),
        out_specs=[far] * 3 + [far] * len(pieces),
        out_shape=[split] * 3 + sum_shapes,
        scratch_shapes=[
            VMEM((parts, tokens, width), BF16),
            VMEM((parts, width, tokens), BF16),
            VMEM((parts, heads, 1, tokens), F32),
            VMEM((parts, width, tokens), F32),
            VMEM((parts, tokens, width), F32),
            VMEM((parts, tokens, width), F32),
            VMEM((parts, tokens, width), BF16),
            VMEM((parts, tokens, width), BF16),
            VMEM((parts, tokens, width), BF16),
            pltpu.SemaphoreType.DMA((parts,)),
            pltpu.SemaphoreType.DMA((parts,)),
            pltpu.SemaphoreType.DMA((3, parts)),
            pltpu.SemaphoreType.DMA((3, parts)),
            *sum_scratch,
        ],
        compiler_params=pltpu.CompilerParams(
            collective_id=2, has_side_effects=True, vmem_limit_bytes=60 * MIB
        ),
        cost_estimate=pl.CostEstimate(
            flops=4 * flops, bytes_accessed=20 * q.size, transcendentals=flops // 640
        ),
        name="attend_back",
    )(d_att, q, k, v, o, lse, start, *grads)
    return results[:3], results[3:]


class Place:
    def __init__(self):
        self.xs = lax.axis_size("dp") // 2
        seq = lax.axis_size("seq")
        self.bs = 2 if seq <= 8 else 4
        self.as_ = seq // self.bs
        dp, rank = lax.axis_index("dp"), lax.axis_index("seq")
        self.x, self.core = dp // 2, lax.rem(dp, 2)
        self.a, self.b = rank // self.bs, lax.rem(rank, self.bs)

    def device(self, x=None, core=None, a=None, b=None):
        x, core = (self.x if x is None else x), (self.core if core is None else core)
        a, b = (self.a if a is None else a), (self.b if b is None else b)
        return (x * 2 + core, a * self.bs + b)

    def peers(self, axis):
        size = {"x": self.xs, "a": self.as_, "b": self.bs}[axis]
        own = getattr(self, axis)
        return [(step - 1, lax.rem(own + step, size)) for step in range(1, size)]

    def greet(self, greeted=0):
        barrier = pltpu.get_barrier_semaphore()
        others = [self.device(core=1 - self.core)]
        for axis in "x" if greeted else "xab":
            others += [self.device(**{axis: index}) for _, index in self.peers(axis)]
        for other in others:
            pl.semaphore_signal(barrier, 1, device_id=other, device_id_type=MESH)
        pl.semaphore_wait(barrier, len(others) + greeted)

    @property
    def inner(self):
        return (self.a == 1) | (self.a == 2)

    @property
    def beside(self):
        return self.a + 1 - 2 * lax.rem(self.a, 2)


def column_pieces(columns, wanted):
    tiles = columns // 128
    wanted = min(wanted, tiles)
    edges = [tiles * n // wanted * 128 for n in range(wanted)] + [columns]
    return [(edges[n], edges[n + 1] - edges[n]) for n in range(wanted)]


def placed(place, value):
    return value.reshape(place.xs, 2, place.as_, place.bs, *value.shape[1:])


def remote(source, target, send_sem, recv_sem, device):
    return pltpu.make_async_remote_copy(
        src_ref=source,
        dst_ref=target,
        send_sem=send_sem,
        recv_sem=recv_sem,
        device_id=device,
        device_id_type=MESH,
    )


def flat(ref):
    rows, columns = ref.shape[-2:]
    return ref.reshape(ref.size // (rows * columns), rows, columns)


class Relay:
    def __init__(self, place, source, target, sems):
        self.p, self.source, self.target, self.sems = place, source, target, sems
        assert place.as_ == 4

    def near(self):
        p = self.p
        return remote(
            self.source, self.target.at[p.a],
            self.sems.at[0, 0], self.sems.at[1, 0], p.device(a=p.beside),
        )

    def middle(self):
        p = self.p
        held = self.target.at[pl.ds(p.a // 2 * 2, 2)]
        return remote(
            held, held, self.sems.at[0, 1], self.sems.at[1, 1], p.device(a=3 - p.a)
        )

    def outward(self):
        p = self.p
        held = self.target.at[pl.ds((1 - p.a // 2) * 2, 2)]
        return remote(
            held, held, self.sems.at[0, 2], self.sems.at[1, 1], p.device(a=p.beside)
        )

    def local(self):
        return pltpu.make_async_copy(self.source, self.target.at[self.p.a], self.sems.at[1, 2])

    def step(self, number):
        if number == 0:
            self.local().start()
            self.near().start()
        elif number == 1:
            self.local().wait()
            self.near().wait_recv()
            pl.when(self.p.inner)(lambda: self.middle().start())
        elif number == 2:

            @pl.when(self.p.inner)
            def _():
                self.middle().wait_recv()
                self.outward().start()
        else:

            @pl.when(jnp.logical_not(self.p.inner))
            def _():
                self.middle().wait_recv()

            @pl.when(self.p.inner)
            def _():
                self.middle().wait_send()
                self.outward().wait_send()

            self.near().wait_send()


class Direct:
    def __init__(self, place, source, target, sems):
        self.p, self.source, self.target, self.sems = place, source, target, sems

    def copies(self):
        p = self.p
        return [
            remote(
                self.source, self.target.at[p.a],
                self.sems.at[0, s], self.sems.at[1, s], p.device(a=index),
            )
            for s, index in p.peers("a")
        ]

    def local(self):
        return pltpu.make_async_copy(self.source, self.target.at[self.p.a], self.sems.at[0, 3])

    def step(self, number):
        if number == 0:
            self.local().start()
            for copy in self.copies():
                copy.start()
        elif number == 3:
            self.local().wait()
            for copy in self.copies():
                copy.wait()


class Piece:
    def __init__(self, array, start, size, order, deep):
        self.array, self.start, self.size, self.order, self.deep = array, start, size, order, deep

    @staticmethod
    def all(shapes):
        pieces = []
        for array, kinds in enumerate(
            ([("bx", 0)], [("bx", 1)] * 2, [("xb", 1), ("bx", 1)], [("bx", 0)] * 2)
        ):
            for (start, size), kind in zip(column_pieces(shapes[array][1], len(kinds)), kinds):
                pieces.append(Piece(array, start, size, *kind))
        return pieces

    def held(self, place, rows):
        lead = {"": (), "b": (place.bs,), "x": (place.xs,)}[self.order[0] if self.deep else ""]
        lead = (*lead, place.as_) if self.order[0] == "x" else (place.as_, *lead)
        return jax.ShapeDtypeStruct((*lead, rows, self.size), BF16)

    def along_a(self, place, held):
        if not self.deep:
            return held
        return held.at[place.x] if self.order[0] == "x" else held.at[:, place.b]

    def columns(self, ref):
        return ref.at[(slice(None),) * (len(ref.shape) - 1) + (pl.ds(self.start, self.size),)]


class Spread:
    def __init__(self, place, views, order, sems, source=None, first=0):
        self.place, self.views, self.order, self.sems = place, views, order, sems
        self.source, self.first = source, first

    @staticmethod
    def views_of(place, full, order):
        p = place
        middle = full.at[:, p.core, :, p.b] if order == "xb" else full.at[p.x, p.core]
        return full.at[p.x, p.core, :, p.b], middle, full.at[:, p.core]

    def copies(self, number):
        p, view = self.place, self.views[number]
        source = self.source if self.source is not None and number == self.first else view
        base = sum([len(p.peers(axis)) for axis in self.order][:number])
        if number == 2:
            devices = [(0, p.device(core=1 - p.core))]
        else:
            axis = self.order[number]
            devices = [(s, p.device(**{axis: index})) for s, index in p.peers(axis)]
        return [
            remote(source, view, self.sems.at[0, base + s], self.sems.at[1, base + s], device)
            for s, device in devices
        ]

    def local(self):
        return pltpu.make_async_copy(self.source, self.views[self.first], self.sems.at[2, 0])

    def start(self, number):
        if self.source is not None and number == self.first:
            self.local().start()
        for copy in self.copies(number):
            copy.start()

    def finish(self, number):
        if self.source is not None and number == self.first:
            self.local().wait()
        for copy in self.copies(number):
            copy.wait_recv()
            copy.wait_send()

    def then(self, number):
        self.finish(number)
        if number < 2:
            self.start(number + 1)


def spread_semaphores(place):
    return pltpu.SemaphoreType.DMA((3, place.xs + place.bs - 1))


RELAY_SEMAPHORES = (2, 4)


class InRows:
    def at_row(self, row, count):
        for at in sorted({at for at, _ in self.actions() if at < 12}):

            @pl.when(row == at * count // 12)
            def _():
                for own_row, action in self.actions():
                    if own_row == at:
                        action()

    def finish(self):
        for at, action in self.actions():
            if at >= 12:
                action()


class WeightSpread(InRows):
    def __init__(self, place, pieces, sources, fulls, sems):
        self.units = []
        for piece, source, own_sems in zip(pieces, sources, sems):
            full = piece.columns(fulls[piece.array])
            views = Spread.views_of(place, full, piece.order)
            self.units.append(Spread(place, views, piece.order, own_sems, source, piece.deep))

    def actions(self):
        out, gate0, gate1, up0, up1, down0, down1 = self.units
        start = lambda unit: functools.partial(unit.start, unit.first)
        then = lambda unit, number: functools.partial(unit.then, number)
        done = [(0, start(unit)) for unit in (gate0, down0, gate1, down1, up1, out, up0)]
        done += [(4, then(down0, 0)), (5, then(down1, 0)), (6, then(out, 0))]
        done += [(7, then(gate0, 1)), (8, then(gate1, 1)), (9, then(up0, 1)), (10, then(up1, 1))]
        done += [(12, then(unit, 1)) for unit in (down0, down1, out)]
        done += [(12, then(unit, 2)) for unit in (gate0, gate1, up0, up1, down0, down1, out)]
        return done


class TotalSum:
    def __init__(self, place, mine, got, sems):
        self.place, self.mine, self.got, self.sems = place, mine, got, sems

    def slots(self, number):
        p = self.place
        devices = [[p.device(core=1 - p.core)]]
        devices += [[p.device(**{axis: index}) for _, index in p.peers(axis)] for axis in "xba"]
        return sum(len(some) for some in devices[:number]), devices[number]

    def copies(self, number):
        base, devices = self.slots(number)
        return [
            remote(
                self.mine, self.got.at[base + n],
                self.sems.at[0, base + n], self.sems.at[1, base + n], device,
            )
            for n, device in enumerate(devices)
        ]

    def start(self, number):
        for copy in self.copies(number):
            copy.start()

    def then(self, number):
        for copy in self.copies(number):
            copy.wait()
        base, devices = self.slots(number)
        for slot in range(len(devices)):
            self.mine[...] += self.got[base + slot]
        if number < 3:
            self.start(number + 1)


def opening_kernel(
    plan, pieces, parted,
    x, first, cosine, sine, gains, w_query, w_key, w_value, *refs,
):
    shares, refs = refs[:parted], refs[parted:]
    q_out, k_out, v_out, hidden, gains_total, *fulls = refs[:8]
    helds, refs = refs[8 : 8 + len(pieces)], refs[8 + len(pieces) :]
    got_gains, gain_sems, relay_sems, *sems = refs
    place = Place()
    parts, tokens, width = q_out.shape
    dim = parts * width
    place.greet()
    gains_total[...] = gains[...]
    total = TotalSum(place, gains_total, got_gains, gain_sems)
    units, relays = [], []
    sources = (w_query, w_key, w_value)
    for number, (array, start, size, order) in enumerate(plan):
        views = Spread.views_of(place, fulls[array].at[:, :, :, :, :, pl.ds(start, size)], order)
        relays.append(
            Direct(place, sources[array].at[:, pl.ds(start, size)], views[0], relay_sems.at[number])
        )
        units.append(Spread(place, views, order, sems[number]))
    deep, flat_relays, deep_relays = [], [], []
    for number, (piece, held) in enumerate(zip(pieces, helds)):
        view = piece.along_a(place, held)
        index = len(plan) + number
        relay = Relay(place, piece.columns(shares[piece.array]), view, relay_sems.at[index])
        (deep_relays if piece.deep else flat_relays).append(relay)
        if piece.deep:
            deep.append(Spread(place, [view], piece.order, sems[index]))

    def step(group, number):
        for relay in group:
            relay.step(number)

    def then(some, number):
        for unit in some:
            unit.then(number)

    def weight(array, start, size):
        full = fulls[array]
        rows, columns = full.shape[-2:]
        fold = dim // columns
        value = full[:, :, :, :, :, start % columns : start % columns + size]
        if fold > 1:
            share = rows // fold
            part = start // columns * share
            value = value.astype(F32)[:, :, :, :, part : part + share]
        return value.reshape(dim, size).astype(BF16)

    def project(array):
        for start in range(0, dim, 256):
            raw = dot(hidden[...], weight(array, start, 256))
            if array == 2:
                raw = 0.5 * raw + 0.5 * first[:, start : start + 256].astype(F32)
            for begin in range(0, 256, 128):
                value = raw[:, begin : begin + 128]
                if array < 2:
                    value = turned(value, cosine[...], sine[...])
                if array == 0:
                    value = value * HEAD_DIM**-0.5
                for lane in range(0, 128, width):
                    out = (q_out, k_out, v_out)[array]
                    out[(start + begin + lane) // width] = value[:, lane : lane + width].astype(BF16)

    half = len(units) // 2
    line = deep_relays + flat_relays

    def tick(number):
        for back in (3, 2, 1, 0):
            index = number - back
            if 0 <= index < len(line):
                line[index].step(back)
                if back == 3 and index < len(deep):
                    deep[index].start(0)

    step(relays, 0)
    total.start(0)
    step(relays, 1)
    tick(0)
    step(relays, 2)
    total.then(0)
    for relay, unit in zip(relays, units):
        relay.step(3)
        unit.start(0)
    tick(1)
    total.then(1)
    then(units[:half], 0)
    tick(2)
    then(units[half:], 0)
    total.then(2)
    tick(3)
    total.then(3)
    values = x[...].astype(F32)
    scale = lax.rsqrt(jnp.mean(values * values, axis=-1, keepdims=True) + EPS)
    hidden[...] = (values * scale * gains_total[0:1]).astype(BF16)
    tick(4)
    then(units[:half], 1)
    tick(5)
    then(units[half:], 1)
    for array in range(3):
        then([unit for unit, piece in zip(units, plan) if piece[0] == array], 2)
        project(array)
        tick(6 + array)
    for number in range(9, len(line) + 3):
        tick(number)
    for unit in deep:
        unit.finish(0)


def opening(x, first, cosine, sine, gains, weights, parted, pieces, parts, collective_id):
    place = Place()
    xs, as_, bs = place.xs, place.as_, place.bs
    tokens, dim = x.shape
    plan = []
    for number, array in enumerate(weights):
        for start, size in column_pieces(array.shape[1], 2):
            plan.append((number, start, size, "xb" if len(plan) % 2 == 1 else "bx"))
    shape = jax.ShapeDtypeStruct
    near = [shape((parts, tokens, dim // parts), BF16)] * 3
    near += [shape((tokens, dim), BF16), shape(gains.shape, F32)]
    near += [shape((xs, 2, as_, bs, *array.shape), array.dtype) for array in weights]
    held = [piece.held(place, parted[piece.array].shape[0]) for piece in pieces]
    far, whole = pl.BlockSpec(memory_space=pl.ANY), pl.BlockSpec(memory_space=VMEM)
    count = len(plan) + len(pieces)
    peers = 1 + (xs - 1) + (bs - 1) + (as_ - 1)
    results = pl.pallas_call(
        functools.partial(opening_kernel, plan, pieces, len(parted)),
        in_specs=[whole] * 5 + [far] * (3 + len(parted)),
        out_specs=[whole] * (len(near) + len(held)),
        out_shape=near + held,
        scratch_shapes=[
            VMEM((peers, *gains.shape), F32),
            pltpu.SemaphoreType.DMA((2, peers)),
            pltpu.SemaphoreType.DMA((count, *RELAY_SEMAPHORES)),
            *[spread_semaphores(place)] * count,
        ],
        compiler_params=pltpu.CompilerParams(
            collective_id=collective_id, has_side_effects=True, vmem_limit_bytes=48 * MIB
        ),
        cost_estimate=pl.CostEstimate(
            flops=6 * tokens * dim * dim, bytes_accessed=20 * dim * dim, transcendentals=0
        ),
        name="opening",
    )(x, first, cosine, sine, gains, *weights, *parted)
    devices = xs * 2 * as_ * bs
    fulls = [value.reshape(devices, *value.shape[4:]) for value in results[5:8]]
    return results[:4], results[4], fulls, results[8:]


def add_up(mine, others):
    lead = mine.shape[:-2]

    def at(ref, step):
        index = []
        for size in reversed(lead):
            index.insert(0, lax.rem(step, size))
            step = step // size
        return ref.at[tuple(index)]

    def body(step, _):
        total = at(mine, step)[...].astype(F32)
        for other in others:
            total += at(other, step)[...].astype(F32)
        at(mine, step)[...] = total.astype(mine.dtype)
        return 0

    count = 1
    for size in lead:
        count *= size
    lax.fori_loop(0, count, body, 0)


class RelaySum:
    def __init__(self, place, own, inward, middle, last, sems, result):
        self.p, self.own, self.sems, self.result = place, own, sems, result
        self.inward, self.middle, self.last = inward, middle, last
        assert place.as_ == 4

    def move(self, number):
        p = self.p
        far = self.own.at[pl.ds((1 - p.a // 2) * 2, 2)]
        if number == 0:
            source, target, device = far, self.inward, p.beside
        elif number == 1:
            source, target, device = far, self.middle, 3 - p.a
        else:
            source, target, device = self.own.at[p.beside], self.last, p.beside
        return remote(
            source, target, self.sems.at[0, number], self.sems.at[1, number], p.device(a=device)
        )

    def step(self, number):
        p, inner = self.p, self.p.inner
        outer = jnp.logical_not(inner)
        if number == 0:
            pl.when(outer)(lambda: self.move(0).start())
            pl.when(outer)(lambda: self.move(2).start())
        elif number == 1:

            @pl.when(inner)
            def _():
                self.move(0).wait_recv()
                add_up(self.own.at[pl.ds((1 - p.a // 2) * 2, 2)], [self.inward])
                self.move(1).start()
        elif number == 2:

            @pl.when(inner)
            def _():
                self.move(1).wait_recv()
                add_up(self.own.at[pl.ds(p.a // 2 * 2, 2)], [self.middle])
                self.move(2).start()
        else:
            self.move(2).wait_recv()
            self.result[...] = self.own[p.a].astype(F32) + self.last[...].astype(F32)
            pl.when(outer)(lambda: self.move(0).wait_send())
            pl.when(inner)(lambda: self.move(1).wait_send())
            self.move(2).wait_send()

    @staticmethod
    def scratch(rows, columns, dtype):
        return [
            VMEM((2, rows, columns), dtype),
            VMEM((2, rows, columns), dtype),
            VMEM((rows, columns), dtype),
            pltpu.SemaphoreType.DMA((2, 3)),
        ]


class DirectSum:
    def __init__(self, place, own, got, sems, result):
        self.p, self.own, self.got, self.sems, self.result = place, own, got, sems, result

    def copies(self):
        p = self.p
        return [
            remote(
                self.own.at[index], self.got.at[s],
                self.sems.at[0, s], self.sems.at[1, s], p.device(a=index),
            )
            for s, index in p.peers("a")
        ]

    def step(self, number):
        if number == 0:
            for copy in self.copies():
                copy.start()
        elif number == 3:
            total = self.own[self.p.a].astype(F32)
            for slot, copy in enumerate(self.copies()):
                copy.wait()
                total += self.got[slot].astype(F32)
            self.result[...] = total

    @staticmethod
    def scratch(place, rows, columns, dtype):
        return [
            VMEM((place.as_ - 1, rows, columns), dtype),
            pltpu.SemaphoreType.DMA((2, place.as_ - 1)),
        ]


class Sum:
    def __init__(self, place, source, order, buffers):
        self.place, self.order, self.source = place, order, source
        self.own, self.got0, self.got1, self.got2, self.sems = buffers
        self.copied = self.own is not None
        if not self.copied:
            self.own = source.at[:, place.core]

    @property
    def held(self):
        return self.own.at[self.place.x, :, self.place.b]

    @property
    def part(self):
        p = self.place
        return self.own.at[p.x] if self.order[0] == "x" else self.own.at[:, :, p.b]

    def moves(self, number):
        p = self.place
        if number == 0:
            return [(self.source.at[:, 1 - p.core], self.got0, 0, p.device(core=1 - p.core))]
        axis = self.order[number - 1]
        got = self.got1 if number == 1 else self.got2
        moves = []
        for slot, index in p.peers(axis):
            if axis == "x":
                piece = self.own.at[index] if number == 1 else self.own.at[index, :, p.b]
            else:
                piece = self.own.at[:, :, index] if number == 1 else self.own.at[p.x, :, index]
            moves.append((piece, got.at[slot], slot, p.device(**{axis: index})))
        return moves

    def copies(self, number):
        base = sum(([1] + [len(self.place.peers(axis)) for axis in self.order])[:number])
        return [
            remote(source, target, self.sems.at[0, base + s], self.sems.at[1, base + s], device)
            for source, target, s, device in self.moves(number)
        ]

    def local(self):
        return pltpu.make_async_copy(
            self.source.at[:, self.place.core], self.own, self.sems.at[2, 0]
        )

    def start(self, number):
        for copy in self.copies(number):
            copy.start()
        if number == 0 and self.copied:
            self.local().start()

    def finish(self, number):
        p = self.place
        if number == 0 and self.copied:
            self.local().wait()
        for copy in self.copies(number):
            copy.wait_recv()
            copy.wait_send()
        if number == 0:
            add_up(self.own, [self.got0])
        else:
            mine = self.held if number == 2 else self.part
            got = self.got1 if number == 1 else self.got2
            add_up(mine, [got.at[slot] for slot in range(len(p.peers(self.order[number - 1])))])

    @staticmethod
    def scratch(place, rows, size, order, dtype, copied=True):
        xs, as_, bs = place.xs, place.as_, place.bs
        shapes = {
            "x": ((xs - 1, as_, bs, rows, size), (xs - 1, as_, rows, size)),
            "b": ((bs - 1, xs, as_, rows, size), (bs - 1, as_, rows, size)),
        }
        return [VMEM((xs, as_, bs, rows, size), dtype)] * copied + [
            VMEM((xs, as_, bs, rows, size), dtype),
            VMEM(shapes[order[0]][0], dtype),
            VMEM(shapes[order[1]][1], dtype),
            pltpu.SemaphoreType.DMA((3, xs + bs - 1)),
        ]


class GradSums(InRows):
    def __init__(self, place, pieces, grads, results, buffers):
        self.units, self.outs = [], []
        for piece, result in zip(pieces, results):
            source = piece.columns(grads[piece.array])
            unit, buffers = Sum(place, source, piece.order[::-1], buffers[:5]), buffers[5:]
            self.units.append(unit)
            self.outs.append((unit.part if piece.deep else unit.held, result))

    @staticmethod
    def scratch(place, pieces, grads):
        return [
            item
            for piece in pieces
            for item in Sum.scratch(
                place, grads[piece.array].shape[1], piece.size, piece.order[::-1], BF16
            )
        ]

    def actions(self):
        out, gate0, gate1, up0, up1, down0, down1 = self.units

        def copy_of(unit):
            source, result = self.outs[self.units.index(unit)]
            return pltpu.make_async_copy(source, result, unit.sems.at[2, 1])

        def then(unit, number):
            def action():
                unit.finish(number)
                if number < (1 if unit in (gate0, gate1, up0, up1) else 2):
                    unit.start(number + 1)
                else:
                    copy_of(unit).start()

            return action

        order = (down0, down1, out, up0, gate0, gate1, up1)
        done = [(0, functools.partial(unit.start, 0)) for unit in order]
        done += [(row, then(unit, 0)) for row, unit in zip((0, 1, 1, 2, 2, 3, 3), order)]
        done += [(6, then(down0, 1)), (7, then(down1, 1)), (8, then(out, 1)), (9, then(up0, 1))]
        done += [(10, then(gate0, 1)), (11, then(down0, 2))]
        done += [(12, then(down1, 2)), (12, then(out, 2)), (12, then(gate1, 1)), (12, then(up1, 1))]
        done += [(12, lambda unit=unit: copy_of(unit).wait()) for unit in order]
        return done


class HeldSum:
    def __init__(self, place, piece, source, buffers, result):
        self.place, self.piece, self.source = place, piece, source
        self.own, self.got, self.sems, *relay = buffers
        self.relay = RelaySum(place, self.own, *relay, result)
        self.axis = piece.order[0]

    def copies(self):
        if not self.piece.deep:
            return []
        p = self.place
        at = lambda index: self.source.at[index] if self.axis == "x" else self.source.at[:, index]
        return [
            remote(
                at(index), self.got.at[s], self.sems.at[0, s], self.sems.at[1, s],
                p.device(**{self.axis: index}),
            )
            for s, index in p.peers(self.axis)
        ]

    def local(self):
        mine = self.piece.along_a(self.place, self.source)
        return pltpu.make_async_copy(mine, self.own, self.sems.at[2, 0])

    def start(self):
        self.local().start()
        for copy in self.copies():
            copy.start()

    def finish(self):
        self.local().wait()
        copies = self.copies()
        for copy in copies:
            copy.wait_recv()
            copy.wait_send()
        if len(copies):
            add_up(self.own, [self.got.at[slot] for slot in range(len(copies))])
        self.relay.step(0)

    @staticmethod
    def scratch(place, piece, rows):
        count = len(place.peers(piece.order[0])) if piece.deep else 1
        got = (count, place.as_, rows, piece.size) if piece.deep else (1, 1, 16, 128)
        return [
            VMEM((place.as_, rows, piece.size), BF16),
            VMEM(got, BF16),
            pltpu.SemaphoreType.DMA((3, count)),
            *RelaySum.scratch(rows, piece.size, BF16),
        ]


def closing_kernel(
    plan, pieces, rows, fold, parted,
    dq, dk, dv, w_query, w_key, w_value, hidden, x, d_middle, gains, cosine, sine, gain, *refs,
):
    helds, refs = refs[: len(pieces)], refs[len(pieces) :]
    grad_first, grad_x, gains_total, *refs = refs
    results, buffers = refs[: 3 + parted], refs[3 + parted :]
    slopes, weights, hidden_in, x_in, middle, hidden_turn, d_hidden, got_gains, gain_sems = buffers[:9]
    loads, buffers = buffers[9], buffers[10:]
    place = Place()
    parts, tokens, width = dq.shape
    dim = parts * width
    devices = dim // rows
    place.greet()
    copies = [
        pltpu.make_async_copy(source, target, loads.at[n])
        for n, (source, target) in enumerate(
            (
                (hidden, hidden_in), (dq, slopes.at[0]), (w_query, weights.at[0]),
                (dk, slopes.at[1]), (w_key, weights.at[1]), (dv, slopes.at[2]),
                (w_value, weights.at[2]), (x, x_in), (d_middle, middle),
            )
        )
    ]
    for copy in copies:
        copy.start()
    units, relays, grads, rest = [], [], [], []
    for array, start, size, order in plan:
        source = buffers[0]
        unit = Sum(place, source, order, (None, *buffers[1:5]))
        result = results[array].at[:, pl.ds(start, size)]
        relays.append(DirectSum(place, unit.held, *buffers[5:7], result))
        units.append(unit)
        grads.append(source)
        buffers = buffers[7:]
    for piece, held in zip(pieces, helds):
        result = piece.columns(results[3 + piece.array])
        rest.append(HeldSum(place, piece, held, buffers[:7], result))
        buffers = buffers[7:]
    deep = [unit for unit in rest if unit.piece.deep]
    simple = [unit for unit in rest if not unit.piece.deep]
    total = TotalSum(place, gains_total, got_gains, gain_sems)
    for unit in simple + deep:
        unit.start()

    def low(array, first, size):
        done = []
        for start in range(first, first + size, 128):
            picks = range(start // width, (start + 128) // width)
            value = jnp.concatenate([slopes[array, n] for n in picks], axis=1).astype(F32)
            if array < 2:
                value = turned(value, cosine[...], -sine[...])
            else:
                value = 0.5 * value
                grad_first[:, start : start + 128] = value.astype(BF16)
            done.append(value.astype(BF16))
        return jnp.concatenate(done, axis=1)

    def compute(index):
        array, start, size, _ = plan[index]
        blocks = []
        for part in range(fold):
            first = part * (dim // fold) + start
            slope = low(array, first, size)
            blocks.append(dot(hidden_turn[...], slope).reshape(devices, rows, size))
            d_hidden[...] += against(slope, weights[array, :, first : first + size])
        block = (blocks[0] if fold == 1 else jnp.concatenate(blocks, axis=1)).astype(BF16)
        grads[index][...] = block.reshape(grads[index].shape)

    def step(group, number):
        for unit in group:
            unit.relay.step(number)

    def then(index, number):
        units[index].finish(number)
        if number < 2:
            units[index].start(number + 1)
        else:
            relays[index].step(0)

    copies[0].wait()
    hidden_turn[...] = hidden_in[...].T
    d_hidden[...] = jnp.zeros_like(d_hidden)
    count = len(units)
    for index in range(count):
        array = plan[index][0]
        if index == 0 or plan[index - 1][0] != array:
            copies[1 + 2 * array].wait()
            copies[2 + 2 * array].wait()
        compute(index)
        units[index].start(0)
        if index == 0:
            for unit in simple:
                unit.finish()
        else:
            then(index - 1, 0)
        if index == 2:
            step(simple, 1)
        if index == 4:
            step(simple, 2)
    copies[7].wait()
    copies[8].wait()
    grad_values, grad_gain = norm_back(d_hidden[...], x_in[...].astype(F32), gain[...])
    grad_x[...] = grad_values + middle[...]
    gains_total[...] = gains[...]
    gains_total[0:1] = grad_gain[None]
    total.start(0)
    then(count - 1, 0)
    for unit in deep:
        unit.finish()
    step(simple, 3)
    for index in range(count // 2):
        then(index, 1)
    step(deep, 1)
    total.then(0)
    for index in range(count // 2, count):
        then(index, 1)
    step(deep, 2)
    total.then(1)
    for index in range(count // 2):
        then(index, 2)
    total.then(2)
    for relay in relays[: count // 2]:
        relay.step(1)
    for index in range(count // 2, count):
        then(index, 2)
    step(deep, 3)
    for relay in relays[count // 2 :]:
        relay.step(1)
    total.then(3)
    for relay in relays:
        relay.step(2)
    for relay in relays:
        relay.step(3)


def closing(
    slopes, weights, hidden, x, d_middle, grad_gain, cosine, sine, gain, rows, helds, pieces,
    shapes, collective_id,
):
    place = Place()
    parts, tokens, width = slopes[0].shape
    dim = parts * width
    fold = 1
    while rows * fold % 16:
        fold *= 2
    plan, scratch = [], []
    for array in range(3):
        for start, size in column_pieces(dim // fold, 2):
            order = "bx" if len(plan) % 2 == 1 else "xb"
            plan.append((array, start, size, order))
            lead = (place.xs, 2, place.as_, place.bs)
            scratch.append(VMEM((*lead, rows * fold, size), BF16))
            scratch += Sum.scratch(place, rows * fold, size, order, BF16, False)
            scratch += DirectSum.scratch(place, rows * fold, size, BF16)
    for piece in pieces:
        scratch += HeldSum.scratch(place, piece, shapes[piece.array][0])
    peers = 1 + (place.xs - 1) + (place.bs - 1) + (place.as_ - 1)
    gains = jnp.pad(grad_gain[None], ((1, 6), (0, 0)))
    far, whole = pl.BlockSpec(memory_space=pl.ANY), pl.BlockSpec(memory_space=VMEM)
    shape = jax.ShapeDtypeStruct
    out = [shape((tokens, dim), BF16), shape((tokens, dim), F32), shape((8, dim), F32)]
    out += [shape((rows * fold, dim // fold), F32)] * 3
    out += [shape(each, F32) for each in shapes]
    return pl.pallas_call(
        functools.partial(closing_kernel, plan, pieces, rows, fold, len(shapes)),
        in_specs=[far] * 9 + [whole] * 4 + [far] * len(helds),
        out_specs=[whole] * len(out),
        out_shape=out,
        scratch_shapes=[
            VMEM((3, parts, tokens, width), BF16),
            VMEM((3, dim, dim), BF16),
            VMEM((tokens, dim), BF16),
            VMEM((tokens, dim), BF16),
            VMEM((tokens, dim), F32),
            VMEM((dim, tokens), BF16),
            VMEM((tokens, dim), F32),
            VMEM((peers, 8, dim), F32),
            pltpu.SemaphoreType.DMA((2, peers)),
            pltpu.SemaphoreType.DMA((9,)),
            *scratch,
        ],
        compiler_params=pltpu.CompilerParams(
            collective_id=collective_id, has_side_effects=True, vmem_limit_bytes=60 * MIB
        ),
        cost_estimate=pl.CostEstimate(
            flops=12 * tokens * dim * dim, bytes_accessed=20 * dim * dim, transcendentals=0
        ),
        name="closing",
    )(*slopes, *weights, hidden, x, d_middle, gains, cosine, sine, gain, *helds)


def stacked(value, devices):
    rows, columns = value.shape[0] // devices, value.shape[1]
    fold = 1
    while rows * fold % 16:
        fold *= 2
    value = value.reshape(devices, rows, fold, columns // fold)
    return value.transpose(0, 2, 1, 3).reshape(devices, rows * fold, columns // fold)


def unstacked(value, rows):
    devices, high, columns = value.shape
    value = value.reshape(devices, high // rows, rows, columns).transpose(0, 2, 1, 3)
    return value.reshape(devices * rows, high // rows * columns)


def settle_kernel(share, padded, first, grad_x, gate, up, down, *refs):
    others, (first_out, x_out, gate_out, up_out, down_out, *others_out) = refs[:4], refs[4:]
    first_out[...] = first[...].astype(F32)
    x_out[...] = grad_x[...]

    @pl.when(pl.program_id(0) == 0)
    def _():
        for source, target in ((gate, gate_out), (up, up_out)):
            count = source.shape[1] // padded
            target[...] = jnp.concatenate(
                [source[:, n * padded : n * padded + share] for n in range(count)], axis=1
            )
        down_out[...] = down[:share]
        for source, target in zip(others, others_out):
            target[...] = source[...]


def settle(first, grad_x, gate, up, down, others, share):
    tokens, dim = grad_x.shape
    padded = down.shape[0]
    units = gate.shape[1] // padded * share
    block = pl.BlockSpec((tokens // 4, dim), lambda g: (g, 0))
    whole = lambda value: pl.BlockSpec(value.shape, lambda g: (0,) * len(value.shape))
    shape = lambda *dims: jax.ShapeDtypeStruct(dims, F32)
    outs = [shape(gate.shape[0], units)] * 2 + [shape(share, dim)]
    outs += [shape(*value.shape) for value in others]
    return pl.pallas_call(
        functools.partial(settle_kernel, share, padded),
        grid=(4,),
        in_specs=[block, block] + [whole(value) for value in (gate, up, down, *others)],
        out_specs=[block, block] + [whole(value) for value in outs],
        out_shape=[shape(tokens, dim)] * 2 + outs,
        compiler_params=pltpu.CompilerParams(vmem_limit_bytes=62 * MIB),
        name="settle",
    )(first, grad_x, gate, up, down, *others)


def middle_kernel(
    steps, x, att, dy, w_out, gain, w_gate, w_up, w_down,
    out, d_middle, d_att, g_out, g_gate, g_up, g_down, g_gain,
    attended, middle, hidden, hidden_turn, result, d_hidden,
):
    step = pl.program_id(0)
    parts, _, width = att.shape

    @pl.when(step == 0)
    def _():
        for part in range(parts):
            attended[:, part * width : (part + 1) * width] = att[part]
        total = x[...].astype(F32) + dot(attended[...], w_out[...])
        scale = lax.rsqrt(jnp.mean(total * total, axis=-1, keepdims=True) + EPS)
        normed = (total * scale * gain[...]).astype(BF16)
        middle[...] = total
        result[...] = total
        hidden[...] = normed
        hidden_turn[...] = normed.T
        d_hidden[...] = jnp.zeros_like(d_hidden)

    grad = dy[...]
    gate = dot(hidden[...], w_gate[...])
    up = dot(hidden[...], w_up[...])
    d_inner = against(grad, w_down[...])
    sigma = jax.nn.sigmoid(gate)
    silu = gate * sigma
    inner = (silu * up).astype(BF16)
    d_gate = (d_inner * up * sigma * (1.0 + gate * (1.0 - sigma))).astype(BF16)
    d_up = (d_inner * silu).astype(BF16)
    result[...] += dot(inner, w_down[...])
    g_down[...] = across(inner, grad).astype(BF16)
    g_gate[...] = dot(hidden_turn[...], d_gate).astype(BF16)
    g_up[...] = dot(hidden_turn[...], d_up).astype(BF16)
    d_hidden[...] += against(d_gate, w_gate[...]) + against(d_up, w_up[...])

    @pl.when(step == steps - 1)
    def _():
        out[...] = result[...].astype(BF16)
        grad_values, grad_gain = norm_back(d_hidden[...], middle[...], gain[...])
        total = grad_values + dy[...].astype(F32)
        d_middle[...] = total
        g_gain[...] = grad_gain[None]
        d_branch = total.astype(BF16)
        g_out[...] = across(attended[...], d_branch).astype(BF16)
        back = against(d_branch, w_out[...]).astype(BF16)
        for part in range(parts):
            d_att[part] = back[:, part * width : (part + 1) * width]


def between(x, att, dy, w_out, gain, w_gate, w_up, w_down):
    tokens, dim = x.shape
    units = w_gate.shape[1]
    chunk = 512 if units % 512 == 0 else 128
    whole = lambda value: pl.BlockSpec(value.shape, lambda g: (0,) * len(value.shape))
    wide = pl.BlockSpec((dim, chunk), lambda g: (0, g))
    tall = pl.BlockSpec((chunk, dim), lambda g: (g, 0))
    shape = jax.ShapeDtypeStruct
    outs = [
        shape((tokens, dim), BF16),
        shape((tokens, dim), F32),
        shape(att.shape, BF16),
        shape(w_out.shape, BF16),
        shape(w_gate.shape, BF16),
        shape(w_up.shape, BF16),
        shape(w_down.shape, BF16),
        shape((1, dim), F32),
    ]
    return pl.pallas_call(
        functools.partial(middle_kernel, units // chunk),
        grid=(units // chunk,),
        in_specs=[whole(v) for v in (x, att, dy, w_out, gain)] + [wide, wide, tall],
        out_specs=[whole(v) for v in outs[:4]] + [wide, wide, tall, whole(outs[7])],
        out_shape=outs,
        scratch_shapes=[
            VMEM((tokens, dim), BF16),
            VMEM((tokens, dim), F32),
            VMEM((tokens, dim), BF16),
            VMEM((dim, tokens), BF16),
            VMEM((tokens, dim), F32),
            VMEM((tokens, dim), F32),
        ],
        compiler_params=pltpu.CompilerParams(vmem_limit_bytes=62 * MIB),
        cost_estimate=pl.CostEstimate(
            flops=18 * tokens * dim * units, bytes_accessed=12 * dim * units, transcendentals=0
        ),
        name="between",
    )(x, att, dy, w_out, gain, w_gate, w_up, w_down)


def shards(
    inputs, first_values, lengths, w_query, w_key, w_value, w_out, gain_attn,
    w_gate, w_up, w_down, gain_mlp, cotangent,
):
    row_count, tokens, width = inputs.shape
    assert row_count == 1
    parts = lax.axis_size("seq")
    rank = lax.axis_index("seq")
    devices = lax.axis_size("dp") * parts
    rows, down_rows = w_query.shape[0], w_down.shape[0]
    multiple = 16 if down_rows >= 64 else 8
    down_padded = -(-down_rows // multiple) * multiple

    def spaced(value):
        value = value.reshape(rows, devices, down_rows)
        value = jnp.pad(value, ((0, 0), (0, 0), (0, down_padded - down_rows)))
        return value.reshape(rows, devices * down_padded)

    index = lax.axis_index("dp") * parts + rank
    gains = jnp.pad(jnp.stack([gain_attn, gain_mlp]).astype(F32), ((0, 6), (0, width - rows)))
    gains = jnp.roll(gains, index * rows, axis=1)
    wide = lambda value: stacked(value, 1)[0]
    padded_down = jnp.pad(w_down, ((0, down_padded - down_rows), (0, 0)))
    parted = [wide(w_out), wide(spaced(w_gate)), wide(spaced(w_up)), wide(padded_down)]
    shapes = [value.shape for value in parted]
    pieces = Piece.all(shapes)
    upto = jnp.arange(lengths.shape[1])
    ends = jnp.sum(jnp.where(upto[:, None] >= upto[None, :], lengths, 0), axis=1)
    begins = ends - lengths[0]
    time = jnp.arange(tokens * parts, dtype=jnp.int32)
    inside = (time[:, None] >= begins[None, :]) & (time[:, None] < ends[None, :])
    start_all = jnp.sum(jnp.where(inside, begins[None, :], 0), axis=1)
    own_start = lax.dynamic_slice_in_dim(start_all, rank * tokens, tokens)
    position = (rank * tokens + jnp.arange(tokens, dtype=jnp.int32) - own_start).astype(F32)
    half = HEAD_DIM // 2
    angles = position[:, None] * THETA ** (-jnp.arange(half, dtype=F32) * 2.0 / HEAD_DIM)
    cosine = jnp.tile(jnp.cos(angles), (1, 4))
    sine = jnp.sin(angles)
    sine = jnp.tile(jnp.concatenate([-sine, sine], axis=1), (1, 2))
    start = start_all.reshape(parts, 1, tokens)

    x_low = inputs.reshape(tokens, width)
    (q, k, v, hidden_in), gains, fulls, helds = opening(
        x_low, first_values.reshape(tokens, width), cosine, sine, gains,
        [wide(w_query), wide(w_key), wide(w_value)], parted, pieces, parts, 3,
    )
    tall = lambda value: unstacked(value, rows)
    query_full, key_full, value_full = (tall(value) for value in fulls)
    gain_one, gain_two = gains[0], gains[1]
    (q_all, k_all, v_all, o_all, lse_all, attended), (*weights, down_full) = attend(
        q, k, v, start, helds, pieces, shapes
    )
    out_full, gate_full, up_full = (tall(value) for value in weights)
    down_full = unstacked(down_full, down_padded)
    output, grad_middle, d_att, grad_out, grad_gate, grad_up, grad_down, grad_gain_two = between(
        x_low, attended, cotangent.reshape(tokens, width), out_full, gain_two[None],
        gate_full, up_full, down_full,
    )
    grad_gain_two = grad_gain_two[0]

    share = lambda grad: stacked(grad.astype(BF16), devices)
    (dq, dk, dv), helds = attend_back(
        d_att, q_all, k_all, v_all, o_all, lse_all, start,
        [share(grad_out), share(grad_gate), share(grad_up), share(grad_down)], pieces,
    )
    (
        grad_first, grad_x, gains_total, total_query, total_key, total_value,
        total_out, total_gate, total_up, total_down,
    ) = closing(
        (dq, dk, dv), (query_full, key_full, value_full), hidden_in, x_low, grad_middle,
        grad_gain_two, cosine, sine, gain_one[None], rows, helds, pieces, shapes, 4,
    )
    own_gain = lambda n: lax.dynamic_slice_in_dim(gains_total[n], index * rows, rows)
    if rows % 16 == 0:
        grad_first, grad_x, total_gate, total_up, total_down, *totals = settle(
            grad_first, grad_x, total_gate, total_up, total_down,
            (total_query, total_key, total_value, total_out), down_rows,
        )
    else:
        low = lambda total: unstacked(total[None], rows)
        close = lambda total: low(total).reshape(rows, devices, down_padded)[:, :, :down_rows]
        total_gate, total_up = (
            close(total).reshape(rows, devices * down_rows) for total in (total_gate, total_up)
        )
        total_down = unstacked(total_down[None], down_padded)[:down_rows]
        totals = [low(total) for total in (total_query, total_key, total_value, total_out)]
        grad_first = grad_first.astype(F32)
    return (
        output.reshape(inputs.shape),
        grad_x.reshape(inputs.shape),
        grad_first.reshape(inputs.shape),
        *totals,
        own_gain(0),
        total_gate,
        total_up,
        total_down,
        own_gain(1),
    )


def solution(mesh):
    tokens = P("dp", "seq", None)
    matrix = P(("dp", "seq"), None)
    vector = P(("dp", "seq"))
    return jax.shard_map(
        shards,
        mesh=mesh,
        in_specs=(
            tokens, tokens, P("dp", None), matrix, matrix, matrix, matrix, vector,
            matrix, matrix, matrix, vector, tokens,
        ),
        out_specs=(
            tokens, tokens, tokens, matrix, matrix, matrix, matrix, vector,
            matrix, matrix, matrix, vector,
        ),
        check_vma=False,
    )
```

```python
import functools

import jax
import jax.numpy as jnp
from jax import lax
from jax.experimental import pallas as pl
from jax.experimental.pallas import tpu as pltpu
from jax.sharding import PartitionSpec as P

HEAD_DIM = 64
EPS = 1e-06
THETA = 10000.0
NEG = -1e30
MESH = pl.DeviceIdType.MESH
BF16 = jnp.bfloat16
F32 = jnp.float32
VMEM = pltpu.VMEM
MIB = 1 << 20


def dot(left, right, left_dim=1, right_dim=0):
    return lax.dot_general(
        left, right, (((left_dim,), (right_dim,)), ((), ())), preferred_element_type=F32
    )


def across(left, right):
    return dot(left, right, 0, 0)


def against(left, right):
    return dot(left, right, 1, 1)


def norm_back(grad_normed, values, gain):
    scale_inv = lax.rsqrt(jnp.mean(values * values, axis=-1, keepdims=True) + EPS)
    normed = values * scale_inv
    grad_scaled = grad_normed * gain
    grad_values = scale_inv * (
        grad_scaled - normed * jnp.mean(grad_scaled * normed, axis=-1, keepdims=True)
    )
    grad_gain = jnp.sum(grad_normed * normed, axis=0)
    return (grad_values, grad_gain)


def turned(values, cosine, sine):
    lane = lax.broadcasted_iota(jnp.int32, values.shape, 1) % HEAD_DIM
    other = jnp.where(
        lane < HEAD_DIM // 2,
        pltpu.roll(values, 128 - HEAD_DIM // 2, 1),
        pltpu.roll(values, HEAD_DIM // 2, 1),
    )
    return values * cosine + other * sine


def greet(parts, me):
    barrier = pltpu.get_barrier_semaphore()
    for step in range(1, parts):
        pl.semaphore_signal(
            barrier, 1, device_id={"seq": lax.rem(me + step, parts)}, device_id_type=MESH
        )
    return parts - 1


def send(source, target, send_sem, recv_sem, peer):
    return pltpu.make_async_remote_copy(
        src_ref=source,
        dst_ref=target,
        send_sem=send_sem,
        recv_sem=recv_sem,
        device_id={"seq": peer},
        device_id_type=MESH,
    )


def arrive(ref, sem):
    pltpu.make_async_copy(ref, ref, sem).wait()


def own_head(values, head, width):
    if width == HEAD_DIM:
        return values
    lane = lax.broadcasted_iota(jnp.int32, values.shape, 1)
    return jnp.where(lane // HEAD_DIM == head, values, jnp.zeros_like(values))


def allowed_tile(i, j, tokens, start):
    key = j * tokens + lax.broadcasted_iota(jnp.int32, (tokens, tokens), 0)
    query = i * tokens + lax.broadcasted_iota(jnp.int32, (tokens, tokens), 1)
    return (key <= query) & (key >= start[i])


def forward_kernel(
    parts, heads, pieces, count,
    q_in, k_in, v_in, start, *refs,
):
    helds, refs = refs[: len(pieces)], refs[len(pieces) :]
    kept, (lse_all, attended), refs = refs[:4], refs[4:6], refs[6:]
    fulls, refs = refs[:count], refs[count:]
    q_all, k_all, v_all, o_all, keep, *refs = refs
    v_turn, total, o_send, in_send, in_recv, o_out, o_in, *sems = refs
    place = Place()
    _, tokens, width = q_in.shape
    half = parts // 2
    me = lax.axis_index("seq")
    own = me // half
    place.greet(greet(parts, me))
    spread = WeightSpread(place, pieces, helds, fulls, sems)
    pairs = ((q_in, q_all), (k_in, k_all), (v_in, v_all))

    def moved(index, peer):
        source, target = pairs[index]
        return send(
            source.at[peer], target.at[me], in_send.at[index, peer], in_recv.at[index, me], peer
        )

    def over(first, action):
        def body(step, _):
            action(first + lax.rem(me + step, half))
            return 0

        lax.fori_loop(0, half, body, 0)

    def start_cross(indices):
        over((1 - own) * half, lambda peer: [moved(index, peer).start() for index in indices])

    def sent_cross(indices):
        over((1 - own) * half, lambda peer: [moved(index, peer).wait_send() for index in indices])

    for index, (source, target) in enumerate(pairs):
        pltpu.make_async_copy(source.at[me], target.at[me], in_recv.at[index, me]).start()
    def start_near(peer):
        @pl.when(peer != me)
        def _():
            for index in range(3):
                moved(index, peer).start()

    over(own * half, start_near)
    pl.when(own == 0)(lambda: start_cross((1, 2)))
    pl.when(own == 1)(lambda: start_cross((0,)))

    def got(index, block):
        arrive(pairs[index][1].at[block], in_recv.at[index, block])

    def got_keys(block):
        got(1, block)
        got(2, block)
        v_turn[block] = v_all[block].T

    def tile(i, j, masked):
        if masked:
            allowed = allowed_tile(i, j, tokens, start)
        queries, keys = q_all[i], k_all[j]
        for head in range(heads):
            rows = slice(head * HEAD_DIM, (head + 1) * HEAD_DIM)
            scores = against(keys, own_head(queries, head, width))
            if masked:
                scores = jnp.where(allowed, scores, NEG)
            old = lse_all[i, head]
            new = jnp.maximum(old, jnp.max(scores, axis=0, keepdims=True))
            weights = jnp.exp(scores - new)
            factor = jnp.exp(old - new)
            lse_all[i, head] = new
            total[i, head] = total[i, head] * factor + jnp.sum(weights, axis=0, keepdims=True)
            o_all[i, rows] = o_all[i, rows] * factor + dot(
                v_turn[j, rows], weights.astype(BF16)
            )

    def tile_row(row, _):
        phase, place_in = row // half, lax.rem(row, half)
        lower = jnp.where(phase == 0, own, 1 - own) * half
        i = jnp.where(phase == 1, half, lower) + place_in
        first = jnp.where(phase == 1, 0, lower)
        last = jnp.where(phase == 1, half, i + 1)
        spread.at_row(row, 3 * half)

        @pl.when(phase == 0)
        def _():
            got(0, i)
            got_keys(i)

        @pl.when((row == half) & (own == 0))
        def _():
            lax.fori_loop(half, parts, lambda block, _: got(0, block) or 0, 0)

        @pl.when((row == half) & (own == 1))
        def _():
            lax.fori_loop(0, half, lambda block, _: got_keys(block) or 0, 0)

        @pl.when((row == half * 3 // 4) & (own == 1))
        def _():
            sent_cross((0,))
            start_cross((1, 2))

        @pl.when((row == half + half // 2) & (own == 0))
        def _():
            sent_cross((1, 2))
            start_cross((0,))

        @pl.when((phase == 2) & (own == 0))
        def _():
            got_keys(i)

        @pl.when((phase == 2) & (own == 1))
        def _():
            got(0, i)

        @pl.when((phase == 0) | ((phase == 1) & (own == 0)) | ((phase == 2) & (own == 1)))
        def _():
            lse_all[i] = jnp.full(lse_all.shape[1:], NEG, F32)
            total[i] = jnp.zeros(total.shape[1:], F32)
            o_all[i] = jnp.zeros(o_all.shape[1:], F32)

        def key_block(j, _):
            masked = (j == 0) | (j == i) | (i == parts - 1)
            pl.when(masked)(lambda: tile(i, j, True))
            pl.when(jnp.logical_not(masked))(lambda: tile(i, j, False))
            return 0

        lax.fori_loop(first, last, key_block, 0)

        @pl.when(((phase == 0) & (own == 0)) | ((phase == 1) & (own == 1)) | (phase == 2))
        def _():
            for head in range(heads):
                rows = slice(head * HEAD_DIM, (head + 1) * HEAD_DIM)
                o_all[i, rows] = o_all[i, rows] / total[i, head]
                lse_all[i, head] = lse_all[i, head] + jnp.log(total[i, head])
            o_send[i] = o_all[i].T.astype(BF16)

            @pl.when(i == me)
            def _():
                pltpu.make_async_copy(o_send.at[i], attended.at[me], o_in.at[me]).start()

            @pl.when(i != me)
            def _():
                send(o_send.at[i], attended.at[me], o_out.at[i], o_in.at[me], i).start()

        return 0

    lax.fori_loop(0, 3 * half, tile_row, 0)
    keeps = [
        pltpu.make_async_copy(source, target, keep.at[n])
        for n, (source, target) in enumerate(zip((q_all, k_all, v_all, o_all), kept))
    ]
    for copy in keeps:
        copy.start()
    spread.finish()
    pl.when(own == 0)(lambda: sent_cross((0,)))
    pl.when(own == 1)(lambda: sent_cross((1, 2)))

    def sent_near(peer):
        @pl.when(peer != me)
        def _():
            for index in range(3):
                moved(index, peer).wait_send()

    over(own * half, sent_near)

    def finish(step, _):
        peer = lax.rem(me + step, parts)
        arrive(o_send.at[peer], o_out.at[peer])
        arrive(attended.at[peer], o_in.at[peer])
        return 0

    lax.fori_loop(1, parts, finish, 0)
    arrive(attended.at[me], o_in.at[me])
    for copy in keeps:
        copy.wait()


def attend(q, k, v, start, helds, pieces, shapes):
    parts, tokens, width = q.shape
    heads = width // HEAD_DIM
    place = Place()
    whole = pl.BlockSpec(memory_space=VMEM)
    far = pl.BlockSpec(memory_space=pl.ANY)
    split = jax.ShapeDtypeStruct(q.shape, BF16)
    flops = 4 * parts * parts * tokens * tokens * width // 2
    fulls = [
        jax.ShapeDtypeStruct((place.xs, 2, place.as_, place.bs, *shape), BF16) for shape in shapes
    ]
    results = pl.pallas_call(
        functools.partial(forward_kernel, parts, heads, pieces, len(shapes)),
        in_specs=[far] * 3 + [whole] * (1 + len(pieces)),
        out_specs=[far] * 4 + [whole] * 2 + [far] * len(shapes),
        out_shape=[
            split,
            split,
            split,
            jax.ShapeDtypeStruct((parts, width, tokens), F32),
            jax.ShapeDtypeStruct((parts, heads, 1, tokens), F32),
            split,
            *fulls,
        ],
        scratch_shapes=[
            *[VMEM(split.shape, BF16)] * 3,
            VMEM((parts, width, tokens), F32),
            pltpu.SemaphoreType.DMA((4,)),
            VMEM((parts, width, tokens), BF16),
            VMEM((parts, heads, 1, tokens), F32),
            VMEM((parts, tokens, width), BF16),
            pltpu.SemaphoreType.DMA((3, parts)),
            pltpu.SemaphoreType.DMA((3, parts)),
            pltpu.SemaphoreType.DMA((parts,)),
            pltpu.SemaphoreType.DMA((parts,)),
            *[spread_semaphores(place)] * len(pieces),
        ],
        compiler_params=pltpu.CompilerParams(
            collective_id=1, has_side_effects=True, vmem_limit_bytes=48 * MIB
        ),
        cost_estimate=pl.CostEstimate(
            flops=4 * flops, bytes_accessed=16 * q.size, transcendentals=flops // 256
        ),
        name="attend",
    )(q, k, v, start, *helds)
    devices = place.xs * 2 * place.as_ * place.bs
    weights = [value.reshape(devices, *value.shape[4:]) for value in results[6:]]
    return results[:6], weights


def backward_kernel(
    parts, heads, pieces, count,
    d_in, q_kept, k_kept, v_kept, o_kept, lse_all, start, *refs,
):
    grads, refs = refs[:count], refs[count:]
    (dq_got, dk_got, dv_got), refs = refs[:3], refs[3:]
    results, refs = refs[: len(pieces)], refs[len(pieces) :]
    q_all, k_all, v_all, o_all, keep, *refs = refs
    d_all, k_turn, delta, dq_turn, dk_sum, dv_sum, dq_send, dk_send, dv_send = refs[:9]
    in_send, in_recv, out_send, out_recv, *buffers = refs[9:]
    place = Place()
    _, tokens, width = d_in.shape
    half = parts // 2
    me = lax.axis_index("seq")
    own = me // half
    keeps = [
        pltpu.make_async_copy(source, target, keep.at[n])
        for n, (source, target) in enumerate(
            zip((q_kept, k_kept, v_kept, o_kept), (q_all, k_all, v_all, o_all))
        )
    ]
    for copy in keeps:
        copy.start()
    place.greet(greet(parts, me))
    adding = GradSums(place, pieces, grads, results, buffers)

    def over(first, action):
        def body(step, _):
            action(first + lax.rem(me + step, half))
            return 0

        lax.fori_loop(0, half, body, 0)

    def moved(peer):
        return send(d_in.at[peer], d_all.at[me], in_send.at[peer], in_recv.at[me], peer)

    pltpu.make_async_copy(d_in.at[me], d_all.at[me], in_recv.at[me]).start()

    def start_near(peer):
        pl.when(peer != me)(lambda: moved(peer).start())

    over(own * half, start_near)
    over((1 - own) * half, lambda peer: moved(peer).start())
    sends = ((dq_send, dq_got), (dk_send, dk_got), (dv_send, dv_got))

    def give(index, block):
        source, target = sends[index]

        @pl.when(block == me)
        def _():
            pltpu.make_async_copy(
                source.at[block], target.at[me], out_recv.at[index, me]
            ).start()

        @pl.when(block != me)
        def _():
            send(
                source.at[block], target.at[me],
                out_send.at[index, block], out_recv.at[index, me], block,
            ).start()

    def give_query(i):
        dq_send[i] = (dq_turn[i] * HEAD_DIM**-0.5).T.astype(BF16)
        give(0, i)

    def give_keys(j):
        dk_send[j] = dk_sum[j].astype(BF16)
        dv_send[j] = dv_sum[j].astype(BF16)
        give(1, j)
        give(2, j)

    def tile(i, j, masked):
        if masked:
            allowed = allowed_tile(i, j, tokens, start)
        queries, grads_out, keys, mixed = q_all[i], d_all[i], k_all[j], v_all[j]
        for head in range(heads):
            rows = slice(head * HEAD_DIM, (head + 1) * HEAD_DIM)
            query, grad = own_head(queries, head, width), own_head(grads_out, head, width)
            scores = against(keys, query)
            if masked:
                scores = jnp.where(allowed, scores, NEG)
            weights = jnp.exp(scores - lse_all[i, head])
            dv_sum[j] += dot(weights.astype(BF16), grad)
            slope = against(mixed, grad) - delta[i, head]
            d_scores = (weights * slope).astype(BF16)
            dk_sum[j] += dot(d_scores, query)
            dq_turn[i, rows] += dot(k_turn[j, rows], d_scores)

    def prepare(block):
        arrive(d_all.at[block], in_recv.at[block])
        product = d_all[block].astype(F32).T * o_all[block]
        for head in range(heads):
            rows = slice(head * HEAD_DIM, (head + 1) * HEAD_DIM)
            delta[block, head] = jnp.sum(product[rows], axis=0, keepdims=True)
        k_turn[block] = k_all[block].T
        dq_turn[block] = jnp.zeros(dq_turn.shape[1:], F32)
        dk_sum[block] = jnp.zeros(dk_sum.shape[1:], F32)
        dv_sum[block] = jnp.zeros(dv_sum.shape[1:], F32)

    def tile_row(row, _):
        phase, place_in = row // half, lax.rem(row, half)
        adding.at_row(row, 3 * half)

        @pl.when(row == 0)
        def _():
            lax.fori_loop(0, half, lambda n, _: prepare(own * half + n) or 0, 0)

        @pl.when(row == half)
        def _():
            lax.fori_loop(0, half, lambda n, _: prepare((1 - own) * half + n) or 0, 0)

        by_query = jnp.where(phase == 1, own == 1, own == 0)
        lower = jnp.where(phase == 0, own, 1 - own) * half
        outer = jnp.where(
            phase == 2, jnp.where(by_query, half, 0), lower
        ) + place_in
        first = jnp.where(phase == 2, jnp.where(by_query, 0, half), jnp.where(by_query, lower, outer))
        last = jnp.where(
            phase == 2,
            jnp.where(by_query, half, parts),
            jnp.where(by_query, outer + 1, lower + half),
        )

        def inner_block(inner, _):
            i, j = jnp.where(by_query, outer, inner), jnp.where(by_query, inner, outer)
            masked = (j == 0) | (j == i) | (i == parts - 1)
            pl.when(masked)(lambda: tile(i, j, True))
            pl.when(jnp.logical_not(masked))(lambda: tile(i, j, False))
            return 0

        lax.fori_loop(first, last, inner_block, 0)
        pl.when(by_query)(lambda: give_query(outer))
        pl.when(jnp.logical_not(by_query))(lambda: give_keys(outer))
        return 0

    for copy in keeps:
        copy.wait()
    lax.fori_loop(0, 3 * half, tile_row, 0)
    pl.when(own == 0)(lambda: over(0, give_keys))
    pl.when(own == 1)(lambda: over(half, give_query))
    adding.finish()

    def finish(step, _):
        peer = lax.rem(me + step, parts)
        moved(peer).wait_send()
        for index, (source, target) in enumerate(sends):
            arrive(source.at[peer], out_send.at[index, peer])
            arrive(target.at[peer], out_recv.at[index, peer])
        return 0

    lax.fori_loop(1, parts, finish, 0)
    for index, (_, target) in enumerate(sends):
        arrive(target.at[me], out_recv.at[index, me])


def attend_back(d_att, q, k, v, o, lse, start, grads, pieces):
    parts, tokens, width = q.shape
    heads = width // HEAD_DIM
    place = Place()
    whole = pl.BlockSpec(memory_space=VMEM)
    far = pl.BlockSpec(memory_space=pl.ANY)
    split = jax.ShapeDtypeStruct(q.shape, BF16)
    flops = 10 * parts * parts * tokens * tokens * width // 2
    sum_shapes = [piece.held(place, grads[piece.array].shape[1]) for piece in pieces]
    sum_scratch = GradSums.scratch(place, pieces, grads)
    grads = [placed(place, grad) for grad in grads]
    results = pl.pallas_call(
        functools.partial(backward_kernel, parts, heads, pieces, len(grads)),
        in_specs=[far] * 5 + [whole] * 2 + [far] * len(grads),
        out_specs=[far] * 3 + [far] * len(pieces),
        out_shape=[split] * 3 + sum_shapes,
        scratch_shapes=[
            *[VMEM(split.shape, BF16)] * 3,
            VMEM((parts, width, tokens), F32),
            pltpu.SemaphoreType.DMA((4,)),
            VMEM((parts, tokens, width), BF16),
            VMEM((parts, width, tokens), BF16),
            VMEM((parts, heads, 1, tokens), F32),
            VMEM((parts, width, tokens), F32),
            VMEM((parts, tokens, width), F32),
            VMEM((parts, tokens, width), F32),
            VMEM((parts, tokens, width), BF16),
            VMEM((parts, tokens, width), BF16),
            VMEM((parts, tokens, width), BF16),
            pltpu.SemaphoreType.DMA((parts,)),
            pltpu.SemaphoreType.DMA((parts,)),
            pltpu.SemaphoreType.DMA((3, parts)),
            pltpu.SemaphoreType.DMA((3, parts)),
            *sum_scratch,
        ],
        compiler_params=pltpu.CompilerParams(
            collective_id=2, has_side_effects=True, vmem_limit_bytes=60 * MIB
        ),
        cost_estimate=pl.CostEstimate(
            flops=4 * flops, bytes_accessed=20 * q.size, transcendentals=flops // 640
        ),
        name="attend_back",
    )(d_att, q, k, v, o, lse, start, *grads)
    return results[:3], results[3:]


class Place:
    def __init__(self):
        self.xs = lax.axis_size("dp") // 2
        seq = lax.axis_size("seq")
        self.bs = 2 if seq <= 8 else 4
        self.as_ = seq // self.bs
        dp, rank = lax.axis_index("dp"), lax.axis_index("seq")
        self.x, self.core = dp // 2, lax.rem(dp, 2)
        self.a, self.b = rank // self.bs, lax.rem(rank, self.bs)

    def device(self, x=None, core=None, a=None, b=None):
        x, core = (self.x if x is None else x), (self.core if core is None else core)
        a, b = (self.a if a is None else a), (self.b if b is None else b)
        return (x * 2 + core, a * self.bs + b)

    def peers(self, axis):
        size = {"x": self.xs, "a": self.as_, "b": self.bs}[axis]
        own = getattr(self, axis)
        return [(step - 1, lax.rem(own + step, size)) for step in range(1, size)]

    def greet(self, greeted=0):
        barrier = pltpu.get_barrier_semaphore()
        others = [self.device(core=1 - self.core)]
        for axis in "x" if greeted else "xab":
            others += [self.device(**{axis: index}) for _, index in self.peers(axis)]
        for other in others:
            pl.semaphore_signal(barrier, 1, device_id=other, device_id_type=MESH)
        pl.semaphore_wait(barrier, len(others) + greeted)

    @property
    def inner(self):
        return (self.a == 1) | (self.a == 2)

    @property
    def beside(self):
        return self.a + 1 - 2 * lax.rem(self.a, 2)


def column_pieces(columns, wanted):
    tiles = columns // 128
    wanted = min(wanted, tiles)
    edges = [tiles * n // wanted * 128 for n in range(wanted)] + [columns]
    return [(edges[n], edges[n + 1] - edges[n]) for n in range(wanted)]


def placed(place, value):
    return value.reshape(place.xs, 2, place.as_, place.bs, *value.shape[1:])


def remote(source, target, send_sem, recv_sem, device):
    return pltpu.make_async_remote_copy(
        src_ref=source,
        dst_ref=target,
        send_sem=send_sem,
        recv_sem=recv_sem,
        device_id=device,
        device_id_type=MESH,
    )


def flat(ref):
    rows, columns = ref.shape[-2:]
    return ref.reshape(ref.size // (rows * columns), rows, columns)


class Relay:
    def __init__(self, place, source, target, sems):
        self.p, self.source, self.target, self.sems = place, source, target, sems
        assert place.as_ == 4

    def near(self):
        p = self.p
        return remote(
            self.source, self.target.at[p.a],
            self.sems.at[0, 0], self.sems.at[1, 0], p.device(a=p.beside),
        )

    def middle(self):
        p = self.p
        held = self.target.at[pl.ds(p.a // 2 * 2, 2)]
        return remote(
            held, held, self.sems.at[0, 1], self.sems.at[1, 1], p.device(a=3 - p.a)
        )

    def outward(self):
        p = self.p
        held = self.target.at[pl.ds((1 - p.a // 2) * 2, 2)]
        return remote(
            held, held, self.sems.at[0, 2], self.sems.at[1, 1], p.device(a=p.beside)
        )

    def local(self):
        return pltpu.make_async_copy(self.source, self.target.at[self.p.a], self.sems.at[1, 2])

    def step(self, number):
        if number == 0:
            self.local().start()
            self.near().start()
        elif number == 1:
            self.local().wait()
            self.near().wait_recv()
            pl.when(self.p.inner)(lambda: self.middle().start())
        elif number == 2:

            @pl.when(self.p.inner)
            def _():
                self.middle().wait_recv()
                self.outward().start()
        else:

            @pl.when(jnp.logical_not(self.p.inner))
            def _():
                self.middle().wait_recv()

            @pl.when(self.p.inner)
            def _():
                self.middle().wait_send()
                self.outward().wait_send()

            self.near().wait_send()


class Direct:
    def __init__(self, place, source, target, sems):
        self.p, self.source, self.target, self.sems = place, source, target, sems

    def copies(self):
        p = self.p
        return [
            remote(
                self.source, self.target.at[p.a],
                self.sems.at[0, s], self.sems.at[1, s], p.device(a=index),
            )
            for s, index in p.peers("a")
        ]

    def local(self):
        return pltpu.make_async_copy(self.source, self.target.at[self.p.a], self.sems.at[0, 3])

    def step(self, number):
        if number == 0:
            self.local().start()
            for copy in self.copies():
                copy.start()
        elif number == 3:
            self.local().wait()
            for copy in self.copies():
                copy.wait()


class Piece:
    def __init__(self, array, start, size, order, deep):
        self.array, self.start, self.size, self.order, self.deep = array, start, size, order, deep

    @staticmethod
    def all(shapes):
        pieces = []
        for array, kinds in enumerate(
            ([("bx", 0)], [("bx", 1)] * 2, [("xb", 1), ("bx", 1)], [("bx", 0)] * 2)
        ):
            for (start, size), kind in zip(column_pieces(shapes[array][1], len(kinds)), kinds):
                pieces.append(Piece(array, start, size, *kind))
        return pieces

    def held(self, place, rows):
        lead = {"": (), "b": (place.bs,), "x": (place.xs,)}[self.order[0] if self.deep else ""]
        lead = (*lead, place.as_) if self.order[0] == "x" else (place.as_, *lead)
        return jax.ShapeDtypeStruct((*lead, rows, self.size), BF16)

    def along_a(self, place, held):
        if not self.deep:
            return held
        return held.at[place.x] if self.order[0] == "x" else held.at[:, place.b]

    def columns(self, ref):
        return ref.at[(slice(None),) * (len(ref.shape) - 1) + (pl.ds(self.start, self.size),)]


class Spread:
    def __init__(self, place, views, order, sems, source=None, first=0):
        self.place, self.views, self.order, self.sems = place, views, order, sems
        self.source, self.first = source, first

    @staticmethod
    def views_of(place, full, order):
        p = place
        middle = full.at[:, p.core, :, p.b] if order == "xb" else full.at[p.x, p.core]
        return full.at[p.x, p.core, :, p.b], middle, full.at[:, p.core]

    def copies(self, number):
        p, view = self.place, self.views[number]
        source = self.source if self.source is not None and number == self.first else view
        base = sum([len(p.peers(axis)) for axis in self.order][:number])
        if number == 2:
            devices = [(0, p.device(core=1 - p.core))]
        else:
            axis = self.order[number]
            devices = [(s, p.device(**{axis: index})) for s, index in p.peers(axis)]
        return [
            remote(source, view, self.sems.at[0, base + s], self.sems.at[1, base + s], device)
            for s, device in devices
        ]

    def local(self):
        return pltpu.make_async_copy(self.source, self.views[self.first], self.sems.at[2, 0])

    def start(self, number):
        if self.source is not None and number == self.first:
            self.local().start()
        for copy in self.copies(number):
            copy.start()

    def finish(self, number):
        if self.source is not None and number == self.first:
            self.local().wait()
        for copy in self.copies(number):
            copy.wait_recv()
            copy.wait_send()

    def then(self, number):
        self.finish(number)
        if number < 2:
            self.start(number + 1)


def spread_semaphores(place):
    return pltpu.SemaphoreType.DMA((3, place.xs + place.bs - 1))


RELAY_SEMAPHORES = (2, 4)


class InRows:
    def at_row(self, row, count):
        for at in sorted({at for at, _ in self.actions() if at < 12}):

            @pl.when(row == at * count // 12)
            def _():
                for own_row, action in self.actions():
                    if own_row == at:
                        action()

    def finish(self):
        for at, action in self.actions():
            if at >= 12:
                action()


class WeightSpread(InRows):
    def __init__(self, place, pieces, sources, fulls, sems):
        self.units = []
        for piece, source, own_sems in zip(pieces, sources, sems):
            full = piece.columns(fulls[piece.array])
            views = Spread.views_of(place, full, piece.order)
            self.units.append(Spread(place, views, piece.order, own_sems, source, piece.deep))

    def actions(self):
        out, gate0, gate1, up0, up1, down0, down1 = self.units
        start = lambda unit: functools.partial(unit.start, unit.first)
        then = lambda unit, number: functools.partial(unit.then, number)
        done = [(0, start(unit)) for unit in (gate0, down0, gate1, down1, up1, out, up0)]
        done += [(4, then(down0, 0)), (5, then(down1, 0)), (6, then(out, 0))]
        done += [(7, then(gate0, 1)), (8, then(gate1, 1)), (9, then(up0, 1)), (10, then(up1, 1))]
        done += [(12, then(unit, 1)) for unit in (down0, down1, out)]
        done += [(12, then(unit, 2)) for unit in (gate0, gate1, up0, up1, down0, down1, out)]
        return done


class TotalSum:
    def __init__(self, place, mine, got, sems):
        self.place, self.mine, self.got, self.sems = place, mine, got, sems

    def slots(self, number):
        p = self.place
        devices = [[p.device(core=1 - p.core)]]
        devices += [[p.device(**{axis: index}) for _, index in p.peers(axis)] for axis in "xba"]
        return sum(len(some) for some in devices[:number]), devices[number]

    def copies(self, number):
        base, devices = self.slots(number)
        return [
            remote(
                self.mine, self.got.at[base + n],
                self.sems.at[0, base + n], self.sems.at[1, base + n], device,
            )
            for n, device in enumerate(devices)
        ]

    def start(self, number):
        for copy in self.copies(number):
            copy.start()

    def then(self, number):
        for copy in self.copies(number):
            copy.wait()
        base, devices = self.slots(number)
        for slot in range(len(devices)):
            self.mine[...] += self.got[base + slot]
        if number < 3:
            self.start(number + 1)


def opening_kernel(
    plan, pieces, parted, padded,
    x, first, cosine, sine, gains, w_query, w_key, w_value, *refs,
):
    shares, refs = refs[:parted], refs[parted:]
    (q_out, k_out, v_out, hidden, gains_total), kept, refs = refs[:5], refs[5:8], refs[8:]
    helds, refs = refs[: len(pieces)], refs[len(pieces) :]
    fulls, (keep, got_gains, gain_sems, relay_sems, *refs) = refs[:3], refs[3:]
    spaced, sems = refs[:padded], refs[padded:]
    given, shares = shares, [*shares[: parted - padded], *spaced]
    place = Place()
    parts, tokens, width = q_out.shape
    dim = parts * width
    place.greet()
    gains_total[...] = gains[...]
    total = TotalSum(place, gains_total, got_gains, gain_sems)
    units, relays = [], []
    sources = (w_query, w_key, w_value)
    for number, (array, start, size, order) in enumerate(plan):
        views = Spread.views_of(place, fulls[array].at[:, :, :, :, :, pl.ds(start, size)], order)
        relays.append(
            Direct(place, sources[array].at[:, pl.ds(start, size)], views[0], relay_sems.at[number])
        )
        units.append(Spread(place, views, order, sems[number]))
    deep, flat_relays, deep_relays = [], [], []
    for number, (piece, held) in enumerate(zip(pieces, helds)):
        view = piece.along_a(place, held)
        index = len(plan) + number
        relay = Relay(place, piece.columns(shares[piece.array]), view, relay_sems.at[index])
        (deep_relays if piece.deep else flat_relays).append(relay)
        if piece.deep:
            deep.append(Spread(place, [view], piece.order, sems[index]))

    def step(group, number):
        for relay in group:
            relay.step(number)

    def then(some, number):
        for unit in some:
            unit.then(number)

    def weight(array, start, size):
        full = fulls[array]
        rows, columns = full.shape[-2:]
        fold = dim // columns
        value = full[:, :, :, :, :, start % columns : start % columns + size]
        if fold > 1:
            share = rows // fold
            part = start // columns * share
            value = value.astype(F32)[:, :, :, :, part : part + share]
        return value.reshape(dim, size).astype(BF16)

    def project(array):
        for start in range(0, dim, 256):
            raw = dot(hidden[...], weight(array, start, 256))
            if array == 2:
                raw = 0.5 * raw + 0.5 * first[:, start : start + 256].astype(F32)
            for begin in range(0, 256, 128):
                value = raw[:, begin : begin + 128]
                if array < 2:
                    value = turned(value, cosine[...], sine[...])
                if array == 0:
                    value = value * HEAD_DIM**-0.5
                for lane in range(0, 128, width):
                    out = (q_out, k_out, v_out)[array]
                    out[(start + begin + lane) // width] = value[:, lane : lane + width].astype(BF16)

    half = len(units) // 2
    line = deep_relays + flat_relays

    def tick(number):
        for back in (3, 2, 1, 0):
            index = number - back
            if 0 <= index < len(line):
                line[index].step(back)
                if back == 3 and index < len(deep):
                    deep[index].start(0)

    step(relays, 0)
    total.start(0)
    if padded:
        *wides, tall = given[parted - padded :]
        for source, target in zip(wides, spaced):
            share = tall.shape[0]
            gap = spaced[-1].shape[0] - share
            value, gaps = source[...].astype(F32), jnp.zeros((source.shape[0], gap), F32)
            parts_of = [value[:, n : n + share] for n in range(0, value.shape[1], share)]
            target[...] = jnp.concatenate(
                [part for value in parts_of for part in (value, gaps)], axis=1
            ).astype(BF16)
        gaps = jnp.zeros((gap, tall.shape[1]), F32)
        spaced[-1][...] = jnp.concatenate([tall[...].astype(F32), gaps], axis=0).astype(BF16)
    step(relays, 1)
    tick(0)
    step(relays, 2)
    total.then(0)
    for relay, unit in zip(relays, units):
        relay.step(3)
        unit.start(0)
    tick(1)
    total.then(1)
    then(units[:half], 0)
    tick(2)
    then(units[half:], 0)
    total.then(2)
    tick(3)
    total.then(3)
    values = x[...].astype(F32)
    scale = lax.rsqrt(jnp.mean(values * values, axis=-1, keepdims=True) + EPS)
    hidden[...] = (values * scale * gains_total[0:1]).astype(BF16)
    tick(4)
    then(units[:half], 1)
    tick(5)
    then(units[half:], 1)
    keeps = []
    for array in range(3):
        then([unit for unit, piece in zip(units, plan) if piece[0] == array], 2)
        keeps.append(pltpu.make_async_copy(fulls[array], kept[array], keep.at[array]))
        keeps[array].start()
        project(array)
        tick(6 + array)
    for number in range(9, len(line) + 3):
        tick(number)
    for unit in deep:
        unit.finish(0)
    for copy in keeps:
        copy.wait()


def opening(
    x, first, cosine, sine, gains, weights, parted, shapes, pieces, parts, collective_id
):
    place = Place()
    xs, as_, bs = place.xs, place.as_, place.bs
    tokens, dim = x.shape
    plan = []
    for number, array in enumerate(weights):
        for start, size in column_pieces(array.shape[1], 2):
            plan.append((number, start, size, "xb" if len(plan) % 2 == 1 else "bx"))
    shape = jax.ShapeDtypeStruct
    near = [shape((parts, tokens, dim // parts), BF16)] * 3
    near += [shape((tokens, dim), BF16), shape(gains.shape, F32)]
    near += [shape((xs, 2, as_, bs, *array.shape), array.dtype) for array in weights]
    held = [piece.held(place, shapes[piece.array][0]) for piece in pieces]
    padded = sum(array.shape != shape for array, shape in zip(parted, shapes))
    ready = len(parted) - padded
    far, whole = pl.BlockSpec(memory_space=pl.ANY), pl.BlockSpec(memory_space=VMEM)
    count = len(plan) + len(pieces)
    peers = 1 + (xs - 1) + (bs - 1) + (as_ - 1)
    results = pl.pallas_call(
        functools.partial(opening_kernel, plan, pieces, len(parted), padded),
        in_specs=[whole] * 5 + [far] * (3 + ready) + [whole] * padded,
        out_specs=[whole] * 5 + [far] * 3 + [whole] * len(held),
        out_shape=near + held,
        scratch_shapes=[
            *[VMEM(each.shape, BF16) for each in near[5:]],
            pltpu.SemaphoreType.DMA((3,)),
            VMEM((peers, *gains.shape), F32),
            pltpu.SemaphoreType.DMA((2, peers)),
            pltpu.SemaphoreType.DMA((count, *RELAY_SEMAPHORES)),
            *[VMEM(shape, BF16) for shape in shapes[ready:]],
            *[spread_semaphores(place)] * count,
        ],
        compiler_params=pltpu.CompilerParams(
            collective_id=collective_id, has_side_effects=True, vmem_limit_bytes=48 * MIB
        ),
        cost_estimate=pl.CostEstimate(
            flops=6 * tokens * dim * dim, bytes_accessed=20 * dim * dim, transcendentals=0
        ),
        name="opening",
    )(x, first, cosine, sine, gains, *weights, *parted)
    devices = xs * 2 * as_ * bs
    fulls = [value.reshape(devices, *value.shape[4:]) for value in results[5:8]]
    return results[:4], results[4], fulls, results[8:]


def add_up(mine, others):
    lead = mine.shape[:-2]

    def at(ref, step):
        index = []
        for size in reversed(lead):
            index.insert(0, lax.rem(step, size))
            step = step // size
        return ref.at[tuple(index)]

    def body(step, _):
        total = at(mine, step)[...].astype(F32)
        for other in others:
            total += at(other, step)[...].astype(F32)
        at(mine, step)[...] = total.astype(mine.dtype)
        return 0

    count = 1
    for size in lead:
        count *= size
    lax.fori_loop(0, count, body, 0)


class RelaySum:
    def __init__(self, place, own, inward, middle, last, sems, result):
        self.p, self.own, self.sems, self.result = place, own, sems, result
        self.inward, self.middle, self.last = inward, middle, last
        assert place.as_ == 4

    def move(self, number):
        p = self.p
        far = self.own.at[pl.ds((1 - p.a // 2) * 2, 2)]
        if number == 0:
            source, target, device = far, self.inward, p.beside
        elif number == 1:
            source, target, device = far, self.middle, 3 - p.a
        else:
            source, target, device = self.own.at[p.beside], self.last, p.beside
        return remote(
            source, target, self.sems.at[0, number], self.sems.at[1, number], p.device(a=device)
        )

    def step(self, number):
        p, inner = self.p, self.p.inner
        outer = jnp.logical_not(inner)
        if number == 0:
            pl.when(outer)(lambda: self.move(0).start())
            pl.when(outer)(lambda: self.move(2).start())
        elif number == 1:

            @pl.when(inner)
            def _():
                self.move(0).wait_recv()
                add_up(self.own.at[pl.ds((1 - p.a // 2) * 2, 2)], [self.inward])
                self.move(1).start()
        elif number == 2:

            @pl.when(inner)
            def _():
                self.move(1).wait_recv()
                add_up(self.own.at[pl.ds(p.a // 2 * 2, 2)], [self.middle])
                self.move(2).start()
        else:
            self.move(2).wait_recv()
            self.result[...] = self.own[p.a].astype(F32) + self.last[...].astype(F32)
            pl.when(outer)(lambda: self.move(0).wait_send())
            pl.when(inner)(lambda: self.move(1).wait_send())
            self.move(2).wait_send()

    @staticmethod
    def scratch(rows, columns, dtype):
        return [
            VMEM((2, rows, columns), dtype),
            VMEM((2, rows, columns), dtype),
            VMEM((rows, columns), dtype),
            pltpu.SemaphoreType.DMA((2, 3)),
        ]


class DirectSum:
    def __init__(self, place, own, got, sems, result):
        self.p, self.own, self.got, self.sems, self.result = place, own, got, sems, result

    def copies(self):
        p = self.p
        return [
            remote(
                self.own.at[index], self.got.at[s],
                self.sems.at[0, s], self.sems.at[1, s], p.device(a=index),
            )
            for s, index in p.peers("a")
        ]

    def step(self, number):
        if number == 0:
            for copy in self.copies():
                copy.start()
        elif number == 3:
            total = self.own[self.p.a].astype(F32)
            for slot, copy in enumerate(self.copies()):
                copy.wait()
                total += self.got[slot].astype(F32)
            self.result[...] = total

    @staticmethod
    def scratch(place, rows, columns, dtype):
        return [
            VMEM((place.as_ - 1, rows, columns), dtype),
            pltpu.SemaphoreType.DMA((2, place.as_ - 1)),
        ]


class Sum:
    def __init__(self, place, source, order, buffers):
        self.place, self.order, self.source = place, order, source
        self.own, self.got0, self.got1, self.got2, self.sems = buffers
        self.copied = self.own is not None
        if not self.copied:
            self.own = source.at[:, place.core]

    @property
    def held(self):
        return self.own.at[self.place.x, :, self.place.b]

    @property
    def part(self):
        p = self.place
        return self.own.at[p.x] if self.order[0] == "x" else self.own.at[:, :, p.b]

    def moves(self, number):
        p = self.place
        if number == 0:
            return [(self.source.at[:, 1 - p.core], self.got0, 0, p.device(core=1 - p.core))]
        axis = self.order[number - 1]
        got = self.got1 if number == 1 else self.got2
        moves = []
        for slot, index in p.peers(axis):
            if axis == "x":
                piece = self.own.at[index] if number == 1 else self.own.at[index, :, p.b]
            else:
                piece = self.own.at[:, :, index] if number == 1 else self.own.at[p.x, :, index]
            moves.append((piece, got.at[slot], slot, p.device(**{axis: index})))
        return moves

    def copies(self, number):
        base = sum(([1] + [len(self.place.peers(axis)) for axis in self.order])[:number])
        return [
            remote(source, target, self.sems.at[0, base + s], self.sems.at[1, base + s], device)
            for source, target, s, device in self.moves(number)
        ]

    def local(self):
        return pltpu.make_async_copy(
            self.source.at[:, self.place.core], self.own, self.sems.at[2, 0]
        )

    def start(self, number):
        for copy in self.copies(number):
            copy.start()
        if number == 0 and self.copied:
            self.local().start()

    def finish(self, number):
        p = self.place
        if number == 0 and self.copied:
            self.local().wait()
        for copy in self.copies(number):
            copy.wait_recv()
            copy.wait_send()
        if number == 0:
            add_up(self.own, [self.got0])
        else:
            mine = self.held if number == 2 else self.part
            got = self.got1 if number == 1 else self.got2
            add_up(mine, [got.at[slot] for slot in range(len(p.peers(self.order[number - 1])))])

    @staticmethod
    def scratch(place, rows, size, order, dtype, copied=True):
        xs, as_, bs = place.xs, place.as_, place.bs
        shapes = {
            "x": ((xs - 1, as_, bs, rows, size), (xs - 1, as_, rows, size)),
            "b": ((bs - 1, xs, as_, rows, size), (bs - 1, as_, rows, size)),
        }
        return [VMEM((xs, as_, bs, rows, size), dtype)] * copied + [
            VMEM((xs, as_, bs, rows, size), dtype),
            VMEM(shapes[order[0]][0], dtype),
            VMEM(shapes[order[1]][1], dtype),
            pltpu.SemaphoreType.DMA((3, xs + bs - 1)),
        ]


class GradSums(InRows):
    def __init__(self, place, pieces, grads, results, buffers):
        self.units, self.outs = [], []
        for piece, result in zip(pieces, results):
            source = piece.columns(grads[piece.array])
            unit, buffers = Sum(place, source, piece.order[::-1], buffers[:5]), buffers[5:]
            self.units.append(unit)
            self.outs.append((unit.part if piece.deep else unit.held, result))

    @staticmethod
    def scratch(place, pieces, grads):
        return [
            item
            for piece in pieces
            for item in Sum.scratch(
                place, grads[piece.array].shape[1], piece.size, piece.order[::-1], BF16
            )
        ]

    def actions(self):
        out, gate0, gate1, up0, up1, down0, down1 = self.units

        def copy_of(unit):
            source, result = self.outs[self.units.index(unit)]
            return pltpu.make_async_copy(source, result, unit.sems.at[2, 1])

        def then(unit, number):
            def action():
                unit.finish(number)
                if number < (1 if unit in (gate0, gate1, up0, up1) else 2):
                    unit.start(number + 1)
                else:
                    copy_of(unit).start()

            return action

        order = (down0, down1, out, up0, gate0, gate1, up1)
        done = [(0, functools.partial(unit.start, 0)) for unit in order]
        done += [(row, then(unit, 0)) for row, unit in zip((0, 1, 1, 2, 2, 3, 3), order)]
        done += [(6, then(down0, 1)), (7, then(down1, 1)), (8, then(out, 1)), (9, then(up0, 1))]
        done += [(10, then(gate0, 1)), (11, then(down0, 2))]
        done += [(12, then(down1, 2)), (12, then(out, 2)), (12, then(gate1, 1)), (12, then(up1, 1))]
        done += [(12, lambda unit=unit: copy_of(unit).wait()) for unit in order]
        return done


class HeldSum:
    def __init__(self, place, piece, source, buffers, result):
        self.place, self.piece, self.source = place, piece, source
        self.own, self.got, self.sems, *relay = buffers
        self.relay = RelaySum(place, self.own, *relay, result)
        self.axis = piece.order[0]

    def copies(self):
        if not self.piece.deep:
            return []
        p = self.place
        at = lambda index: self.source.at[index] if self.axis == "x" else self.source.at[:, index]
        return [
            remote(
                at(index), self.got.at[s], self.sems.at[0, s], self.sems.at[1, s],
                p.device(**{self.axis: index}),
            )
            for s, index in p.peers(self.axis)
        ]

    def local(self):
        mine = self.piece.along_a(self.place, self.source)
        return pltpu.make_async_copy(mine, self.own, self.sems.at[2, 0])

    def start(self):
        self.local().start()
        for copy in self.copies():
            copy.start()

    def finish(self):
        self.local().wait()
        copies = self.copies()
        for copy in copies:
            copy.wait_recv()
            copy.wait_send()
        if len(copies):
            add_up(self.own, [self.got.at[slot] for slot in range(len(copies))])
        self.relay.step(0)

    @staticmethod
    def scratch(place, piece, rows):
        count = len(place.peers(piece.order[0])) if piece.deep else 1
        got = (count, place.as_, rows, piece.size) if piece.deep else (1, 1, 16, 128)
        return [
            VMEM((place.as_, rows, piece.size), BF16),
            VMEM(got, BF16),
            pltpu.SemaphoreType.DMA((3, count)),
            *RelaySum.scratch(rows, piece.size, BF16),
        ]


def closing_kernel(
    plan, pieces, rows, fold, parted,
    dq, dk, dv, w_query, w_key, w_value, hidden, x, d_middle, gains, cosine, sine, gain, *refs,
):
    helds, refs = refs[: len(pieces)], refs[len(pieces) :]
    first_out, x_out, gains_total, *refs = refs
    results, buffers = refs[: 3 + parted], refs[3 + parted :]
    slopes, weights, hidden_in, x_in, middle, hidden_turn, d_hidden, got_gains, gain_sems = buffers[:9]
    loads, grad_first, grad_x, *buffers = buffers[9:]
    place = Place()
    parts, tokens, width = dq.shape
    dim = parts * width
    devices = dim // rows
    place.greet()
    copies = [
        pltpu.make_async_copy(source, target, loads.at[n])
        for n, (source, target) in enumerate(
            (
                (hidden, hidden_in), (dq, slopes.at[0]), (w_query, weights.at[0]),
                (dk, slopes.at[1]), (w_key, weights.at[1]), (dv, slopes.at[2]),
                (w_value, weights.at[2]), (x, x_in), (d_middle, middle),
            )
        )
    ]
    for copy in copies:
        copy.start()
    units, relays, grads, rest = [], [], [], []
    for array, start, size, order in plan:
        source = buffers[0]
        unit = Sum(place, source, order, (None, *buffers[1:5]))
        result = results[array].at[:, pl.ds(start, size)]
        relays.append(DirectSum(place, unit.held, *buffers[5:7], result))
        units.append(unit)
        grads.append(source)
        buffers = buffers[7:]
    for piece, held in zip(pieces, helds):
        result = piece.columns(results[3 + piece.array])
        rest.append(HeldSum(place, piece, held, buffers[:7], result))
        buffers = buffers[7:]
    deep = [unit for unit in rest if unit.piece.deep]
    simple = [unit for unit in rest if not unit.piece.deep]
    total = TotalSum(place, gains_total, got_gains, gain_sems)
    for unit in simple + deep:
        unit.start()

    def low(array, first, size):
        done = []
        for start in range(first, first + size, 128):
            picks = range(start // width, (start + 128) // width)
            value = jnp.concatenate([slopes[array, n] for n in picks], axis=1).astype(F32)
            if array < 2:
                value = turned(value, cosine[...], -sine[...])
            else:
                value = 0.5 * value
                grad_first[:, start : start + 128] = value.astype(BF16)
            done.append(value.astype(BF16))
        return jnp.concatenate(done, axis=1)

    def compute(index):
        array, start, size, _ = plan[index]
        blocks = []
        for part in range(fold):
            first = part * (dim // fold) + start
            slope = low(array, first, size)
            blocks.append(dot(hidden_turn[...], slope).reshape(devices, rows, size))
            d_hidden[...] += against(slope, weights[array, :, first : first + size])
        block = (blocks[0] if fold == 1 else jnp.concatenate(blocks, axis=1)).astype(BF16)
        grads[index][...] = block.reshape(grads[index].shape)

    def step(group, number):
        for unit in group:
            unit.relay.step(number)

    def then(index, number):
        units[index].finish(number)
        if number < 2:
            units[index].start(number + 1)
        else:
            relays[index].step(0)

    copies[0].wait()
    hidden_turn[...] = hidden_in[...].T
    d_hidden[...] = jnp.zeros_like(d_hidden)
    count = len(units)
    for index in range(count):
        array = plan[index][0]
        if index == 0 or plan[index - 1][0] != array:
            copies[1 + 2 * array].wait()
            copies[2 + 2 * array].wait()
        compute(index)
        units[index].start(0)
        if index == 0:
            for unit in simple:
                unit.finish()
        else:
            then(index - 1, 0)
        if index == 2:
            step(simple, 1)
        if index == 4:
            step(simple, 2)
    copies[7].wait()
    copies[8].wait()
    grad_values, grad_gain = norm_back(d_hidden[...], x_in[...].astype(F32), gain[...])
    grad_x[...] = grad_values + middle[...]
    keeps = [
        pltpu.make_async_copy(grad_first, first_out, loads.at[0]),
        pltpu.make_async_copy(grad_x, x_out, loads.at[1]),
    ]
    for copy in keeps:
        copy.start()
    gains_total[...] = gains[...]
    gains_total[0:1] = grad_gain[None]
    total.start(0)
    then(count - 1, 0)
    for unit in deep:
        unit.finish()
    step(simple, 3)
    for index in range(count // 2):
        then(index, 1)
    step(deep, 1)
    total.then(0)
    for index in range(count // 2, count):
        then(index, 1)
    step(deep, 2)
    total.then(1)
    for index in range(count // 2):
        then(index, 2)
    total.then(2)
    for relay in relays[: count // 2]:
        relay.step(1)
    for index in range(count // 2, count):
        then(index, 2)
    step(deep, 3)
    for relay in relays[count // 2 :]:
        relay.step(1)
    total.then(3)
    for relay in relays:
        relay.step(2)
    for relay in relays:
        relay.step(3)
    for copy in keeps:
        copy.wait()


def closing(
    slopes, weights, hidden, x, d_middle, grad_gain, cosine, sine, gain, rows, helds, pieces,
    shapes, collective_id,
):
    place = Place()
    parts, tokens, width = slopes[0].shape
    dim = parts * width
    fold = 1
    while rows * fold % 16:
        fold *= 2
    plan, scratch = [], []
    for array in range(3):
        for start, size in column_pieces(dim // fold, 2):
            order = "bx" if len(plan) % 2 == 1 else "xb"
            plan.append((array, start, size, order))
            lead = (place.xs, 2, place.as_, place.bs)
            scratch.append(VMEM((*lead, rows * fold, size), BF16))
            scratch += Sum.scratch(place, rows * fold, size, order, BF16, False)
            scratch += DirectSum.scratch(place, rows * fold, size, BF16)
    for piece in pieces:
        scratch += HeldSum.scratch(place, piece, shapes[piece.array][0])
    peers = 1 + (place.xs - 1) + (place.bs - 1) + (place.as_ - 1)
    far, whole = pl.BlockSpec(memory_space=pl.ANY), pl.BlockSpec(memory_space=VMEM)
    shape = jax.ShapeDtypeStruct
    out = [shape((tokens, dim), BF16), shape((tokens, dim), F32), shape((8, dim), F32)]
    out += [shape((rows * fold, dim // fold), F32)] * 3
    out += [shape(each, F32) for each in shapes]
    return pl.pallas_call(
        functools.partial(closing_kernel, plan, pieces, rows, fold, len(shapes)),
        in_specs=[far] * 9 + [whole] * 4 + [far] * len(helds),
        out_specs=[far] * 2 + [whole] * (len(out) - 2),
        out_shape=out,
        scratch_shapes=[
            VMEM((3, parts, tokens, width), BF16),
            VMEM((3, dim, dim), BF16),
            VMEM((tokens, dim), BF16),
            VMEM((tokens, dim), BF16),
            VMEM((tokens, dim), F32),
            VMEM((dim, tokens), BF16),
            VMEM((tokens, dim), F32),
            VMEM((peers, 8, dim), F32),
            pltpu.SemaphoreType.DMA((2, peers)),
            pltpu.SemaphoreType.DMA((9,)),
            VMEM((tokens, dim), BF16),
            VMEM((tokens, dim), F32),
            *scratch,
        ],
        compiler_params=pltpu.CompilerParams(
            collective_id=collective_id, has_side_effects=True, vmem_limit_bytes=60 * MIB
        ),
        cost_estimate=pl.CostEstimate(
            flops=12 * tokens * dim * dim, bytes_accessed=20 * dim * dim, transcendentals=0
        ),
        name="closing",
    )(*slopes, *weights, hidden, x, d_middle, grad_gain, cosine, sine, gain, *helds)


def stacked(value, devices):
    rows, columns = value.shape[0] // devices, value.shape[1]
    fold = 1
    while rows * fold % 16:
        fold *= 2
    value = value.reshape(devices, rows, fold, columns // fold)
    return value.transpose(0, 2, 1, 3).reshape(devices, rows * fold, columns // fold)


def unstacked(value, rows):
    devices, high, columns = value.shape
    value = value.reshape(devices, high // rows, rows, columns).transpose(0, 2, 1, 3)
    return value.reshape(devices * rows, high // rows * columns)


def settle_kernel(share, padded, first, grad_x, gate, up, down, *refs):
    others, (first_out, x_out, gate_out, up_out, down_out, *others_out) = refs[:4], refs[4:]
    first_out[...] = first[...].astype(F32)
    x_out[...] = grad_x[...]

    @pl.when(pl.program_id(0) == 0)
    def _():
        for source, target in ((gate, gate_out), (up, up_out)):
            count = source.shape[1] // padded
            target[...] = jnp.concatenate(
                [source[:, n * padded : n * padded + share] for n in range(count)], axis=1
            )
        down_out[...] = down[:share]
        for source, target in zip(others, others_out):
            target[...] = source[...]


def settle(first, grad_x, gate, up, down, others, share):
    tokens, dim = grad_x.shape
    padded = down.shape[0]
    units = gate.shape[1] // padded * share
    block = pl.BlockSpec((tokens // 4, dim), lambda g: (g, 0))
    whole = lambda value: pl.BlockSpec(value.shape, lambda g: (0,) * len(value.shape))
    shape = lambda *dims: jax.ShapeDtypeStruct(dims, F32)
    outs = [shape(gate.shape[0], units)] * 2 + [shape(share, dim)]
    outs += [shape(*value.shape) for value in others]
    return pl.pallas_call(
        functools.partial(settle_kernel, share, padded),
        grid=(4,),
        in_specs=[block, block] + [whole(value) for value in (gate, up, down, *others)],
        out_specs=[block, block] + [whole(value) for value in outs],
        out_shape=[shape(tokens, dim)] * 2 + outs,
        compiler_params=pltpu.CompilerParams(vmem_limit_bytes=62 * MIB),
        name="settle",
    )(first, grad_x, gate, up, down, *others)


def middle_kernel(
    steps, x, att, dy, w_out, gain, w_gate, w_up, w_down,
    out, d_middle, d_att, g_out, g_gate, g_up, g_down, g_gain,
    attended, middle, hidden, hidden_turn, result, d_hidden,
):
    step = pl.program_id(0)
    parts, _, width = att.shape

    @pl.when(step == 0)
    def _():
        for part in range(parts):
            attended[:, part * width : (part + 1) * width] = att[part]
        total = x[...].astype(F32) + dot(attended[...], w_out[...])
        scale = lax.rsqrt(jnp.mean(total * total, axis=-1, keepdims=True) + EPS)
        normed = (total * scale * gain[...]).astype(BF16)
        middle[...] = total
        result[...] = total
        hidden[...] = normed
        hidden_turn[...] = normed.T
        d_hidden[...] = jnp.zeros_like(d_hidden)

    grad = dy[...]
    gate = dot(hidden[...], w_gate[...])
    up = dot(hidden[...], w_up[...])
    d_inner = against(grad, w_down[...])
    sigma = jax.nn.sigmoid(gate)
    silu = gate * sigma
    inner = (silu * up).astype(BF16)
    d_gate = (d_inner * up * sigma * (1.0 + gate * (1.0 - sigma))).astype(BF16)
    d_up = (d_inner * silu).astype(BF16)
    result[...] += dot(inner, w_down[...])
    g_down[...] = across(inner, grad).astype(BF16)
    g_gate[...] = dot(hidden_turn[...], d_gate).astype(BF16)
    g_up[...] = dot(hidden_turn[...], d_up).astype(BF16)
    d_hidden[...] += against(d_gate, w_gate[...]) + against(d_up, w_up[...])

    @pl.when(step == steps - 1)
    def _():
        out[...] = result[...].astype(BF16)
        grad_values, grad_gain = norm_back(d_hidden[...], middle[...], gain[...])
        total = grad_values + dy[...].astype(F32)
        d_middle[...] = total
        g_gain[...] = jnp.zeros_like(g_gain)
        g_gain[1:2] = grad_gain[None]
        d_branch = total.astype(BF16)
        g_out[...] = across(attended[...], d_branch).astype(BF16)
        back = against(d_branch, w_out[...]).astype(BF16)
        for part in range(parts):
            d_att[part] = back[:, part * width : (part + 1) * width]


def between(x, att, dy, w_out, gain, w_gate, w_up, w_down):
    tokens, dim = x.shape
    units = w_gate.shape[1]
    chunk = 512 if units % 512 == 0 else 128
    whole = lambda value: pl.BlockSpec(value.shape, lambda g: (0,) * len(value.shape))
    wide = pl.BlockSpec((dim, chunk), lambda g: (0, g))
    tall = pl.BlockSpec((chunk, dim), lambda g: (g, 0))
    shape = jax.ShapeDtypeStruct
    outs = [
        shape((tokens, dim), BF16),
        shape((tokens, dim), F32),
        shape(att.shape, BF16),
        shape(w_out.shape, BF16),
        shape(w_gate.shape, BF16),
        shape(w_up.shape, BF16),
        shape(w_down.shape, BF16),
        shape((8, dim), F32),
    ]
    return pl.pallas_call(
        functools.partial(middle_kernel, units // chunk),
        grid=(units // chunk,),
        in_specs=[whole(v) for v in (x, att, dy, w_out, gain)] + [wide, wide, tall],
        out_specs=[whole(v) for v in outs[:4]] + [wide, wide, tall, whole(outs[7])],
        out_shape=outs,
        scratch_shapes=[
            VMEM((tokens, dim), BF16),
            VMEM((tokens, dim), F32),
            VMEM((tokens, dim), BF16),
            VMEM((dim, tokens), BF16),
            VMEM((tokens, dim), F32),
            VMEM((tokens, dim), F32),
        ],
        compiler_params=pltpu.CompilerParams(vmem_limit_bytes=62 * MIB),
        cost_estimate=pl.CostEstimate(
            flops=18 * tokens * dim * units, bytes_accessed=12 * dim * units, transcendentals=0
        ),
        name="between",
    )(x, att, dy, w_out, gain, w_gate, w_up, w_down)


def shards(
    inputs, first_values, lengths, w_query, w_key, w_value, w_out, gain_attn,
    w_gate, w_up, w_down, gain_mlp, cotangent,
):
    row_count, tokens, width = inputs.shape
    assert row_count == 1
    parts = lax.axis_size("seq")
    rank = lax.axis_index("seq")
    devices = lax.axis_size("dp") * parts
    rows, down_rows = w_query.shape[0], w_down.shape[0]
    multiple = 16 if down_rows >= 64 else 8
    down_padded = -(-down_rows // multiple) * multiple

    def spaced(value):
        value = value.reshape(rows, devices, down_rows)
        value = jnp.pad(value, ((0, 0), (0, 0), (0, down_padded - down_rows)))
        return value.reshape(rows, devices * down_padded)

    index = lax.axis_index("dp") * parts + rank
    gains = jnp.pad(jnp.stack([gain_attn, gain_mlp]).astype(F32), ((0, 6), (0, width - rows)))
    gains = jnp.roll(gains, index * rows, axis=1)
    wide = lambda value: stacked(value, 1)[0]
    padded_units = devices * down_padded
    if rows % 16 == 0:
        parted = [w_out, w_gate, w_up, w_down]
        shapes = [w_out.shape, *[(rows, padded_units)] * 2, (down_padded, width)]
    else:
        padded_down = jnp.pad(w_down, ((0, down_padded - down_rows), (0, 0)))
        parted = [wide(w_out), wide(spaced(w_gate)), wide(spaced(w_up)), wide(padded_down)]
        shapes = [value.shape for value in parted]
    pieces = Piece.all(shapes)
    upto = jnp.arange(lengths.shape[1])
    ends = jnp.sum(jnp.where(upto[:, None] >= upto[None, :], lengths, 0), axis=1)
    begins = ends - lengths[0]
    time = jnp.arange(tokens * parts, dtype=jnp.int32)
    inside = (time[:, None] >= begins[None, :]) & (time[:, None] < ends[None, :])
    start_all = jnp.sum(jnp.where(inside, begins[None, :], 0), axis=1)
    own_start = lax.dynamic_slice_in_dim(start_all, rank * tokens, tokens)
    position = (rank * tokens + jnp.arange(tokens, dtype=jnp.int32) - own_start).astype(F32)
    half = HEAD_DIM // 2
    angles = position[:, None] * THETA ** (-jnp.arange(half, dtype=F32) * 2.0 / HEAD_DIM)
    cosine = jnp.tile(jnp.cos(angles), (1, 4))
    sine = jnp.sin(angles)
    sine = jnp.tile(jnp.concatenate([-sine, sine], axis=1), (1, 2))
    start = start_all.reshape(parts, 1, tokens)

    x_low = inputs.reshape(tokens, width)
    (q, k, v, hidden_in), gains, fulls, helds = opening(
        x_low, first_values.reshape(tokens, width), cosine, sine, gains,
        [wide(w_query), wide(w_key), wide(w_value)], parted, shapes, pieces, parts, 3,
    )
    tall = lambda value: unstacked(value, rows)
    query_full, key_full, value_full = (tall(value) for value in fulls)
    gain_one, gain_two = gains[0], gains[1]
    (q_all, k_all, v_all, o_all, lse_all, attended), (*weights, down_full) = attend(
        q, k, v, start, helds, pieces, shapes
    )
    out_full, gate_full, up_full = (tall(value) for value in weights)
    down_full = unstacked(down_full, down_padded)
    output, grad_middle, d_att, grad_out, grad_gate, grad_up, grad_down, grad_gain_two = between(
        x_low, attended, cotangent.reshape(tokens, width), out_full, gain_two[None],
        gate_full, up_full, down_full,
    )

    share = lambda grad: stacked(grad.astype(BF16), devices)
    (dq, dk, dv), helds = attend_back(
        d_att, q_all, k_all, v_all, o_all, lse_all, start,
        [share(grad_out), share(grad_gate), share(grad_up), share(grad_down)], pieces,
    )
    (
        grad_first, grad_x, gains_total, total_query, total_key, total_value,
        total_out, total_gate, total_up, total_down,
    ) = closing(
        (dq, dk, dv), (query_full, key_full, value_full), hidden_in, x_low, grad_middle,
        grad_gain_two, cosine, sine, gain_one[None], rows, helds, pieces, shapes, 4,
    )
    own_gain = lambda n: lax.dynamic_slice_in_dim(gains_total[n], index * rows, rows)
    if rows % 16 == 0:
        grad_first, grad_x, total_gate, total_up, total_down, *totals = settle(
            grad_first, grad_x, total_gate, total_up, total_down,
            (total_query, total_key, total_value, total_out), down_rows,
        )
    else:
        low = lambda total: unstacked(total[None], rows)
        close = lambda total: low(total).reshape(rows, devices, down_padded)[:, :, :down_rows]
        total_gate, total_up = (
            close(total).reshape(rows, devices * down_rows) for total in (total_gate, total_up)
        )
        total_down = unstacked(total_down[None], down_padded)[:down_rows]
        totals = [low(total) for total in (total_query, total_key, total_value, total_out)]
        grad_first = grad_first.astype(F32)
    return (
        output.reshape(inputs.shape),
        grad_x.reshape(inputs.shape),
        grad_first.reshape(inputs.shape),
        *totals,
        own_gain(0),
        total_gate,
        total_up,
        total_down,
        own_gain(1),
    )


def solution(mesh):
    tokens = P("dp", "seq", None)
    matrix = P(("dp", "seq"), None)
    vector = P(("dp", "seq"))
    return jax.shard_map(
        shards,
        mesh=mesh,
        in_specs=(
            tokens, tokens, P("dp", None), matrix, matrix, matrix, matrix, vector,
            matrix, matrix, matrix, vector, tokens,
        ),
        out_specs=(
            tokens, tokens, tokens, matrix, matrix, matrix, matrix, vector,
            matrix, matrix, matrix, vector,
        ),
        check_vma=False,
    )
```

```python
import functools

import jax
import jax.numpy as jnp
from jax import lax
from jax.experimental import pallas as pl
from jax.experimental.pallas import tpu as pltpu
from jax.sharding import PartitionSpec as P

HEAD_DIM = 64
EPS = 1e-06
THETA = 10000.0
NEG = -1e30
MESH = pl.DeviceIdType.MESH
BF16 = jnp.bfloat16
F32 = jnp.float32
VMEM = pltpu.VMEM
MIB = 1 << 20


def dot(left, right, left_dim=1, right_dim=0):
    return lax.dot_general(
        left, right, (((left_dim,), (right_dim,)), ((), ())), preferred_element_type=F32
    )


def across(left, right):
    return dot(left, right, 0, 0)


def against(left, right):
    return dot(left, right, 1, 1)


def norm_back(grad_normed, values, gain):
    scale_inv = lax.rsqrt(jnp.mean(values * values, axis=-1, keepdims=True) + EPS)
    normed = values * scale_inv
    grad_scaled = grad_normed * gain
    grad_values = scale_inv * (
        grad_scaled - normed * jnp.mean(grad_scaled * normed, axis=-1, keepdims=True)
    )
    grad_gain = jnp.sum(grad_normed * normed, axis=0)
    return (grad_values, grad_gain)


def turned(values, cosine, sine):
    lane = lax.broadcasted_iota(jnp.int32, values.shape, 1) % HEAD_DIM
    other = jnp.where(
        lane < HEAD_DIM // 2,
        pltpu.roll(values, 128 - HEAD_DIM // 2, 1),
        pltpu.roll(values, HEAD_DIM // 2, 1),
    )
    return values * cosine + other * sine


def greet(parts, me):
    barrier = pltpu.get_barrier_semaphore()
    for step in range(1, parts):
        pl.semaphore_signal(
            barrier, 1, device_id={"seq": lax.rem(me + step, parts)}, device_id_type=MESH
        )
    return parts - 1


def send(source, target, send_sem, recv_sem, peer):
    return pltpu.make_async_remote_copy(
        src_ref=source,
        dst_ref=target,
        send_sem=send_sem,
        recv_sem=recv_sem,
        device_id={"seq": peer},
        device_id_type=MESH,
    )


def arrive(ref, sem):
    pltpu.make_async_copy(ref, ref, sem).wait()


def own_head(values, head, width):
    if width == HEAD_DIM:
        return values
    lane = lax.broadcasted_iota(jnp.int32, values.shape, 1)
    return jnp.where(lane // HEAD_DIM == head, values, jnp.zeros_like(values))


def allowed_tile(i, j, tokens, start):
    key = j * tokens + lax.broadcasted_iota(jnp.int32, (tokens, tokens), 0)
    query = i * tokens + lax.broadcasted_iota(jnp.int32, (tokens, tokens), 1)
    return (key <= query) & (key >= start[i])


def forward_kernel(
    parts, heads, pieces, count,
    q_in, k_in, v_in, start, *refs,
):
    helds, refs = refs[: len(pieces)], refs[len(pieces) :]
    kept, (lse_all, attended), refs = refs[:4], refs[4:6], refs[6:]
    fulls, refs = refs[:count], refs[count:]
    q_all, k_all, v_all, o_all, keep, *refs = refs
    v_turn, total, o_send, in_send, in_recv, o_out, o_in, *sems = refs
    place = Place()
    _, tokens, width = q_in.shape
    half = parts // 2
    me = lax.axis_index("seq")
    own = me // half
    place.greet(greet(parts, me))
    spread = WeightSpread(place, pieces, helds, fulls, sems)
    pairs = ((q_in, q_all), (k_in, k_all), (v_in, v_all))

    def moved(index, peer):
        source, target = pairs[index]
        return send(
            source.at[peer], target.at[me], in_send.at[index, peer], in_recv.at[index, me], peer
        )

    def over(first, action):
        def body(step, _):
            action(first + lax.rem(me + step, half))
            return 0

        lax.fori_loop(0, half, body, 0)

    def start_cross(indices):
        over((1 - own) * half, lambda peer: [moved(index, peer).start() for index in indices])

    def sent_cross(indices):
        over((1 - own) * half, lambda peer: [moved(index, peer).wait_send() for index in indices])

    for index, (source, target) in enumerate(pairs):
        pltpu.make_async_copy(source.at[me], target.at[me], in_recv.at[index, me]).start()
    def start_near(peer):
        @pl.when(peer != me)
        def _():
            for index in range(3):
                moved(index, peer).start()

    over(own * half, start_near)
    pl.when(own == 0)(lambda: start_cross((1, 2)))
    pl.when(own == 1)(lambda: start_cross((0,)))

    def got(index, block):
        arrive(pairs[index][1].at[block], in_recv.at[index, block])

    def got_keys(block):
        got(1, block)
        got(2, block)
        v_turn[block] = v_all[block].T

    def tile(i, j, masked):
        if masked:
            allowed = allowed_tile(i, j, tokens, start)
        queries, keys = q_all[i], k_all[j]
        for head in range(heads):
            rows = slice(head * HEAD_DIM, (head + 1) * HEAD_DIM)
            scores = against(keys, own_head(queries, head, width))
            if masked:
                scores = jnp.where(allowed, scores, NEG)
            old = lse_all[i, head]
            new = jnp.maximum(old, jnp.max(scores, axis=0, keepdims=True))
            weights = jnp.exp(scores - new)
            factor = jnp.exp(old - new)
            lse_all[i, head] = new
            total[i, head] = total[i, head] * factor + jnp.sum(weights, axis=0, keepdims=True)
            o_all[i, rows] = o_all[i, rows] * factor + dot(
                v_turn[j, rows], weights.astype(BF16)
            )

    def tile_row(row, _):
        phase, place_in = row // half, lax.rem(row, half)
        lower = jnp.where(phase == 0, own, 1 - own) * half
        i = jnp.where(phase == 1, half, lower) + place_in
        first = jnp.where(phase == 1, 0, lower)
        last = jnp.where(phase == 1, half, i + 1)
        spread.at_row(row, 3 * half)

        @pl.when(phase == 0)
        def _():
            got(0, i)
            got_keys(i)

        @pl.when((row == half) & (own == 0))
        def _():
            lax.fori_loop(half, parts, lambda block, _: got(0, block) or 0, 0)

        @pl.when((row == half) & (own == 1))
        def _():
            lax.fori_loop(0, half, lambda block, _: got_keys(block) or 0, 0)

        @pl.when((row == half * 3 // 4) & (own == 1))
        def _():
            sent_cross((0,))
            start_cross((1, 2))

        @pl.when((row == half + half // 2) & (own == 0))
        def _():
            sent_cross((1, 2))
            start_cross((0,))

        @pl.when((phase == 2) & (own == 0))
        def _():
            got_keys(i)

        @pl.when((phase == 2) & (own == 1))
        def _():
            got(0, i)

        @pl.when((phase == 0) | ((phase == 1) & (own == 0)) | ((phase == 2) & (own == 1)))
        def _():
            lse_all[i] = jnp.full(lse_all.shape[1:], NEG, F32)
            total[i] = jnp.zeros(total.shape[1:], F32)
            o_all[i] = jnp.zeros(o_all.shape[1:], F32)

        def key_block(j, _):
            masked = (j == 0) | (j == i) | (i == parts - 1)
            pl.when(masked)(lambda: tile(i, j, True))
            pl.when(jnp.logical_not(masked))(lambda: tile(i, j, False))
            return 0

        lax.fori_loop(first, last, key_block, 0)

        @pl.when(((phase == 0) & (own == 0)) | ((phase == 1) & (own == 1)) | (phase == 2))
        def _():
            for head in range(heads):
                rows = slice(head * HEAD_DIM, (head + 1) * HEAD_DIM)
                o_all[i, rows] = o_all[i, rows] / total[i, head]
                lse_all[i, head] = lse_all[i, head] + jnp.log(total[i, head])
            o_send[i] = o_all[i].T.astype(BF16)

            @pl.when(i == me)
            def _():
                pltpu.make_async_copy(o_send.at[i], attended.at[me], o_in.at[me]).start()

            @pl.when(i != me)
            def _():
                send(o_send.at[i], attended.at[me], o_out.at[i], o_in.at[me], i).start()

        return 0

    lax.fori_loop(0, 3 * half, tile_row, 0)
    keeps = [
        pltpu.make_async_copy(source, target, keep.at[n])
        for n, (source, target) in enumerate(zip((q_all, k_all, v_all, o_all), kept))
    ]
    for copy in keeps:
        copy.start()
    spread.finish()
    pl.when(own == 0)(lambda: sent_cross((0,)))
    pl.when(own == 1)(lambda: sent_cross((1, 2)))

    def sent_near(peer):
        @pl.when(peer != me)
        def _():
            for index in range(3):
                moved(index, peer).wait_send()

    over(own * half, sent_near)

    def finish(step, _):
        peer = lax.rem(me + step, parts)
        arrive(o_send.at[peer], o_out.at[peer])
        arrive(attended.at[peer], o_in.at[peer])
        return 0

    lax.fori_loop(1, parts, finish, 0)
    arrive(attended.at[me], o_in.at[me])
    for copy in keeps:
        copy.wait()


def attend(q, k, v, start, helds, pieces, shapes):
    parts, tokens, width = q.shape
    heads = width // HEAD_DIM
    place = Place()
    whole = pl.BlockSpec(memory_space=VMEM)
    far = pl.BlockSpec(memory_space=pl.ANY)
    split = jax.ShapeDtypeStruct(q.shape, BF16)
    flops = 4 * parts * parts * tokens * tokens * width // 2
    fulls = [
        jax.ShapeDtypeStruct((place.xs, 2, place.as_, place.bs, *shape), BF16) for shape in shapes
    ]
    results = pl.pallas_call(
        functools.partial(forward_kernel, parts, heads, pieces, len(shapes)),
        in_specs=[far] * 3 + [whole] * (1 + len(pieces)),
        out_specs=[far] * 4 + [whole] * 2 + [far] * len(shapes),
        out_shape=[
            split,
            split,
            split,
            jax.ShapeDtypeStruct((parts, width, tokens), F32),
            jax.ShapeDtypeStruct((parts, heads, 1, tokens), F32),
            split,
            *fulls,
        ],
        scratch_shapes=[
            *[VMEM(split.shape, BF16)] * 3,
            VMEM((parts, width, tokens), F32),
            pltpu.SemaphoreType.DMA((4,)),
            VMEM((parts, width, tokens), BF16),
            VMEM((parts, heads, 1, tokens), F32),
            VMEM((parts, tokens, width), BF16),
            pltpu.SemaphoreType.DMA((3, parts)),
            pltpu.SemaphoreType.DMA((3, parts)),
            pltpu.SemaphoreType.DMA((parts,)),
            pltpu.SemaphoreType.DMA((parts,)),
            *[spread_semaphores(place)] * len(pieces),
        ],
        compiler_params=pltpu.CompilerParams(
            collective_id=1, has_side_effects=True, vmem_limit_bytes=48 * MIB
        ),
        cost_estimate=pl.CostEstimate(
            flops=4 * flops, bytes_accessed=16 * q.size, transcendentals=flops // 256
        ),
        name="attend",
    )(q, k, v, start, *helds)
    devices = place.xs * 2 * place.as_ * place.bs
    weights = [value.reshape(devices, *value.shape[4:]) for value in results[6:]]
    return results[:6], weights


def backward_kernel(
    parts, heads, pieces, count,
    d_in, q_kept, k_kept, v_kept, o_kept, lse_all, start, *refs,
):
    grads, refs = refs[:count], refs[count:]
    (dq_got, dk_got, dv_got), refs = refs[:3], refs[3:]
    results, refs = refs[: len(pieces)], refs[len(pieces) :]
    q_all, k_all, v_all, o_all, keep, *refs = refs
    d_all, k_turn, delta, dq_turn, dk_sum, dv_sum, dq_send, dk_send, dv_send = refs[:9]
    in_send, in_recv, out_send, out_recv, *buffers = refs[9:]
    place = Place()
    _, tokens, width = d_in.shape
    half = parts // 2
    me = lax.axis_index("seq")
    own = me // half
    keeps = [
        pltpu.make_async_copy(source, target, keep.at[n])
        for n, (source, target) in enumerate(
            zip((q_kept, k_kept, v_kept, o_kept), (q_all, k_all, v_all, o_all))
        )
    ]
    for copy in keeps:
        copy.start()
    place.greet(greet(parts, me))
    adding = GradSums(place, pieces, grads, results, buffers)

    def over(first, action):
        def body(step, _):
            action(first + lax.rem(me + step, half))
            return 0

        lax.fori_loop(0, half, body, 0)

    def moved(peer):
        return send(d_in.at[peer], d_all.at[me], in_send.at[peer], in_recv.at[me], peer)

    pltpu.make_async_copy(d_in.at[me], d_all.at[me], in_recv.at[me]).start()

    def start_near(peer):
        pl.when(peer != me)(lambda: moved(peer).start())

    over(own * half, start_near)
    over((1 - own) * half, lambda peer: moved(peer).start())
    sends = ((dq_send, dq_got), (dk_send, dk_got), (dv_send, dv_got))

    def give(index, block):
        source, target = sends[index]

        @pl.when(block == me)
        def _():
            pltpu.make_async_copy(
                source.at[block], target.at[me], out_recv.at[index, me]
            ).start()

        @pl.when(block != me)
        def _():
            send(
                source.at[block], target.at[me],
                out_send.at[index, block], out_recv.at[index, me], block,
            ).start()

    def give_query(i):
        dq_send[i] = (dq_turn[i] * HEAD_DIM**-0.5).T.astype(BF16)
        give(0, i)

    def give_keys(j):
        dk_send[j] = dk_sum[j].astype(BF16)
        dv_send[j] = dv_sum[j].astype(BF16)
        give(1, j)
        give(2, j)

    def tile(i, j, masked):
        if masked:
            allowed = allowed_tile(i, j, tokens, start)
        queries, grads_out, keys, mixed = q_all[i], d_all[i], k_all[j], v_all[j]
        for head in range(heads):
            rows = slice(head * HEAD_DIM, (head + 1) * HEAD_DIM)
            query, grad = own_head(queries, head, width), own_head(grads_out, head, width)
            scores = against(keys, query)
            if masked:
                scores = jnp.where(allowed, scores, NEG)
            weights = jnp.exp(scores - lse_all[i, head])
            dv_sum[j] += dot(weights.astype(BF16), grad)
            slope = against(mixed, grad) - delta[i, head]
            d_scores = (weights * slope).astype(BF16)
            dk_sum[j] += dot(d_scores, query)
            dq_turn[i, rows] += dot(k_turn[j, rows], d_scores)

    def prepare(block):
        arrive(d_all.at[block], in_recv.at[block])
        product = d_all[block].astype(F32).T * o_all[block]
        for head in range(heads):
            rows = slice(head * HEAD_DIM, (head + 1) * HEAD_DIM)
            delta[block, head] = jnp.sum(product[rows], axis=0, keepdims=True)
        k_turn[block] = k_all[block].T
        dq_turn[block] = jnp.zeros(dq_turn.shape[1:], F32)
        dk_sum[block] = jnp.zeros(dk_sum.shape[1:], F32)
        dv_sum[block] = jnp.zeros(dv_sum.shape[1:], F32)

    def tile_row(row, _):
        phase, place_in = row // half, lax.rem(row, half)
        adding.at_row(row, 3 * half)

        @pl.when(row == 0)
        def _():
            lax.fori_loop(0, half, lambda n, _: prepare(own * half + n) or 0, 0)

        @pl.when(row == half)
        def _():
            lax.fori_loop(0, half, lambda n, _: prepare((1 - own) * half + n) or 0, 0)

        by_query = jnp.where(phase == 1, own == 1, own == 0)
        lower = jnp.where(phase == 0, own, 1 - own) * half
        outer = jnp.where(
            phase == 2, jnp.where(by_query, half, 0), lower
        ) + place_in
        first = jnp.where(phase == 2, jnp.where(by_query, 0, half), jnp.where(by_query, lower, outer))
        last = jnp.where(
            phase == 2,
            jnp.where(by_query, half, parts),
            jnp.where(by_query, outer + 1, lower + half),
        )

        def inner_block(inner, _):
            i, j = jnp.where(by_query, outer, inner), jnp.where(by_query, inner, outer)
            masked = (j == 0) | (j == i) | (i == parts - 1)
            pl.when(masked)(lambda: tile(i, j, True))
            pl.when(jnp.logical_not(masked))(lambda: tile(i, j, False))
            return 0

        lax.fori_loop(first, last, inner_block, 0)
        pl.when(by_query)(lambda: give_query(outer))
        pl.when(jnp.logical_not(by_query))(lambda: give_keys(outer))
        return 0

    for copy in keeps:
        copy.wait()
    lax.fori_loop(0, 3 * half, tile_row, 0)
    pl.when(own == 0)(lambda: over(0, give_keys))
    pl.when(own == 1)(lambda: over(half, give_query))
    adding.finish()

    def finish(step, _):
        peer = lax.rem(me + step, parts)
        moved(peer).wait_send()
        for index, (source, target) in enumerate(sends):
            arrive(source.at[peer], out_send.at[index, peer])
            arrive(target.at[peer], out_recv.at[index, peer])
        return 0

    lax.fori_loop(1, parts, finish, 0)
    for index, (_, target) in enumerate(sends):
        arrive(target.at[me], out_recv.at[index, me])


def attend_back(d_att, q, k, v, o, lse, start, grads, pieces):
    parts, tokens, width = q.shape
    heads = width // HEAD_DIM
    place = Place()
    whole = pl.BlockSpec(memory_space=VMEM)
    far = pl.BlockSpec(memory_space=pl.ANY)
    split = jax.ShapeDtypeStruct(q.shape, BF16)
    flops = 10 * parts * parts * tokens * tokens * width // 2
    sum_shapes = [piece.held(place, grads[piece.array].shape[1]) for piece in pieces]
    sum_scratch = GradSums.scratch(place, pieces, grads)
    grads = [placed(place, grad) for grad in grads]
    results = pl.pallas_call(
        functools.partial(backward_kernel, parts, heads, pieces, len(grads)),
        in_specs=[far] * 5 + [whole] * 2 + [far] * len(grads),
        out_specs=[far] * 3 + [far] * len(pieces),
        out_shape=[split] * 3 + sum_shapes,
        scratch_shapes=[
            *[VMEM(split.shape, BF16)] * 3,
            VMEM((parts, width, tokens), F32),
            pltpu.SemaphoreType.DMA((4,)),
            VMEM((parts, tokens, width), BF16),
            VMEM((parts, width, tokens), BF16),
            VMEM((parts, heads, 1, tokens), F32),
            VMEM((parts, width, tokens), F32),
            VMEM((parts, tokens, width), F32),
            VMEM((parts, tokens, width), F32),
            VMEM((parts, tokens, width), BF16),
            VMEM((parts, tokens, width), BF16),
            VMEM((parts, tokens, width), BF16),
            pltpu.SemaphoreType.DMA((parts,)),
            pltpu.SemaphoreType.DMA((parts,)),
            pltpu.SemaphoreType.DMA((3, parts)),
            pltpu.SemaphoreType.DMA((3, parts)),
            *sum_scratch,
        ],
        compiler_params=pltpu.CompilerParams(
            collective_id=2, has_side_effects=True, vmem_limit_bytes=60 * MIB
        ),
        cost_estimate=pl.CostEstimate(
            flops=4 * flops, bytes_accessed=20 * q.size, transcendentals=flops // 640
        ),
        name="attend_back",
    )(d_att, q, k, v, o, lse, start, *grads)
    return results[:3], results[3:]


class Place:
    def __init__(self):
        self.xs = lax.axis_size("dp") // 2
        seq = lax.axis_size("seq")
        self.bs = 2 if seq <= 8 else 4
        self.as_ = seq // self.bs
        dp, rank = lax.axis_index("dp"), lax.axis_index("seq")
        self.x, self.core = dp // 2, lax.rem(dp, 2)
        self.a, self.b = rank // self.bs, lax.rem(rank, self.bs)

    def device(self, x=None, core=None, a=None, b=None):
        x, core = (self.x if x is None else x), (self.core if core is None else core)
        a, b = (self.a if a is None else a), (self.b if b is None else b)
        return (x * 2 + core, a * self.bs + b)

    def peers(self, axis):
        size = {"x": self.xs, "a": self.as_, "b": self.bs}[axis]
        own = getattr(self, axis)
        return [(step - 1, lax.rem(own + step, size)) for step in range(1, size)]

    def greet(self, greeted=0):
        barrier = pltpu.get_barrier_semaphore()
        others = [self.device(core=1 - self.core)]
        for axis in "x" if greeted else "xab":
            others += [self.device(**{axis: index}) for _, index in self.peers(axis)]
        for other in others:
            pl.semaphore_signal(barrier, 1, device_id=other, device_id_type=MESH)
        pl.semaphore_wait(barrier, len(others) + greeted)

    @property
    def inner(self):
        return (self.a == 1) | (self.a == 2)

    @property
    def beside(self):
        return self.a + 1 - 2 * lax.rem(self.a, 2)


def column_pieces(columns, wanted):
    tiles = columns // 128
    wanted = min(wanted, tiles)
    edges = [tiles * n // wanted * 128 for n in range(wanted)] + [columns]
    return [(edges[n], edges[n + 1] - edges[n]) for n in range(wanted)]


def placed(place, value):
    return value.reshape(place.xs, 2, place.as_, place.bs, *value.shape[1:])


def remote(source, target, send_sem, recv_sem, device):
    return pltpu.make_async_remote_copy(
        src_ref=source,
        dst_ref=target,
        send_sem=send_sem,
        recv_sem=recv_sem,
        device_id=device,
        device_id_type=MESH,
    )


def flat(ref):
    rows, columns = ref.shape[-2:]
    return ref.reshape(ref.size // (rows * columns), rows, columns)


class Relay:
    def __init__(self, place, source, target, sems):
        self.p, self.source, self.target, self.sems = place, source, target, sems
        assert place.as_ == 4

    def near(self):
        p = self.p
        return remote(
            self.source, self.target.at[p.a],
            self.sems.at[0, 0], self.sems.at[1, 0], p.device(a=p.beside),
        )

    def middle(self):
        p = self.p
        held = self.target.at[pl.ds(p.a // 2 * 2, 2)]
        return remote(
            held, held, self.sems.at[0, 1], self.sems.at[1, 1], p.device(a=3 - p.a)
        )

    def outward(self):
        p = self.p
        held = self.target.at[pl.ds((1 - p.a // 2) * 2, 2)]
        return remote(
            held, held, self.sems.at[0, 2], self.sems.at[1, 1], p.device(a=p.beside)
        )

    def local(self):
        return pltpu.make_async_copy(self.source, self.target.at[self.p.a], self.sems.at[1, 2])

    def step(self, number):
        if number == 0:
            self.local().start()
            self.near().start()
        elif number == 1:
            self.local().wait()
            self.near().wait_recv()
            pl.when(self.p.inner)(lambda: self.middle().start())
        elif number == 2:

            @pl.when(self.p.inner)
            def _():
                self.middle().wait_recv()
                self.outward().start()
        else:

            @pl.when(jnp.logical_not(self.p.inner))
            def _():
                self.middle().wait_recv()

            @pl.when(self.p.inner)
            def _():
                self.middle().wait_send()
                self.outward().wait_send()

            self.near().wait_send()


class Direct:
    def __init__(self, place, source, target, sems):
        self.p, self.source, self.target, self.sems = place, source, target, sems

    def copies(self):
        p = self.p
        return [
            remote(
                self.source, self.target.at[p.a],
                self.sems.at[0, s], self.sems.at[1, s], p.device(a=index),
            )
            for s, index in p.peers("a")
        ]

    def local(self):
        return pltpu.make_async_copy(self.source, self.target.at[self.p.a], self.sems.at[0, 3])

    def step(self, number):
        if number == 0:
            self.local().start()
            for copy in self.copies():
                copy.start()
        elif number == 3:
            self.local().wait()
            for copy in self.copies():
                copy.wait()


class Piece:
    def __init__(self, array, start, size, order, deep):
        self.array, self.start, self.size, self.order, self.deep = array, start, size, order, deep

    @staticmethod
    def all(shapes):
        pieces = []
        for array, kinds in enumerate(
            ([("bx", 0)], [("bx", 1)] * 2, [("xb", 1), ("bx", 1)], [("bx", 0)] * 2)
        ):
            for (start, size), kind in zip(column_pieces(shapes[array][1], len(kinds)), kinds):
                pieces.append(Piece(array, start, size, *kind))
        return pieces

    def held(self, place, rows):
        lead = {"": (), "b": (place.bs,), "x": (place.xs,)}[self.order[0] if self.deep else ""]
        lead = (*lead, place.as_) if self.order[0] == "x" else (place.as_, *lead)
        return jax.ShapeDtypeStruct((*lead, rows, self.size), BF16)

    def along_a(self, place, held):
        if not self.deep:
            return held
        return held.at[place.x] if self.order[0] == "x" else held.at[:, place.b]

    def columns(self, ref):
        return ref.at[(slice(None),) * (len(ref.shape) - 1) + (pl.ds(self.start, self.size),)]


class Spread:
    def __init__(self, place, views, order, sems, source=None, first=0):
        self.place, self.views, self.order, self.sems = place, views, order, sems
        self.source, self.first = source, first

    @staticmethod
    def views_of(place, full, order):
        p = place
        middle = full.at[:, p.core, :, p.b] if order == "xb" else full.at[p.x, p.core]
        return full.at[p.x, p.core, :, p.b], middle, full.at[:, p.core]

    def copies(self, number):
        p, view = self.place, self.views[number]
        source = self.source if self.source is not None and number == self.first else view
        base = sum([len(p.peers(axis)) for axis in self.order][:number])
        if number == 2:
            devices = [(0, p.device(core=1 - p.core))]
        else:
            axis = self.order[number]
            devices = [(s, p.device(**{axis: index})) for s, index in p.peers(axis)]
        return [
            remote(source, view, self.sems.at[0, base + s], self.sems.at[1, base + s], device)
            for s, device in devices
        ]

    def local(self):
        return pltpu.make_async_copy(self.source, self.views[self.first], self.sems.at[2, 0])

    def start(self, number):
        if self.source is not None and number == self.first:
            self.local().start()
        for copy in self.copies(number):
            copy.start()

    def finish(self, number):
        if self.source is not None and number == self.first:
            self.local().wait()
        for copy in self.copies(number):
            copy.wait_recv()
            copy.wait_send()

    def then(self, number):
        self.finish(number)
        if number < 2:
            self.start(number + 1)


def spread_semaphores(place):
    return pltpu.SemaphoreType.DMA((3, place.xs + place.bs - 1))


RELAY_SEMAPHORES = (2, 4)


class InRows:
    def at_row(self, row, count):
        for at in sorted({at for at, _ in self.actions() if at < 12}):

            @pl.when(row == at * count // 12)
            def _():
                for own_row, action in self.actions():
                    if own_row == at:
                        action()

    def finish(self):
        for at, action in self.actions():
            if at >= 12:
                action()


class WeightSpread(InRows):
    def __init__(self, place, pieces, sources, fulls, sems):
        self.units = []
        for piece, source, own_sems in zip(pieces, sources, sems):
            full = piece.columns(fulls[piece.array])
            views = Spread.views_of(place, full, piece.order)
            self.units.append(Spread(place, views, piece.order, own_sems, source, piece.deep))

    def actions(self):
        out, gate0, gate1, up0, up1, down0, down1 = self.units
        start = lambda unit: functools.partial(unit.start, unit.first)
        then = lambda unit, number: functools.partial(unit.then, number)
        done = [(0, start(unit)) for unit in (gate0, down0, gate1, down1, up1, out, up0)]
        done += [(4, then(down0, 0)), (5, then(down1, 0)), (6, then(out, 0))]
        done += [(7, then(gate0, 1)), (8, then(gate1, 1)), (9, then(up0, 1)), (10, then(up1, 1))]
        done += [(12, then(unit, 1)) for unit in (down0, down1, out)]
        done += [(12, then(unit, 2)) for unit in (gate0, gate1, up0, up1, down0, down1, out)]
        return done


class TotalSum:
    def __init__(self, place, mine, got, sems):
        self.place, self.mine, self.got, self.sems = place, mine, got, sems

    def slots(self, number):
        p = self.place
        devices = [[p.device(core=1 - p.core)]]
        devices += [[p.device(**{axis: index}) for _, index in p.peers(axis)] for axis in "xba"]
        return sum(len(some) for some in devices[:number]), devices[number]

    def copies(self, number):
        base, devices = self.slots(number)
        return [
            remote(
                self.mine, self.got.at[base + n],
                self.sems.at[0, base + n], self.sems.at[1, base + n], device,
            )
            for n, device in enumerate(devices)
        ]

    def start(self, number):
        for copy in self.copies(number):
            copy.start()

    def then(self, number):
        for copy in self.copies(number):
            copy.wait()
        base, devices = self.slots(number)
        for slot in range(len(devices)):
            self.mine[...] += self.got[base + slot]
        if number < 3:
            self.start(number + 1)


def opening_kernel(
    plan, pieces, parted, padded,
    x, first, cosine, sine, gains, w_query, w_key, w_value, *refs,
):
    shares, refs = refs[:parted], refs[parted:]
    (q_out, k_out, v_out, hidden, gains_total), kept, refs = refs[:5], refs[5:8], refs[8:]
    helds, refs = refs[: len(pieces)], refs[len(pieces) :]
    fulls, (keep, got_gains, gain_sems, relay_sems, *refs) = refs[:3], refs[3:]
    spaced, sems = refs[:padded], refs[padded:]
    given, shares = shares, [*shares[: parted - padded], *spaced]
    place = Place()
    parts, tokens, width = q_out.shape
    dim = parts * width
    place.greet()
    gains_total[...] = gains[...]
    total = TotalSum(place, gains_total, got_gains, gain_sems)
    units, relays = [], []
    sources = (w_query, w_key, w_value)
    for number, (array, start, size, order) in enumerate(plan):
        views = Spread.views_of(place, fulls[array].at[:, :, :, :, :, pl.ds(start, size)], order)
        relays.append(
            Direct(place, sources[array].at[:, pl.ds(start, size)], views[0], relay_sems.at[number])
        )
        units.append(Spread(place, views, order, sems[number]))
    deep, flat_relays, deep_relays = [], [], []
    for number, (piece, held) in enumerate(zip(pieces, helds)):
        view = piece.along_a(place, held)
        index = len(plan) + number
        relay = Relay(place, piece.columns(shares[piece.array]), view, relay_sems.at[index])
        (deep_relays if piece.deep else flat_relays).append(relay)
        if piece.deep:
            deep.append(Spread(place, [view], piece.order, sems[index]))

    def step(group, number):
        for relay in group:
            relay.step(number)

    def then(some, number):
        for unit in some:
            unit.then(number)

    def weight(array, start, size):
        full = fulls[array]
        rows, columns = full.shape[-2:]
        fold = dim // columns
        value = full[:, :, :, :, :, start % columns : start % columns + size]
        if fold > 1:
            share = rows // fold
            part = start // columns * share
            value = value.astype(F32)[:, :, :, :, part : part + share]
        return value.reshape(dim, size).astype(BF16)

    def project(array):
        for start in range(0, dim, 256):
            raw = dot(hidden[...], weight(array, start, 256))
            if array == 2:
                raw = 0.5 * raw + 0.5 * first[:, start : start + 256].astype(F32)
            for begin in range(0, 256, 128):
                value = raw[:, begin : begin + 128]
                if array < 2:
                    value = turned(value, cosine[...], sine[...])
                if array == 0:
                    value = value * HEAD_DIM**-0.5
                for lane in range(0, 128, width):
                    out = (q_out, k_out, v_out)[array]
                    out[(start + begin + lane) // width] = value[:, lane : lane + width].astype(BF16)

    half = len(units) // 2
    line = deep_relays + flat_relays

    def tick(number):
        for back in (3, 2, 1, 0):
            index = number - back
            if 0 <= index < len(line):
                line[index].step(back)
                if back == 3 and index < len(deep):
                    deep[index].start(0)

    step(relays, 0)
    total.start(0)
    if padded:
        *wides, tall = given[parted - padded :]
        for source, target in zip(wides, spaced):
            share = tall.shape[0]
            gap = spaced[-1].shape[0] - share
            value, gaps = source[...].astype(F32), jnp.zeros((source.shape[0], gap), F32)
            parts_of = [value[:, n : n + share] for n in range(0, value.shape[1], share)]
            target[...] = jnp.concatenate(
                [part for value in parts_of for part in (value, gaps)], axis=1
            ).astype(BF16)
        gaps = jnp.zeros((gap, tall.shape[1]), F32)
        spaced[-1][...] = jnp.concatenate([tall[...].astype(F32), gaps], axis=0).astype(BF16)
    step(relays, 1)
    tick(0)
    step(relays, 2)
    total.then(0)
    for relay, unit in zip(relays, units):
        relay.step(3)
        unit.start(0)
    tick(1)
    total.then(1)
    then(units[:half], 0)
    tick(2)
    then(units[half:], 0)
    total.then(2)
    tick(3)
    total.then(3)
    values = x[...].astype(F32)
    scale = lax.rsqrt(jnp.mean(values * values, axis=-1, keepdims=True) + EPS)
    hidden[...] = (values * scale * gains_total[0:1]).astype(BF16)
    tick(4)
    then(units[:half], 1)
    tick(5)
    then(units[half:], 1)
    keeps = []
    for array in range(3):
        then([unit for unit, piece in zip(units, plan) if piece[0] == array], 2)
        keeps.append(pltpu.make_async_copy(fulls[array], kept[array], keep.at[array]))
        keeps[array].start()
        project(array)
        tick(6 + array)
    for number in range(9, len(line) + 3):
        tick(number)
    for unit in deep:
        unit.finish(0)
    for copy in keeps:
        copy.wait()


def opening(
    x, first, cosine, sine, gains, weights, parted, shapes, pieces, parts, collective_id
):
    place = Place()
    xs, as_, bs = place.xs, place.as_, place.bs
    tokens, dim = x.shape
    plan = []
    for number, array in enumerate(weights):
        for start, size in column_pieces(array.shape[1], 2):
            plan.append((number, start, size, "xb" if len(plan) % 2 == 1 else "bx"))
    shape = jax.ShapeDtypeStruct
    near = [shape((parts, tokens, dim // parts), BF16)] * 3
    near += [shape((tokens, dim), BF16), shape(gains.shape, F32)]
    near += [shape((xs, 2, as_, bs, *array.shape), array.dtype) for array in weights]
    held = [piece.held(place, shapes[piece.array][0]) for piece in pieces]
    padded = sum(array.shape != shape for array, shape in zip(parted, shapes))
    ready = len(parted) - padded
    far, whole = pl.BlockSpec(memory_space=pl.ANY), pl.BlockSpec(memory_space=VMEM)
    count = len(plan) + len(pieces)
    peers = 1 + (xs - 1) + (bs - 1) + (as_ - 1)
    results = pl.pallas_call(
        functools.partial(opening_kernel, plan, pieces, len(parted), padded),
        in_specs=[whole] * 5 + [far] * (3 + ready) + [whole] * padded,
        out_specs=[whole] * 5 + [far] * 3 + [whole] * len(held),
        out_shape=near + held,
        scratch_shapes=[
            *[VMEM(each.shape, BF16) for each in near[5:]],
            pltpu.SemaphoreType.DMA((3,)),
            VMEM((peers, *gains.shape), F32),
            pltpu.SemaphoreType.DMA((2, peers)),
            pltpu.SemaphoreType.DMA((count, *RELAY_SEMAPHORES)),
            *[VMEM(shape, BF16) for shape in shapes[ready:]],
            *[spread_semaphores(place)] * count,
        ],
        compiler_params=pltpu.CompilerParams(
            collective_id=collective_id, has_side_effects=True, vmem_limit_bytes=48 * MIB
        ),
        cost_estimate=pl.CostEstimate(
            flops=6 * tokens * dim * dim, bytes_accessed=20 * dim * dim, transcendentals=0
        ),
        name="opening",
    )(x, first, cosine, sine, gains, *weights, *parted)
    devices = xs * 2 * as_ * bs
    fulls = [value.reshape(devices, *value.shape[4:]) for value in results[5:8]]
    return results[:4], results[4], fulls, results[8:]


def add_up(mine, others):
    lead = mine.shape[:-2]

    def at(ref, step):
        index = []
        for size in reversed(lead):
            index.insert(0, lax.rem(step, size))
            step = step // size
        return ref.at[tuple(index)]

    def body(step, _):
        total = at(mine, step)[...].astype(F32)
        for other in others:
            total += at(other, step)[...].astype(F32)
        at(mine, step)[...] = total.astype(mine.dtype)
        return 0

    count = 1
    for size in lead:
        count *= size
    lax.fori_loop(0, count, body, 0)


class RelaySum:
    def __init__(self, place, own, inward, middle, last, sems, result):
        self.p, self.own, self.sems, self.result = place, own, sems, result
        self.inward, self.middle, self.last = inward, middle, last
        assert place.as_ == 4

    def move(self, number):
        p = self.p
        far = self.own.at[pl.ds((1 - p.a // 2) * 2, 2)]
        if number == 0:
            source, target, device = far, self.inward, p.beside
        elif number == 1:
            source, target, device = far, self.middle, 3 - p.a
        else:
            source, target, device = self.own.at[p.beside], self.last, p.beside
        return remote(
            source, target, self.sems.at[0, number], self.sems.at[1, number], p.device(a=device)
        )

    def step(self, number):
        p, inner = self.p, self.p.inner
        outer = jnp.logical_not(inner)
        if number == 0:
            pl.when(outer)(lambda: self.move(0).start())
            pl.when(outer)(lambda: self.move(2).start())
        elif number == 1:

            @pl.when(inner)
            def _():
                self.move(0).wait_recv()
                add_up(self.own.at[pl.ds((1 - p.a // 2) * 2, 2)], [self.inward])
                self.move(1).start()
        elif number == 2:

            @pl.when(inner)
            def _():
                self.move(1).wait_recv()
                add_up(self.own.at[pl.ds(p.a // 2 * 2, 2)], [self.middle])
                self.move(2).start()
        else:
            self.move(2).wait_recv()
            self.result[...] = self.own[p.a].astype(F32) + self.last[...].astype(F32)
            pl.when(outer)(lambda: self.move(0).wait_send())
            pl.when(inner)(lambda: self.move(1).wait_send())
            self.move(2).wait_send()

    @staticmethod
    def scratch(rows, columns, dtype):
        return [
            VMEM((2, rows, columns), dtype),
            VMEM((2, rows, columns), dtype),
            VMEM((rows, columns), dtype),
            pltpu.SemaphoreType.DMA((2, 3)),
        ]


class DirectSum:
    def __init__(self, place, own, got, sems, result):
        self.p, self.own, self.got, self.sems, self.result = place, own, got, sems, result

    def copies(self):
        p = self.p
        return [
            remote(
                self.own.at[index], self.got.at[s],
                self.sems.at[0, s], self.sems.at[1, s], p.device(a=index),
            )
            for s, index in p.peers("a")
        ]

    def step(self, number):
        if number == 0:
            for copy in self.copies():
                copy.start()
        elif number == 3:
            total = self.own[self.p.a].astype(F32)
            for slot, copy in enumerate(self.copies()):
                copy.wait()
                total += self.got[slot].astype(F32)
            self.result[...] = total

    @staticmethod
    def scratch(place, rows, columns, dtype):
        return [
            VMEM((place.as_ - 1, rows, columns), dtype),
            pltpu.SemaphoreType.DMA((2, place.as_ - 1)),
        ]


class Sum:
    def __init__(self, place, source, order, buffers):
        self.place, self.order, self.source = place, order, source
        self.own, self.got0, self.got1, self.got2, self.sems = buffers
        self.copied = self.own is not None
        if not self.copied:
            self.own = source.at[:, place.core]

    @property
    def held(self):
        return self.own.at[self.place.x, :, self.place.b]

    @property
    def part(self):
        p = self.place
        return self.own.at[p.x] if self.order[0] == "x" else self.own.at[:, :, p.b]

    def moves(self, number):
        p = self.place
        if number == 0:
            return [(self.source.at[:, 1 - p.core], self.got0, 0, p.device(core=1 - p.core))]
        axis = self.order[number - 1]
        got = self.got1 if number == 1 else self.got2
        moves = []
        for slot, index in p.peers(axis):
            if axis == "x":
                piece = self.own.at[index] if number == 1 else self.own.at[index, :, p.b]
            else:
                piece = self.own.at[:, :, index] if number == 1 else self.own.at[p.x, :, index]
            moves.append((piece, got.at[slot], slot, p.device(**{axis: index})))
        return moves

    def copies(self, number):
        base = sum(([1] + [len(self.place.peers(axis)) for axis in self.order])[:number])
        return [
            remote(source, target, self.sems.at[0, base + s], self.sems.at[1, base + s], device)
            for source, target, s, device in self.moves(number)
        ]

    def local(self):
        return pltpu.make_async_copy(
            self.source.at[:, self.place.core], self.own, self.sems.at[2, 0]
        )

    def start(self, number):
        for copy in self.copies(number):
            copy.start()
        if number == 0 and self.copied:
            self.local().start()

    def finish(self, number):
        p = self.place
        if number == 0 and self.copied:
            self.local().wait()
        for copy in self.copies(number):
            copy.wait_recv()
            copy.wait_send()
        if number == 0:
            add_up(self.own, [self.got0])
        else:
            mine = self.held if number == 2 else self.part
            got = self.got1 if number == 1 else self.got2
            add_up(mine, [got.at[slot] for slot in range(len(p.peers(self.order[number - 1])))])

    @staticmethod
    def scratch(place, rows, size, order, dtype, copied=True):
        xs, as_, bs = place.xs, place.as_, place.bs
        shapes = {
            "x": ((xs - 1, as_, bs, rows, size), (xs - 1, as_, rows, size)),
            "b": ((bs - 1, xs, as_, rows, size), (bs - 1, as_, rows, size)),
        }
        return [VMEM((xs, as_, bs, rows, size), dtype)] * copied + [
            VMEM((xs, as_, bs, rows, size), dtype),
            VMEM(shapes[order[0]][0], dtype),
            VMEM(shapes[order[1]][1], dtype),
            pltpu.SemaphoreType.DMA((3, xs + bs - 1)),
        ]


class GradSums(InRows):
    def __init__(self, place, pieces, grads, results, buffers):
        self.units, self.outs = [], []
        for piece, result in zip(pieces, results):
            source = piece.columns(grads[piece.array])
            unit, buffers = Sum(place, source, piece.order[::-1], buffers[:5]), buffers[5:]
            self.units.append(unit)
            self.outs.append((unit.part if piece.deep else unit.held, result))

    @staticmethod
    def scratch(place, pieces, grads):
        return [
            item
            for piece in pieces
            for item in Sum.scratch(
                place, grads[piece.array].shape[1], piece.size, piece.order[::-1], BF16
            )
        ]

    def actions(self):
        out, gate0, gate1, up0, up1, down0, down1 = self.units

        def copy_of(unit):
            source, result = self.outs[self.units.index(unit)]
            return pltpu.make_async_copy(source, result, unit.sems.at[2, 1])

        def then(unit, number):
            def action():
                unit.finish(number)
                if number < (1 if unit in (gate0, gate1, up0, up1) else 2):
                    unit.start(number + 1)
                else:
                    copy_of(unit).start()

            return action

        order = (down0, down1, out, up0, gate0, gate1, up1)
        done = [(0, functools.partial(unit.start, 0)) for unit in order]
        done += [(row, then(unit, 0)) for row, unit in zip((0, 1, 1, 2, 2, 3, 3), order)]
        done += [(6, then(down0, 1)), (7, then(down1, 1)), (8, then(out, 1)), (9, then(up0, 1))]
        done += [(10, then(gate0, 1)), (11, then(down0, 2))]
        done += [(12, then(down1, 2)), (12, then(out, 2)), (12, then(gate1, 1)), (12, then(up1, 1))]
        done += [(12, lambda unit=unit: copy_of(unit).wait()) for unit in order]
        return done


class HeldSum:
    def __init__(self, place, piece, source, buffers, result):
        self.place, self.piece, self.source = place, piece, source
        self.own, self.got, self.sems, *relay = buffers
        self.relay = RelaySum(place, self.own, *relay, result)
        self.axis = piece.order[0]

    def copies(self):
        if not self.piece.deep:
            return []
        p = self.place
        at = lambda index: self.source.at[index] if self.axis == "x" else self.source.at[:, index]
        return [
            remote(
                at(index), self.got.at[s], self.sems.at[0, s], self.sems.at[1, s],
                p.device(**{self.axis: index}),
            )
            for s, index in p.peers(self.axis)
        ]

    def local(self):
        mine = self.piece.along_a(self.place, self.source)
        return pltpu.make_async_copy(mine, self.own, self.sems.at[2, 0])

    def start(self):
        self.local().start()
        for copy in self.copies():
            copy.start()

    def finish(self):
        self.local().wait()
        copies = self.copies()
        for copy in copies:
            copy.wait_recv()
            copy.wait_send()
        if len(copies):
            add_up(self.own, [self.got.at[slot] for slot in range(len(copies))])
        self.relay.step(0)

    @staticmethod
    def scratch(place, piece, rows):
        count = len(place.peers(piece.order[0])) if piece.deep else 1
        got = (count, place.as_, rows, piece.size) if piece.deep else (1, 1, 16, 128)
        return [
            VMEM((place.as_, rows, piece.size), BF16),
            VMEM(got, BF16),
            pltpu.SemaphoreType.DMA((3, count)),
            *RelaySum.scratch(rows, piece.size, BF16),
        ]


def closing_kernel(
    plan, pieces, rows, fold, parted, share,
    dq, dk, dv, w_query, w_key, w_value, hidden, x, d_middle, gains, cosine, sine, gain, *refs,
):
    helds, refs = refs[: len(pieces)], refs[len(pieces) :]
    first_out, x_out, gains_total, *refs = refs
    results, buffers = refs[: 3 + parted], refs[3 + parted :]
    closed = results[4:6]
    if share:
        results, buffers = [*results[:4], *buffers[:2], *results[6:]], buffers[2:]
    slopes, weights, hidden_in, x_in, middle, hidden_turn, d_hidden, got_gains, gain_sems = buffers[:9]
    loads, grad_first, grad_x, *buffers = buffers[9:]
    place = Place()
    parts, tokens, width = dq.shape
    dim = parts * width
    devices = dim // rows
    place.greet()
    copies = [
        pltpu.make_async_copy(source, target, loads.at[n])
        for n, (source, target) in enumerate(
            (
                (hidden, hidden_in), (dq, slopes.at[0]), (w_query, weights.at[0]),
                (dk, slopes.at[1]), (w_key, weights.at[1]), (dv, slopes.at[2]),
                (w_value, weights.at[2]), (x, x_in), (d_middle, middle),
            )
        )
    ]
    for copy in copies:
        copy.start()
    units, relays, grads, rest = [], [], [], []
    for array, start, size, order in plan:
        source = buffers[0]
        unit = Sum(place, source, order, (None, *buffers[1:5]))
        result = results[array].at[:, pl.ds(start, size)]
        relays.append(DirectSum(place, unit.held, *buffers[5:7], result))
        units.append(unit)
        grads.append(source)
        buffers = buffers[7:]
    for piece, held in zip(pieces, helds):
        result = piece.columns(results[3 + piece.array])
        rest.append(HeldSum(place, piece, held, buffers[:7], result))
        buffers = buffers[7:]
    deep = [unit for unit in rest if unit.piece.deep]
    simple = [unit for unit in rest if not unit.piece.deep]
    total = TotalSum(place, gains_total, got_gains, gain_sems)
    for unit in simple + deep:
        unit.start()

    def low(array, first, size):
        done = []
        for start in range(first, first + size, 128):
            picks = range(start // width, (start + 128) // width)
            value = jnp.concatenate([slopes[array, n] for n in picks], axis=1).astype(F32)
            if array < 2:
                value = turned(value, cosine[...], -sine[...])
            else:
                value = 0.5 * value
                grad_first[:, start : start + 128] = value.astype(BF16)
            done.append(value.astype(BF16))
        return jnp.concatenate(done, axis=1)

    def compute(index):
        array, start, size, _ = plan[index]
        blocks = []
        for part in range(fold):
            first = part * (dim // fold) + start
            slope = low(array, first, size)
            blocks.append(dot(hidden_turn[...], slope).reshape(devices, rows, size))
            d_hidden[...] += against(slope, weights[array, :, first : first + size])
        block = (blocks[0] if fold == 1 else jnp.concatenate(blocks, axis=1)).astype(BF16)
        grads[index][...] = block.reshape(grads[index].shape)

    def step(group, number):
        for unit in group:
            unit.relay.step(number)

    def then(index, number):
        units[index].finish(number)
        if number < 2:
            units[index].start(number + 1)
        else:
            relays[index].step(0)

    copies[0].wait()
    hidden_turn[...] = hidden_in[...].T
    d_hidden[...] = jnp.zeros_like(d_hidden)
    count = len(units)
    for index in range(count):
        array = plan[index][0]
        if index == 0 or plan[index - 1][0] != array:
            copies[1 + 2 * array].wait()
            copies[2 + 2 * array].wait()
        compute(index)
        units[index].start(0)
        if index == 0:
            for unit in simple:
                unit.finish()
        else:
            then(index - 1, 0)
        if index == 2:
            step(simple, 1)
        if index == 4:
            step(simple, 2)
    copies[7].wait()
    copies[8].wait()
    grad_values, grad_gain = norm_back(d_hidden[...], x_in[...].astype(F32), gain[...])
    grad_x[...] = grad_values + middle[...]
    keeps = [
        pltpu.make_async_copy(grad_first, first_out, loads.at[0]),
        pltpu.make_async_copy(grad_x, x_out, loads.at[1]),
    ]
    for copy in keeps:
        copy.start()
    gains_total[...] = gains[...]
    gains_total[0:1] = grad_gain[None]
    total.start(0)
    then(count - 1, 0)
    for unit in deep:
        unit.finish()
    step(simple, 3)
    for index in range(count // 2):
        then(index, 1)
    step(deep, 1)
    total.then(0)
    for index in range(count // 2, count):
        then(index, 1)
    step(deep, 2)
    total.then(1)
    for index in range(count // 2):
        then(index, 2)
    total.then(2)
    for relay in relays[: count // 2]:
        relay.step(1)
    for index in range(count // 2, count):
        then(index, 2)
    step(deep, 3)
    for relay in relays[count // 2 :]:
        relay.step(1)
    for source, target in zip(results[4:6], closed) if share else ():
        padded = source.shape[1] // devices
        target[...] = jnp.concatenate(
            [source[:, n * padded : n * padded + share] for n in range(devices)], axis=1
        )
    total.then(3)
    for relay in relays:
        relay.step(2)
    for relay in relays:
        relay.step(3)
    for copy in keeps:
        copy.wait()


def closing(
    slopes, weights, hidden, x, d_middle, grad_gain, cosine, sine, gain, rows, helds, pieces,
    shapes, share, collective_id,
):
    place = Place()
    parts, tokens, width = slopes[0].shape
    dim = parts * width
    fold = 1
    while rows * fold % 16:
        fold *= 2
    plan, scratch = [], []
    for array in range(3):
        for start, size in column_pieces(dim // fold, 2):
            order = "bx" if len(plan) % 2 == 1 else "xb"
            plan.append((array, start, size, order))
            lead = (place.xs, 2, place.as_, place.bs)
            scratch.append(VMEM((*lead, rows * fold, size), BF16))
            scratch += Sum.scratch(place, rows * fold, size, order, BF16, False)
            scratch += DirectSum.scratch(place, rows * fold, size, BF16)
    for piece in pieces:
        scratch += HeldSum.scratch(place, piece, shapes[piece.array][0])
    peers = 1 + (place.xs - 1) + (place.bs - 1) + (place.as_ - 1)
    far, whole = pl.BlockSpec(memory_space=pl.ANY), pl.BlockSpec(memory_space=VMEM)
    shape = jax.ShapeDtypeStruct
    out = [shape((tokens, dim), BF16), shape((tokens, dim), F32), shape((8, dim), F32)]
    out += [shape((rows * fold, dim // fold), F32)] * 3
    final = list(shapes)
    if share:
        final[1:3] = [(rows, dim // rows * share)] * 2
    out += [shape(each, F32) for each in final]
    return pl.pallas_call(
        functools.partial(closing_kernel, plan, pieces, rows, fold, len(shapes), share),
        in_specs=[far] * 9 + [whole] * 4 + [far] * len(helds),
        out_specs=[far] * 2 + [whole] * (len(out) - 2),
        out_shape=out,
        scratch_shapes=[
            *[VMEM(each, F32) for each in shapes[1:3] if share],
            VMEM((3, parts, tokens, width), BF16),
            VMEM((3, dim, dim), BF16),
            VMEM((tokens, dim), BF16),
            VMEM((tokens, dim), BF16),
            VMEM((tokens, dim), F32),
            VMEM((dim, tokens), BF16),
            VMEM((tokens, dim), F32),
            VMEM((peers, 8, dim), F32),
            pltpu.SemaphoreType.DMA((2, peers)),
            pltpu.SemaphoreType.DMA((9,)),
            VMEM((tokens, dim), BF16),
            VMEM((tokens, dim), F32),
            *scratch,
        ],
        compiler_params=pltpu.CompilerParams(
            collective_id=collective_id, has_side_effects=True, vmem_limit_bytes=60 * MIB
        ),
        cost_estimate=pl.CostEstimate(
            flops=12 * tokens * dim * dim, bytes_accessed=20 * dim * dim, transcendentals=0
        ),
        name="closing",
    )(*slopes, *weights, hidden, x, d_middle, grad_gain, cosine, sine, gain, *helds)


def stacked(value, devices):
    rows, columns = value.shape[0] // devices, value.shape[1]
    fold = 1
    while rows * fold % 16:
        fold *= 2
    value = value.reshape(devices, rows, fold, columns // fold)
    return value.transpose(0, 2, 1, 3).reshape(devices, rows * fold, columns // fold)


def unstacked(value, rows):
    devices, high, columns = value.shape
    value = value.reshape(devices, high // rows, rows, columns).transpose(0, 2, 1, 3)
    return value.reshape(devices * rows, high // rows * columns)


def settle_kernel(share, first, grad_x, down, *refs):
    count = len(refs) // 2 - 1
    others, (first_out, x_out, down_out, *others_out) = refs[:count], refs[count:]
    first_out[...] = first[...].astype(F32)
    x_out[...] = grad_x[...]

    @pl.when(pl.program_id(0) == 0)
    def _():
        down_out[...] = down[:share]
        for source, target in zip(others, others_out):
            target[...] = source[...]


def settle(first, grad_x, down, others, share):
    tokens, dim = grad_x.shape
    block = pl.BlockSpec((tokens // 4, dim), lambda g: (g, 0))
    whole = lambda value: pl.BlockSpec(value.shape, lambda g: (0,) * len(value.shape))
    shape = lambda *dims: jax.ShapeDtypeStruct(dims, F32)
    outs = [shape(share, dim)]
    outs += [shape(*value.shape) for value in others]
    return pl.pallas_call(
        functools.partial(settle_kernel, share),
        grid=(4,),
        in_specs=[block, block] + [whole(value) for value in (down, *others)],
        out_specs=[block, block] + [whole(value) for value in outs],
        out_shape=[shape(tokens, dim)] * 2 + outs,
        compiler_params=pltpu.CompilerParams(vmem_limit_bytes=62 * MIB),
        name="settle",
    )(first, grad_x, down, *others)


def middle_kernel(
    steps, x, att, dy, w_out, gain, w_gate, w_up, w_down,
    out, d_middle, d_att, g_out, g_gate, g_up, g_down, g_gain,
    attended, middle, hidden, hidden_turn, result, d_hidden,
):
    step = pl.program_id(0)
    parts, _, width = att.shape

    @pl.when(step == 0)
    def _():
        for part in range(parts):
            attended[:, part * width : (part + 1) * width] = att[part]
        total = x[...].astype(F32) + dot(attended[...], w_out[...])
        scale = lax.rsqrt(jnp.mean(total * total, axis=-1, keepdims=True) + EPS)
        normed = (total * scale * gain[...]).astype(BF16)
        middle[...] = total
        result[...] = total
        hidden[...] = normed
        hidden_turn[...] = normed.T
        d_hidden[...] = jnp.zeros_like(d_hidden)

    grad = dy[...]
    gate = dot(hidden[...], w_gate[...])
    up = dot(hidden[...], w_up[...])
    d_inner = against(grad, w_down[...])
    sigma = jax.nn.sigmoid(gate)
    silu = gate * sigma
    inner = (silu * up).astype(BF16)
    d_gate = (d_inner * up * sigma * (1.0 + gate * (1.0 - sigma))).astype(BF16)
    d_up = (d_inner * silu).astype(BF16)
    result[...] += dot(inner, w_down[...])
    g_down[...] = across(inner, grad).astype(BF16)
    g_gate[...] = dot(hidden_turn[...], d_gate).astype(BF16)
    g_up[...] = dot(hidden_turn[...], d_up).astype(BF16)
    d_hidden[...] += against(d_gate, w_gate[...]) + against(d_up, w_up[...])

    @pl.when(step == steps - 1)
    def _():
        out[...] = result[...].astype(BF16)
        grad_values, grad_gain = norm_back(d_hidden[...], middle[...], gain[...])
        total = grad_values + dy[...].astype(F32)
        d_middle[...] = total
        g_gain[...] = jnp.zeros_like(g_gain)
        g_gain[1:2] = grad_gain[None]
        d_branch = total.astype(BF16)
        g_out[...] = across(attended[...], d_branch).astype(BF16)
        back = against(d_branch, w_out[...]).astype(BF16)
        for part in range(parts):
            d_att[part] = back[:, part * width : (part + 1) * width]


def between(x, att, dy, w_out, gain, w_gate, w_up, w_down):
    tokens, dim = x.shape
    units = w_gate.shape[1]
    chunk = 256 if units % 256 == 0 else 128
    whole = lambda value: pl.BlockSpec(value.shape, lambda g: (0,) * len(value.shape))
    wide = pl.BlockSpec((dim, chunk), lambda g: (0, g))
    tall = pl.BlockSpec((chunk, dim), lambda g: (g, 0))
    shape = jax.ShapeDtypeStruct
    outs = [
        shape((tokens, dim), BF16),
        shape((tokens, dim), F32),
        shape(att.shape, BF16),
        shape(w_out.shape, BF16),
        shape(w_gate.shape, BF16),
        shape(w_up.shape, BF16),
        shape(w_down.shape, BF16),
        shape((8, dim), F32),
    ]
    return pl.pallas_call(
        functools.partial(middle_kernel, units // chunk),
        grid=(units // chunk,),
        in_specs=[whole(v) for v in (x, att, dy, w_out, gain)] + [wide, wide, tall],
        out_specs=[whole(v) for v in outs[:4]] + [wide, wide, tall, whole(outs[7])],
        out_shape=outs,
        scratch_shapes=[
            VMEM((tokens, dim), BF16),
            VMEM((tokens, dim), F32),
            VMEM((tokens, dim), BF16),
            VMEM((dim, tokens), BF16),
            VMEM((tokens, dim), F32),
            VMEM((tokens, dim), F32),
        ],
        compiler_params=pltpu.CompilerParams(vmem_limit_bytes=62 * MIB),
        cost_estimate=pl.CostEstimate(
            flops=18 * tokens * dim * units, bytes_accessed=12 * dim * units, transcendentals=0
        ),
        name="between",
    )(x, att, dy, w_out, gain, w_gate, w_up, w_down)


def shards(
    inputs, first_values, lengths, w_query, w_key, w_value, w_out, gain_attn,
    w_gate, w_up, w_down, gain_mlp, cotangent,
):
    row_count, tokens, width = inputs.shape
    assert row_count == 1
    parts = lax.axis_size("seq")
    rank = lax.axis_index("seq")
    devices = lax.axis_size("dp") * parts
    rows, down_rows = w_query.shape[0], w_down.shape[0]
    multiple = 16 if down_rows >= 64 else 8
    down_padded = -(-down_rows // multiple) * multiple

    def spaced(value):
        value = value.reshape(rows, devices, down_rows)
        value = jnp.pad(value, ((0, 0), (0, 0), (0, down_padded - down_rows)))
        return value.reshape(rows, devices * down_padded)

    index = lax.axis_index("dp") * parts + rank
    gains = jnp.pad(jnp.stack([gain_attn, gain_mlp]).astype(F32), ((0, 6), (0, width - rows)))
    gains = jnp.roll(gains, index * rows, axis=1)
    wide = lambda value: stacked(value, 1)[0]
    padded_units = devices * down_padded
    if rows % 16 == 0:
        parted = [w_out, w_gate, w_up, w_down]
        shapes = [w_out.shape, *[(rows, padded_units)] * 2, (down_padded, width)]
    else:
        padded_down = jnp.pad(w_down, ((0, down_padded - down_rows), (0, 0)))
        parted = [wide(w_out), wide(spaced(w_gate)), wide(spaced(w_up)), wide(padded_down)]
        shapes = [value.shape for value in parted]
    pieces = Piece.all(shapes)
    upto = jnp.arange(lengths.shape[1])
    ends = jnp.sum(jnp.where(upto[:, None] >= upto[None, :], lengths, 0), axis=1)
    begins = ends - lengths[0]
    time = jnp.arange(tokens * parts, dtype=jnp.int32)
    inside = (time[:, None] >= begins[None, :]) & (time[:, None] < ends[None, :])
    start_all = jnp.sum(jnp.where(inside, begins[None, :], 0), axis=1)
    own_start = lax.dynamic_slice_in_dim(start_all, rank * tokens, tokens)
    position = (rank * tokens + jnp.arange(tokens, dtype=jnp.int32) - own_start).astype(F32)
    half = HEAD_DIM // 2
    angles = position[:, None] * THETA ** (-jnp.arange(half, dtype=F32) * 2.0 / HEAD_DIM)
    cosine = jnp.tile(jnp.cos(angles), (1, 4))
    sine = jnp.sin(angles)
    sine = jnp.tile(jnp.concatenate([-sine, sine], axis=1), (1, 2))
    start = start_all.reshape(parts, 1, tokens)

    x_low = inputs.reshape(tokens, width)
    (q, k, v, hidden_in), gains, fulls, helds = opening(
        x_low, first_values.reshape(tokens, width), cosine, sine, gains,
        [wide(w_query), wide(w_key), wide(w_value)], parted, shapes, pieces, parts, 3,
    )
    tall = lambda value: unstacked(value, rows)
    query_full, key_full, value_full = (tall(value) for value in fulls)
    gain_one, gain_two = gains[0], gains[1]
    (q_all, k_all, v_all, o_all, lse_all, attended), (*weights, down_full) = attend(
        q, k, v, start, helds, pieces, shapes
    )
    out_full, gate_full, up_full = (tall(value) for value in weights)
    down_full = unstacked(down_full, down_padded)
    output, grad_middle, d_att, grad_out, grad_gate, grad_up, grad_down, grad_gain_two = between(
        x_low, attended, cotangent.reshape(tokens, width), out_full, gain_two[None],
        gate_full, up_full, down_full,
    )

    share = lambda grad: stacked(grad.astype(BF16), devices)
    (dq, dk, dv), helds = attend_back(
        d_att, q_all, k_all, v_all, o_all, lse_all, start,
        [share(grad_out), share(grad_gate), share(grad_up), share(grad_down)], pieces,
    )
    (
        grad_first, grad_x, gains_total, total_query, total_key, total_value,
        total_out, total_gate, total_up, total_down,
    ) = closing(
        (dq, dk, dv), (query_full, key_full, value_full), hidden_in, x_low, grad_middle,
        grad_gain_two, cosine, sine, gain_one[None], rows, helds, pieces, shapes,
        down_rows if rows % 16 == 0 else 0, 4,
    )
    own_gain = lambda n: lax.dynamic_slice_in_dim(gains_total[n], index * rows, rows)
    if rows % 16 == 0:
        grad_first, grad_x, total_down, total_gate, total_up, *totals = settle(
            grad_first, grad_x, total_down,
            (total_gate, total_up, total_query, total_key, total_value, total_out), down_rows,
        )
    else:
        low = lambda total: unstacked(total[None], rows)
        close = lambda total: low(total).reshape(rows, devices, down_padded)[:, :, :down_rows]
        total_gate, total_up = (
            close(total).reshape(rows, devices * down_rows) for total in (total_gate, total_up)
        )
        total_down = unstacked(total_down[None], down_padded)[:down_rows]
        totals = [low(total) for total in (total_query, total_key, total_value, total_out)]
        grad_first = grad_first.astype(F32)
    return (
        output.reshape(inputs.shape),
        grad_x.reshape(inputs.shape),
        grad_first.reshape(inputs.shape),
        *totals,
        own_gain(0),
        total_gate,
        total_up,
        total_down,
        own_gain(1),
    )


def solution(mesh):
    tokens = P("dp", "seq", None)
    matrix = P(("dp", "seq"), None)
    vector = P(("dp", "seq"))
    return jax.shard_map(
        shards,
        mesh=mesh,
        in_specs=(
            tokens, tokens, P("dp", None), matrix, matrix, matrix, matrix, vector,
            matrix, matrix, matrix, vector, tokens,
        ),
        out_specs=(
            tokens, tokens, tokens, matrix, matrix, matrix, matrix, vector,
            matrix, matrix, matrix, vector,
        ),
        check_vma=False,
    )
```
